32 devices in a mesh: lon: 8 (over z, y), lat: 4 (over x, core).
Axes of the slice: x: 2, y: 2, z: 4, core: 2. Of those that a mesh axis runs over, the one named last changes fastest.
Arguments:
- hidden_in: bfloat16 [8, 128, 128, 512], P(None, None, 'lon', 'lat'), may hold values from -6 to 6
- w_conv1: bfloat16 [3, 3, 128, 128], replicated, may hold values from -0.1875 to 0.1875
- b_conv1: float32 [128], replicated, may hold values from -3 to 3
- w_conv2: bfloat16 [3, 3, 128, 12], replicated, may hold values from -0.1875 to 0.1875
- b_conv2: float32 [12], replicated, may hold values from -3.5 to 3.5
- state: float32 [6, 8, 128, 512], P(None, None, 'lon', 'lat'), may hold values from -6 to 6
Outputs:
- velocity: float32 [12, 8, 128, 512], P(None, None, 'lon', 'lat')
- tendency: float32 [6, 8, 128, 512], P(None, None, 'lon', 'lat')
The draws below stay inside these ranges and needn't reach their ends.
All inputs are finite; a program needn't handle non-finite values.
Results may differ from the reference program's by a relative error of at most 0.0013.
Values may be sent and summed in bfloat16 or wider, within the bound.
No kernel may reach another device: no remote copies, remote signals or barrier semaphores. Data moves between devices by JAX's collectives and lax.ppermute only.
A program may use at most 128 MiB of HBM per device.

```python
import math
import jax
import jax.numpy as jnp
from jax import lax

CH = 128
VARS = 6
VEL = 12
LEV = 8
NLON = 128
NLAT = 512


def draw_b_conv2(key, part):
    flip_key = jax.random.fold_in(key, 11)
    drift_key = jax.random.fold_in(key, 12)
    zonal_key = jax.random.fold_in(key, 13)
    flip_bits = jax.random.randint(flip_key, (VEL,), 0, 2)
    drift_bias = (2.0 * flip_bits.astype(jnp.float32) - 1.0) * jax.random.uniform(drift_key, (VEL,), jnp.float32, 2.5, 3.5)
    zonal_bias = 0.5 * jax.random.truncated_normal(zonal_key, -3.0, 3.0, (VEL,), jnp.float32)
    north_mask = lax.broadcasted_iota(jnp.int32, (VEL,), 0) % 2
    return jnp.where(north_mask == 1, drift_bias, zonal_bias)


def draw_state(key, part):
    shape_full = (VARS, LEV, NLON, NLAT)
    lon_pos = lax.broadcasted_iota(jnp.int32, shape_full, 2)
    lat_pos = lax.broadcasted_iota(jnp.int32, shape_full, 3)
    parity = (lon_pos + lat_pos) % 2
    alt_sign = 1.0 - 2.0 * parity.astype(jnp.float32)
    size_term = jax.random.uniform(key, shape_full, jnp.float32, 1.5, 5.5)
    return alt_sign * size_term


def level_of(key, extent, split, low, largest):
    gain, own = 1.0, jax.random.fold_in(key, 6)
    for axis_at, parts in split:
        draws = jnp.exp(jax.random.uniform(jax.random.fold_in(own, axis_at), (parts,), jnp.float32, low / len(split), largest / len(split)))
        gain = gain * jnp.repeat(draws, extent[axis_at] // parts).reshape([-1 if axis == axis_at else 1 for axis in range(len(extent))])
    return gain


def normal_values(key, dims, scale, reach, pieces=(), kind=jnp.bfloat16):
    result = jax.random.normal(key, dims, jnp.float32) * scale
    if len(pieces) > 0:
        result = level_of(key, dims, pieces, -0.22, 0.18) * result
    return jnp.clip(result, min=-reach, max=reach).astype(kind)


def setup_inputs(seed: int = 0) -> dict:
    seeds = jax.random.split(jax.random.key(seed), 7)
    hidden_in = normal_values(seeds[0], (LEV, CH, NLON, NLAT), 1.0, 6.0, ((2, 8), (3, 4)))
    w_conv1 = normal_values(seeds[1], (3, 3, CH, CH), (9 * CH) ** -0.5, 0.1875)
    b_conv1 = normal_values(seeds[2], (CH,), 0.5, 3.0, (), jnp.float32)
    w_conv2 = normal_values(seeds[3], (3, 3, CH, VEL), (9 * CH) ** -0.5, 0.1875)
    b_conv2 = draw_b_conv2(jax.random.fold_in(seeds[6], 71), 0)
    state = draw_state(jax.random.fold_in(seeds[6], 71), 0)
    return {"hidden_in": hidden_in, "w_conv1": w_conv1, "b_conv1": b_conv1, "w_conv2": w_conv2, "b_conv2": b_conv2, "state": state}


time_step = 0.5
speed_cap = 0.6
cos_floor = 0.5


def wrap_pad(field, width):
    field = jnp.concatenate([field[..., -width:, :], field, field[..., :width, :]], axis=-2)
    widths = [(0, 0)] * (field.ndim - 1) + [(width, width)]
    return jnp.pad(field, widths)


def conv_level(padded, weight):
    out_x = padded.shape[1] - 2
    out_y = padded.shape[2] - 2
    total = jnp.zeros((weight.shape[3], out_x, out_y), jnp.float32)
    for row_off in range(3):
        for col_off in range(3):
            window = padded[:, row_off:row_off + out_x, col_off:col_off + out_y].astype(jnp.float32)
            total = total + jnp.einsum("cxy,co->oxy", window, weight[row_off, col_off].astype(jnp.float32))
    return total


def reference(hidden_in, w_conv1, b_conv1, w_conv2, b_conv2, state):
    def level(features):
        first = conv_level(wrap_pad(features, 1), w_conv1) + b_conv1[:, None, None]
        hidden = jax.nn.silu(first).astype(jnp.bfloat16)
        second = conv_level(wrap_pad(hidden, 1), w_conv2) + b_conv2[:, None, None]
        return speed_cap * jnp.tanh(second)

    velocity = jnp.transpose(lax.map(level, hidden_in), (1, 0, 2, 3))
    n_lat = state.shape[3]
    rows = jnp.arange(n_lat).astype(jnp.float32)
    latitude = (rows + 0.5) * (math.pi / n_lat) - 0.5 * math.pi
    cosine = jnp.maximum(jnp.cos(latitude), cos_floor)
    metric = 1.0 / cosine
    zonal = velocity[0::2]
    north = velocity[1::2]
    zonal_pad = wrap_pad(zonal, 1)
    flux_pad = wrap_pad(north * cosine, 1)
    divergence = metric * ((zonal_pad[..., 2:, 1:-1] - zonal_pad[..., :-2, 1:-1]) * 0.5
                           + (flux_pad[..., 1:-1, 2:] - flux_pad[..., 1:-1, :-2]) * 0.5)

    def rate(field):
        padded = wrap_pad(field, 1)
        centre = padded[..., 1:-1, 1:-1]
        back_x = centre - padded[..., :-2, 1:-1]
        fore_x = padded[..., 2:, 1:-1] - centre
        back_y = centre - padded[..., 1:-1, :-2]
        fore_y = padded[..., 1:-1, 2:] - centre
        advect = metric * (jnp.maximum(zonal, 0.0) * back_x + jnp.minimum(zonal, 0.0) * fore_x) \
            + jnp.maximum(north, 0.0) * back_y + jnp.minimum(north, 0.0) * fore_y
        return -(advect + centre * divergence)

    rate_one = rate(state)
    rate_two = rate(state + 0.5 * time_step * rate_one)
    rate_three = rate(state + 0.5 * time_step * rate_two)
    rate_four = rate(state + time_step * rate_three)
    tendency = (rate_one + 2.0 * rate_two + 2.0 * rate_three + rate_four) / 6.0
    return velocity, tendency
```

```python
import functools
import math

import jax
import jax.numpy as jnp
from jax import lax
from jax.experimental import pallas as pl
from jax.experimental.pallas import tpu as pltpu
from jax.sharding import PartitionSpec as P

time_step = 0.5
speed_cap = 0.6
cos_floor = 0.5

SIDE = 8
WIDE = 128
REACH = 4
VG = 8
VMEM_LIMIT = 40 * 2**20


def swap_pairs(count, first, closed):
    pairs = []
    for low in range(first, count, 2):
        high = low + 1
        if high >= count and not closed:
            continue
        pairs += [(low, high % count), (high % count, low)]
    return pairs


def swap(block, axis, first, closed):
    return lax.ppermute(block, axis, swap_pairs(lax.axis_size(axis), first, closed))


def exchange(low_edge, high_edge, axis, closed):
    even = lax.axis_index(axis) % 2 == 0
    got_a = swap(jnp.where(even, high_edge, low_edge), axis, 0, closed)
    got_b = swap(jnp.where(even, low_edge, high_edge), axis, 1, closed)
    before = jnp.where(even, got_b, got_a)
    after = jnp.where(even, got_a, got_b)
    return before, after


def turn_kernel(x_ref, g_ref, s_ref):
    rows = x_ref.shape[2]
    chans = x_ref.shape[1]
    s_ref[...] = x_ref[0].astype(jnp.float32).reshape(chans * rows, x_ref.shape[3])
    for row in range(rows):
        g_ref[0, row] = s_ref[pl.ds(row, chans, stride=rows), :].T.astype(jnp.bfloat16)


def turn(block):
    lev, ch, rows, cols = block.shape
    return pl.pallas_call(
        turn_kernel,
        grid=(lev,),
        in_specs=[pl.BlockSpec((1, ch, rows, cols), lambda i: (i, 0, 0, 0))],
        out_specs=pl.BlockSpec((1, rows, cols, ch), lambda i: (i, 0, 0, 0)),
        out_shape=jax.ShapeDtypeStruct((lev, rows, cols, ch), jnp.bfloat16),
        scratch_shapes=[pltpu.VMEM((ch * rows, cols), jnp.float32)],
        compiler_params=pltpu.CompilerParams(vmem_limit_bytes=VMEM_LIMIT),
    )(block)


def silu(s):
    return s / (1.0 + jnp.exp(-s))


def lay_row(e_ref, s_ref, slot, main, right, left):
    cols = main.shape[0]
    ext = cols + 2 * SIDE
    main = main.astype(jnp.float32)
    left = left.astype(jnp.float32)
    e_ref[slot, 0:SIDE] = left
    e_ref[slot, SIDE : SIDE + cols] = main
    e_ref[slot, SIDE + cols : 2 * SIDE + cols] = right.astype(jnp.float32)
    e_ref[slot, 2 * SIDE + cols : 3 * SIDE + cols] = left
    e_ref[slot, 3 * SIDE + cols : 4 * SIDE + cols] = main[0:SIDE]
    ch = main.shape[1]
    for b in range(3):
        s_ref[slot, :, b * ch : (b + 1) * ch] = e_ref[slot, pl.ds(SIDE - 1 + b, ext), :].astype(jnp.bfloat16)


def spread_row(hid, w2_ref, q_ref, qm_ref, row, cols):
    part = lax.dot_general(w2_ref[...], hid[0:cols], (((1,), (1,)), ((), ())), preferred_element_type=jnp.float32)
    marg = lax.dot_general(w2_ref[...], hid[cols:], (((1,), (1,)), ((), ())), preferred_element_type=jnp.float32)
    for a in range(3):
        at = row + 2 - a
        q_ref[at] += part[a * 6 * VG : (a + 1) * 6 * VG]
        qm_ref[at, :, 0 : 2 * SIDE] += marg[a * 6 * VG : (a + 1) * 6 * VG]


def col_before(main, marg):
    lane = lax.broadcasted_iota(jnp.int32, main.shape, main.ndim - 1)
    ax = main.ndim - 1
    turned = pltpu.roll(main, 1, ax)
    new_main = jnp.where(lane == 0, pltpu.roll(marg, WIDE - (2 * SIDE - 1), ax), turned)
    new_marg = jnp.where(lane == 0, turned, pltpu.roll(marg, 1, ax))
    return new_main, new_marg


def col_after(main, marg):
    lane = lax.broadcasted_iota(jnp.int32, main.shape, main.ndim - 1)
    ax = main.ndim - 1
    moved = pltpu.roll(marg, WIDE - 1, ax)
    new_main = jnp.where(lane == WIDE - 1, moved, pltpu.roll(main, WIDE - 1, ax))
    new_marg = jnp.where(lane == 2 * SIDE - 1, pltpu.roll(main, 2 * SIDE - 1, ax), moved)
    return new_main, new_marg


def join_cols(q_ref, qm_ref, at):
    vg = 2 * VG
    before = col_before(q_ref[at, 0:vg], qm_ref[at, 0:vg])
    after = col_after(q_ref[at, 2 * vg : 3 * vg], qm_ref[at, 2 * vg : 3 * vg])
    main = before[0] + q_ref[at, vg : 2 * vg] + after[0]
    marg = before[1] + qm_ref[at, vg : 2 * vg] + after[1]
    return main, marg


def inner_kernel(g_ref, r_ref, l_ref, w1_ref, w2_ref, b1_ref, keep_ref, ps_ref, pm_ref, e_ref, s_ref, q_ref, qm_ref):
    rows, cols, ch = g_ref.shape[1:]
    q_ref[...] = jnp.zeros_like(q_ref)
    qm_ref[...] = jnp.zeros_like(qm_ref)
    for row in range(rows):
        lay_row(e_ref, s_ref, row, g_ref[0, row], r_ref[0, row], l_ref[0, row])
    for row in range(1, rows - 1, 2):
        lhs = jnp.concatenate([s_ref[row - 1 + r] for r in range(4)], axis=1)
        acc = jnp.dot(lhs, w1_ref[...], preferred_element_type=jnp.float32) + b1_ref[...]
        hid = (silu(acc) * keep_ref[...]).astype(jnp.bfloat16)
        spread_row(hid[:, 0:ch], w2_ref, q_ref, qm_ref, row, cols)
        spread_row(hid[:, ch:], w2_ref, q_ref, qm_ref, row + 1, cols)
    for at in range(rows + 2):
        ps_ref[0, at], pm_ref[0, at] = join_cols(q_ref, qm_ref, at)


def edge_kernel(even_ref, g0_ref, g1_ref, r0_ref, r1_ref, l0_ref, l1_ref, a_ref, b_ref, w1_ref, w2_ref, b1_ref, keep_ref,
                pi_ref, pmi_ref, ps_ref, pm_ref, outa_ref, outb_ref, e_ref, s_ref, q_ref, qm_ref):
    cols, ch = g0_ref.shape[2:]
    rows = ps_ref.shape[1] - 2
    ext = cols + 2 * SIDE
    even = even_ref[0] == 0
    got_a = a_ref[0].astype(jnp.float32)
    got_b = b_ref[0].astype(jnp.float32)
    low = jnp.where(even, got_b, got_a)
    high = jnp.where(even, got_a, got_b)
    q_ref[...] = jnp.zeros_like(q_ref)
    qm_ref[...] = jnp.zeros_like(qm_ref)
    lay_row(e_ref, s_ref, 0, low[0:cols], low[cols : cols + SIDE], low[cols + SIDE : ext])
    lay_row(e_ref, s_ref, 5, high[0:cols], high[cols : cols + SIDE], high[cols + SIDE : ext])
    for k in range(2):
        lay_row(e_ref, s_ref, 1 + k, g0_ref[0, k], r0_ref[0, k], l0_ref[0, k])
        lay_row(e_ref, s_ref, 3 + k, g1_ref[0, k], r1_ref[0, k], l1_ref[0, k])
    for k in range(2):
        lhs = jnp.concatenate([s_ref[3 * k + r] for r in range(3)], axis=1)
        acc = jnp.dot(lhs, w1_ref[...], preferred_element_type=jnp.float32) + b1_ref[...]
        hid = (silu(acc) * keep_ref[...]).astype(jnp.bfloat16)
        spread_row(hid, w2_ref, q_ref, qm_ref, 3 * k, cols)
    ps_ref[...] = pi_ref[...]
    pm_ref[...] = pmi_ref[...]
    for at in range(6):
        main, marg = join_cols(q_ref, qm_ref, at)
        to = at if at < 3 else rows - 4 + at
        ps_ref[0, to] += main
        pm_ref[0, to] += marg

    def packed(start, skip):
        mains, slots = [], []
        for r in range(REACH + 1):
            for part in range(2):
                if (r, part) == (skip, 1):
                    continue
                mains.append(ps_ref[0, start + r, part * VG : (part + 1) * VG])
                slots.append(pm_ref[0, start + r, part * VG : (part + 1) * VG])
        lane = lax.broadcasted_iota(jnp.int32, (VG, WIDE), 1)
        tail = []
        for first in range(0, len(slots), WIDE // (2 * SIDE)):
            out = jnp.zeros((VG, WIDE), jnp.float32)
            for k, slot in enumerate(slots[first : first + WIDE // (2 * SIDE)]):
                moved = pltpu.roll(slot, k * 2 * SIDE, 1) if k else slot
                out = jnp.where(lane // (2 * SIDE) == k, moved, out)
            tail.append(out)
        return jnp.concatenate(mains + tail, axis=0)

    high_out = packed(rows + 1 - REACH, 0)
    low_out = packed(0, REACH)
    pad = jnp.zeros((outa_ref.shape[1] - high_out.shape[0], WIDE), jnp.float32)
    high_out = jnp.concatenate([high_out, pad], axis=0)
    low_out = jnp.concatenate([low_out, pad], axis=0)
    outa_ref[0] = jnp.where(even, high_out, low_out).astype(jnp.bfloat16)
    outb_ref[0] = jnp.where(even, low_out, high_out).astype(jnp.bfloat16)


HALVES = 2 * (REACH + 1) - 1
TAILS = -(-HALVES // (WIDE // (2 * SIDE)))
WIRE = -(-(HALVES + TAILS) * VG // 16) * 16


def unpack_wire(wire, skip):
    mains, margs = [], []
    k = 0
    zero = jnp.zeros((VG, WIDE), jnp.float32)
    per = WIDE // (2 * SIDE)
    for r in range(REACH + 1):
        main_row, marg_row = [], []
        for part in range(2):
            if (r, part) == (skip, 1):
                main_row.append(zero)
                marg_row.append(zero)
                continue
            main_row.append(wire[k * VG : (k + 1) * VG])
            tail = wire[(HALVES + k // per) * VG : (HALVES + k // per + 1) * VG]
            shift = (k % per) * 2 * SIDE
            marg_row.append(pltpu.roll(tail, WIDE - shift, 1) if shift else tail)
            k += 1
        mains.append(jnp.concatenate(main_row, axis=0))
        margs.append(jnp.concatenate(marg_row, axis=0))
    return mains, margs


def advect_kernel(even_ref, ps_ref, pm_ref, a_ref, b_ref, st_ref, slo_ref, shi_ref, sm_ref, b2_ref, lat_ref, latm_ref,
                  vel_ref, ten_ref, st8_ref, out_ref):
    nvar = st_ref.shape[0]
    rows = st_ref.shape[2]
    even = even_ref[0] == 0
    got_a = a_ref[0].astype(jnp.float32)
    got_b = b_ref[0].astype(jnp.float32)
    lo_main, lo_marg = unpack_wire(jnp.where(even, got_b, got_a), 0)
    hi_main, hi_marg = unpack_wire(jnp.where(even, got_a, got_b), REACH)
    main = lo_main[0:REACH] + [ps_ref[0, 1 + r] for r in range(rows)] + hi_main[1:]
    marg = lo_marg[0:REACH] + [pm_ref[0, 1 + r] for r in range(rows)] + hi_marg[1:]
    for stack, own, lo, hi in ((main, ps_ref, lo_main, hi_main), (marg, pm_ref, lo_marg, hi_marg)):
        stack[REACH - 1] += own[0, 0]
        stack[REACH] += lo[REACH]
        stack[REACH + rows - 1] += hi[0]
        stack[REACH + rows] += own[0, rows + 1]
    bias = b2_ref[...]
    total = rows + 2 * REACH
    main = speed_cap * jnp.tanh(jnp.stack(main) + bias)
    marg = speed_cap * jnp.tanh(jnp.stack(marg) + bias) * latm_ref[2:3]
    for part in range(2):
        out_ref[...] = main[REACH : REACH + rows, part * VG : (part + 1) * VG].reshape(rows * VG, WIDE)
        for n in range(nvar):
            vel_ref[2 * n + part, 0] = out_ref[pl.ds(n, rows, stride=VG), :]
    for n in range(nvar):
        st8_ref[0, pl.ds(n, REACH, stride=VG), :] = slo_ref[n, 0]
        st8_ref[0, pl.ds(REACH * VG + n, rows, stride=VG), :] = st_ref[n, 0]
        st8_ref[0, pl.ds((REACH + rows) * VG + n, REACH, stride=VG), :] = shi_ref[n, 0]
        st8_ref[1, pl.ds(n, total, stride=VG), 0 : 2 * SIDE] = sm_ref[n, 0]
    start = [st8_ref[0].reshape(total, VG, WIDE), st8_ref[1].reshape(total, VG, WIDE)]
    cosine = [lat_ref[0:1], latm_ref[0:1]]
    metric = [lat_ref[1:2], latm_ref[1:2]]
    u = [main[:, 0:VG], marg[:, 0:VG]]
    v = [main[1:-1, VG:], marg[1:-1, VG:]]
    flux = [v[k] * cosine[k] for k in range(2)]
    fb = col_before(*flux)
    fa = col_after(*flux)
    coef = []
    for k in range(2):
        div = metric[k] * ((u[k][2:] - u[k][:-2]) * 0.5 + (fa[k] - fb[k]) * 0.5)
        mid = u[k][1:-1]
        cl = metric[k] * jnp.maximum(mid, 0.0)
        cr = -metric[k] * jnp.minimum(mid, 0.0)
        cd = jnp.maximum(v[k], 0.0)
        cu = -jnp.minimum(v[k], 0.0)
        coef.append((-(cl + cr + cd + cu + div), cl, cr, cd, cu))

    def rate(q, depth):
        lo = depth - 1
        hi = total - 2 - lo
        mid = [f[1:-1] for f in q]
        qb = col_before(*mid)
        qa = col_after(*mid)
        out = []
        for k in range(2):
            c0, cl, cr, cd, cu = (c[lo:hi] for c in coef[k])
            out.append(c0 * mid[k] + cl * q[k][:-2] + cr * q[k][2:] + cd * qb[k] + cu * qa[k])
        return out

    one = rate(start, 1)
    two = rate([start[k][1:-1] + 0.5 * time_step * one[k] for k in range(2)], 2)
    three = rate([start[k][2:-2] + 0.5 * time_step * two[k] for k in range(2)], 3)
    four = rate([start[k][3:-3] + time_step * three[k] for k in range(2)], 4)
    ten = (one[0][3:-3] + 2.0 * two[0][2:-2] + 2.0 * three[0][1:-1] + four[0]) / 6.0
    out_ref[...] = ten.reshape(rows * VG, WIDE)
    for n in range(nvar):
        ten_ref[n, 0] = out_ref[pl.ds(n, rows, stride=VG), :]


def full(shape):
    return pl.BlockSpec(shape, lambda *i: (0,) * len(shape))


def per_level(shape):
    return pl.BlockSpec((1,) + shape[1:], lambda i: (i,) + (0,) * (len(shape) - 1))


def body(hidden_in, w_conv1, b_conv1, w_conv2, b_conv2, state):
    lev, ch, rows, cols = hidden_in.shape
    nvar = state.shape[0]
    ext = cols + 2 * SIDE
    f32 = jnp.float32
    params = pltpu.CompilerParams(vmem_limit_bytes=VMEM_LIMIT)
    smem = pl.BlockSpec(memory_space=pltpu.SMEM)

    taps = w_conv1.reshape(3, 3 * ch, ch)
    none = jnp.zeros_like(taps[0])
    w1_pair = jnp.concatenate(
        [
            jnp.concatenate([taps[0], taps[1], taps[2], none], axis=0),
            jnp.concatenate([none, taps[0], taps[1], taps[2]], axis=0),
        ],
        axis=1,
    )
    w1_one = taps.reshape(9 * ch, ch)
    w2 = w_conv2.reshape(3, 3, ch, nvar, 2).transpose(0, 1, 4, 3, 2)
    w2 = jnp.pad(w2, ((0, 0), (0, 0), (0, 0), (0, VG - nvar), (0, 0))).reshape(18 * VG, ch)
    b1 = b_conv1.reshape(1, ch)
    b2 = jnp.pad(b_conv2.reshape(nvar, 2).T, ((0, 0), (0, VG - nvar))).reshape(2 * VG, 1)
    b2 = jnp.broadcast_to(b2, (2 * VG, WIDE))

    n_lat = cols * lax.axis_size("lat")
    place = jnp.concatenate([jnp.arange(cols + SIDE), jnp.arange(-SIDE, 0)]).astype(jnp.int32)
    place = place + lax.axis_index("lat") * cols
    keep = ((place >= 0) & (place < n_lat)).astype(f32)
    phi = (place.astype(f32) + 0.5) * (math.pi / n_lat) - 0.5 * math.pi
    cosine = jnp.maximum(jnp.cos(phi), cos_floor)
    table = jnp.stack([cosine, 1.0 / cosine, keep])
    table = jnp.pad(table, ((0, VG - 3), (0, 0)))
    lat_main = table[:, 0:cols]
    lat_marg = jnp.pad(table[:, cols:], ((0, 0), (0, WIDE - 2 * SIDE)))
    keep_col = keep.reshape(ext, 1)
    even = (lax.axis_index("lon") % 2).astype(jnp.int32).reshape(1)

    before, after = exchange(state[..., 0:SIDE], state[..., cols - SIDE :], "lat", False)
    marg = jnp.concatenate([after, before], axis=-1)
    wide = jnp.concatenate([state, marg], axis=-1)
    lo, hi = exchange(
        wide[:, :, 0:REACH].reshape(-1, WIDE), wide[:, :, rows - REACH :].reshape(-1, WIDE), "lon", True
    )
    lo = lo.reshape(nvar, lev, REACH, ext)
    hi = hi.reshape(nvar, lev, REACH, ext)
    state_marg = jnp.concatenate([lo[..., cols:], marg, hi[..., cols:]], axis=2)
    state_lo = lo[..., 0:cols]
    state_hi = hi[..., 0:cols]

    g = turn(hidden_in)
    left, right = exchange(g[:, :, 0:SIDE], g[:, :, cols - SIDE :], "lat", False)
    row_lo = jnp.concatenate([g[:, 0], right[:, 0], left[:, 0]], axis=1)
    row_hi = jnp.concatenate([g[:, -1], right[:, -1], left[:, -1]], axis=1)
    is_even = lax.axis_index("lon") % 2 == 0
    got_a = swap(jnp.where(is_even, row_hi, row_lo), "lon", 0, True)
    got_b = swap(jnp.where(is_even, row_lo, row_hi), "lon", 1, True)

    ps_shape = (lev, rows + 2, 2 * VG, WIDE)
    ps_out = jax.ShapeDtypeStruct(ps_shape, f32)
    ps, pm = pl.pallas_call(
        inner_kernel,
        grid=(lev,),
        in_specs=[
            per_level(g.shape),
            per_level(right.shape),
            per_level(left.shape),
            full(w1_pair.shape),
            full(w2.shape),
            full((1, 2 * ch)),
            full((ext, 1)),
        ],
        out_specs=[per_level(ps_shape)] * 2,
        out_shape=[ps_out] * 2,
        scratch_shapes=[
            pltpu.VMEM((rows, ext + 2 * SIDE, ch), f32),
            pltpu.VMEM((rows, ext, 3 * ch), jnp.bfloat16),
            pltpu.VMEM((rows + 2, 6 * VG, WIDE), f32),
            pltpu.VMEM((rows + 2, 6 * VG, WIDE), f32),
        ],
        compiler_params=params,
        cost_estimate=pl.CostEstimate(flops=2 * lev * rows * ext * 9 * ch * ch, bytes_accessed=8 * 2**20, transcendentals=0),
    )(g, right, left, w1_pair, w2, jnp.concatenate([b1, b1], axis=1), keep_col)

    def pair_of(first):
        return lambda i: (i, first, 0, 0)

    g_pair = (1, 2, cols, ch)
    s_pair = (1, 2, SIDE, ch)
    top = rows // 2 - 1
    wire_shape = (lev, WIRE, WIDE)
    wire_out = jax.ShapeDtypeStruct(wire_shape, jnp.bfloat16)
    ps, pm, send_a, send_b = pl.pallas_call(
        edge_kernel,
        grid=(lev,),
        in_specs=[
            smem,
            pl.BlockSpec(g_pair, pair_of(0)),
            pl.BlockSpec(g_pair, pair_of(top)),
            pl.BlockSpec(s_pair, pair_of(0)),
            pl.BlockSpec(s_pair, pair_of(top)),
            pl.BlockSpec(s_pair, pair_of(0)),
            pl.BlockSpec(s_pair, pair_of(top)),
            per_level(got_a.shape),
            per_level(got_b.shape),
            full(w1_one.shape),
            full(w2.shape),
            full((1, ch)),
            full((ext, 1)),
            per_level(ps_shape),
            per_level(ps_shape),
        ],
        out_specs=[per_level(ps_shape)] * 2 + [per_level(wire_shape)] * 2,
        out_shape=[ps_out] * 2 + [wire_out] * 2,
        scratch_shapes=[
            pltpu.VMEM((6, ext + 2 * SIDE, ch), f32),
            pltpu.VMEM((6, ext, 3 * ch), jnp.bfloat16),
            pltpu.VMEM((6, 6 * VG, WIDE), f32),
            pltpu.VMEM((6, 6 * VG, WIDE), f32),
        ],
        compiler_params=params,
    )(even, g, g, right, right, left, left, got_a, got_b, w1_one, w2, b1, keep_col, ps, pm)

    wire_a = swap(send_a, "lon", 0, True)
    wire_b = swap(send_b, "lon", 1, True)

    def var_level(shape):
        return pl.BlockSpec((shape[0], 1) + shape[2:], lambda i: (0, i, 0, 0))

    vel_shape = (2 * nvar, lev, rows, cols)
    total = rows + 2 * REACH
    return pl.pallas_call(
        advect_kernel,
        grid=(lev,),
        in_specs=[
            smem,
            per_level(ps_shape),
            per_level(ps_shape),
            per_level(wire_shape),
            per_level(wire_shape),
            var_level(state.shape),
            var_level(state_lo.shape),
            var_level(state_hi.shape),
            var_level(state_marg.shape),
            full(b2.shape),
            full(lat_main.shape),
            full(lat_marg.shape),
        ],
        out_specs=[var_level(vel_shape), var_level(state.shape)],
        out_shape=[jax.ShapeDtypeStruct(vel_shape, f32), jax.ShapeDtypeStruct(state.shape, f32)],
        scratch_shapes=[pltpu.VMEM((2, total * VG, WIDE), f32), pltpu.VMEM((rows * VG, WIDE), f32)],
        compiler_params=params,
    )(even, ps, pm, wire_a, wire_b, state, state_lo, state_hi, state_marg, b2, lat_main, lat_marg)


def solution(mesh):
    placed = (P(None, None, "lon", "lat"), P(), P(), P(), P(), P(None, None, "lon", "lat"))
    return jax.shard_map(
        body,
        mesh=mesh,
        in_specs=placed,
        out_specs=(P(None, None, "lon", "lat"), P(None, None, "lon", "lat")),
        check_vma=False,
    )
```

```python
import functools
import math

import jax
import jax.numpy as jnp
from jax import lax
from jax.experimental import pallas as pl
from jax.experimental.pallas import tpu as pltpu
from jax.sharding import PartitionSpec as P

time_step = 0.5
speed_cap = 0.6
cos_floor = 0.5

SIDE = 8
SLOT = 2 * SIDE
WIDE = 128
REACH = 4
VG = 8
VMEM_LIMIT = 40 * 2**20
f32 = jnp.float32
bf16 = jnp.bfloat16


def swap_pairs(count, first, closed):
    pairs = []
    for low in range(first, count, 2):
        high = low + 1
        if high >= count and not closed:
            continue
        pairs += [(low, high % count), (high % count, low)]
    return pairs


def swap(block, axis, first, closed):
    return lax.ppermute(block, axis, swap_pairs(lax.axis_size(axis), first, closed))


def place(row, rows):
    half, par = row // 2, row % 2
    own = 0 <= half < rows // 2
    return (0 if own else 2) + par, SLOT * (half % (rows // 2))


def lanes(shape):
    return lax.broadcasted_iota(jnp.int32, shape, len(shape) - 1)


def roll(x, by):
    by = by % WIDE
    return pltpu.roll(x, by, x.ndim - 1) if by else x


def col_before(mains, sides, at):
    lane = lanes(next(iter(mains.values())).shape)
    new_sides = {k: roll(s, 1) for k, s in sides.items()}
    new_mains = {}
    for row, main in mains.items():
        k, base = at(row)
        new_mains[row] = jnp.where(lane == 0, roll(sides[k], -(base + SLOT - 1)), roll(main, 1))
        new_sides[k] = jnp.where(lane == base, roll(main, base + 1), new_sides[k])
    return new_mains, new_sides


def col_after(mains, sides, at):
    lane = lanes(next(iter(mains.values())).shape)
    new_sides = {k: roll(s, -1) for k, s in sides.items()}
    new_mains = {}
    for row, main in mains.items():
        k, base = at(row)
        new_mains[row] = jnp.where(lane == WIDE - 1, roll(sides[k], WIDE - 1 - base), roll(main, -1))
        new_sides[k] = jnp.where(lane == base + SLOT - 1, roll(main, base + SLOT - 1), new_sides[k])
    return new_mains, new_sides


def join_taps(mains, sides, at):
    def part(group, b):
        return {k: x[b * SLOT : (b + 1) * SLOT] for k, x in group.items()}

    mb, sb = col_before(part(mains, 0), part(sides, 0), at)
    ma, sa = col_after(part(mains, 2), part(sides, 2), at)
    mm, sm = part(mains, 1), part(sides, 1)
    return {r: mb[r] + mm[r] + ma[r] for r in mains}, {k: sb[k] + sm[k] + sa[k] for k in sides}


def two_terms(x):
    first = x.astype(bf16)
    return [first, (x - first.astype(f32)).astype(bf16)]


def nt(lhs, rhs):
    return lax.dot_general(lhs, rhs, (((1,), (1,)), ((), ())), preferred_element_type=f32)


def silu(s):
    return s / (1.0 + jnp.exp(-s))


def turn_kernel(flag_ref, x_ref, st_ref, g_ref, st8_ref, outa_ref, outb_ref, s_ref, v_ref):
    chans, rows, cols = x_ref.shape[1:]
    nvar = st_ref.shape[0]
    even = flag_ref[1] == 0
    s_ref[...] = x_ref[0].astype(f32).reshape(chans * rows, cols)
    for row in range(rows):
        block = s_ref[pl.ds(row, chans, stride=rows), :].T
        g_ref[0, row] = block.astype(bf16)
        first, last = block[0:SIDE], block[cols - SIDE :]
        v_ref[0, row * SIDE : (row + 1) * SIDE] = jnp.where(even, last, first)
        v_ref[1, row * SIDE : (row + 1) * SIDE] = jnp.where(even, first, last)
    outa_ref[0, 0 : rows * SIDE] = v_ref[0].astype(bf16)
    outb_ref[0, 0 : rows * SIDE] = v_ref[1].astype(bf16)
    for n in range(nvar):
        s_ref[pl.ds(n, rows, stride=VG), :] = st_ref[n, 0]
    lane = lanes((VG, WIDE))
    toright = [jnp.zeros((VG, WIDE), f32)] * 2
    toleft = [jnp.zeros((VG, WIDE), f32)] * 2
    for row in range(rows):
        block = s_ref[row * VG : (row + 1) * VG]
        block = jnp.where(lax.broadcasted_iota(jnp.int32, (VG, WIDE), 0) < nvar, block, 0.0)
        st8_ref[0, row] = block
        par, base = place(row, rows)
        mine = lane // SLOT == base // SLOT
        toleft[par] = jnp.where(mine, roll(block, base), toleft[par])
        toright[par] = jnp.where(mine, roll(block, base + SLOT), toright[par])
    for out, pick in ((outa_ref, [jnp.where(even, r, l) for r, l in zip(toright, toleft)]),
                      (outb_ref, [jnp.where(even, l, r) for r, l in zip(toright, toleft)])):
        out[0, rows * SIDE :] = jnp.concatenate(two_terms(pick[0]) + two_terms(pick[1]), axis=0)


def state_sides(right, left, start):
    both = [x[start:].astype(f32) for x in (right, left)]
    out = []
    for par in range(2):
        r, l = (x[2 * par * VG : (2 * par + 1) * VG] + x[(2 * par + 1) * VG : (2 * par + 2) * VG] for x in both)
        out.append(jnp.where(lanes(r.shape) % SLOT < SIDE, r, l))
    return out


def sides_of(even, a_ref, b_ref):
    a, b = a_ref[0], b_ref[0]
    return jnp.where(even, a, b), jnp.where(even, b, a)


def pack_kernel(flag_ref, a_ref, b_ref, glo_ref, ghi_ref, outa_ref, outb_ref, sst_ref):
    rows = (a_ref.shape[1] - 4 * VG) // SIDE
    cols = glo_ref.shape[2]
    even = flag_ref[0] == 0
    right, left = sides_of(flag_ref[1] == 0, a_ref, b_ref)
    st = state_sides(right, left, rows * SIDE)
    sst_ref[0, 0], sst_ref[0, 1] = st
    lane = lanes((VG, WIDE))
    st_lo = jnp.where(lane < 2 * SLOT, st[0], roll(st[1], 2 * SLOT))
    st_hi = jnp.where(lane >= WIDE - 2 * SLOT, st[0], roll(st[1], -2 * SLOT))

    def wire(g_ref, row, s):
        side = [x[row * SIDE : (row + 1) * SIDE] for x in (right, left)]
        return g_ref[0, 0], jnp.concatenate(side + two_terms(s), axis=0)

    lo, hi = wire(glo_ref, 0, st_lo), wire(ghi_ref, rows - 1, st_hi)
    for out, first, second in ((outa_ref, hi, lo), (outb_ref, lo, hi)):
        out[0, 0:cols] = jnp.where(even, first[0], second[0])
        out[0, cols:] = jnp.where(even, first[1], second[1])


def lay_row(e_ref, slot, s_ref, to, main, right, left):
    cols, ch = main.shape
    ext = cols + SLOT
    main = main.astype(f32)
    left = left.astype(f32)
    e_ref[slot, 0:SIDE] = left
    e_ref[slot, SIDE : SIDE + cols] = main
    e_ref[slot, SIDE + cols : SLOT + cols] = right.astype(f32)
    e_ref[slot, SLOT + cols : SLOT + SIDE + cols] = left
    e_ref[slot, SLOT + SIDE + cols : 2 * SLOT + cols] = main[0:SIDE]
    for b in range(3):
        s_ref[to, :, b * ch : (b + 1) * ch] = e_ref[slot, pl.ds(SIDE - 1 + b, ext), :].astype(bf16)


def inner_kernel(flag_ref, g_ref, a_ref, b_ref, w1_ref, w2_ref, b1_ref, keep_ref, ps_ref, pm_ref,
                 e_ref, se_ref, so_ref, h_ref, hs_ref):
    rows, cols, ch = g_ref.shape[1:]
    half = rows // 2
    right, left = sides_of(flag_ref[1] == 0, a_ref, b_ref)
    right, left = right.astype(f32), left.astype(f32)
    for row in range(rows):
        side = slice(row * SIDE, (row + 1) * SIDE)
        lay_row(e_ref, row, se_ref if row % 2 == 0 else so_ref, row // 2, g_ref[0, row], right[side], left[side])
    none = jnp.zeros((cols, ch), bf16)
    for at in (0, 1, rows, rows + 1):
        h_ref[at] = none
    for par in range(2):
        for at in (0, half):
            hs_ref[par, at * SLOT : (at + 1) * SLOT] = none[0:SLOT]
    for m in range(half - 1):
        lhs = jnp.concatenate([se_ref[m], so_ref[m], se_ref[m + 1], so_ref[m + 1]], axis=1)
        acc = jnp.dot(lhs, w1_ref[...], preferred_element_type=f32) + b1_ref[...]
        hid = silu(acc)
        for k in range(2):
            here = hid[:, k * ch : (k + 1) * ch]
            h_ref[2 * m + 2 + k] = here[0:cols].astype(bf16)
            hs_ref[k, (m + 1) * SLOT : (m + 2) * SLOT] = (here[cols:] * keep_ref[...]).astype(bf16)
    mains = {}
    for m in range(half):
        q = nt(w2_ref[...], jnp.concatenate([h_ref[2 * m + r] for r in range(4)], axis=1))
        for k in range(2):
            mains[2 * m + k] = q[k * 3 * SLOT : (k + 1) * 3 * SLOT]
    part = [hs_ref[r % 2, (r // 2) * SLOT : (r // 2 + half) * SLOT] for r in range(4)]
    q = nt(w2_ref[...], jnp.concatenate(part, axis=1))
    sides = {k: q[k * 3 * SLOT : (k + 1) * 3 * SLOT] for k in range(2)}
    mains, sides = join_taps(mains, sides, lambda row: place(row, rows))
    for row in range(rows):
        ps_ref[0, row] = mains[row]
    for k in range(2):
        pm_ref[0, k] = sides[k]


def edge_kernel(flag_ref, g0_ref, g1_ref, la_ref, lb_ref, a_ref, b_ref, w1_ref, w2_ref, b1_ref, keep_ref,
                ps0_ref, ps1_ref, pmi_ref, pe_ref, pm_ref, outa_ref, outb_ref, e_ref, s_ref, z_ref):
    cols, ch = g0_ref.shape[2:]
    rows = (la_ref.shape[1] - 4 * VG) // SIDE
    ext = cols + SLOT
    even = flag_ref[0] == 0
    right, left = sides_of(flag_ref[1] == 0, la_ref, lb_ref)
    right, left = right.astype(f32), left.astype(f32)
    got_a = a_ref[0].astype(f32)
    got_b = b_ref[0].astype(f32)
    low = jnp.where(even, got_b, got_a)
    high = jnp.where(even, got_a, got_b)
    for to, got in ((0, low), (5, high)):
        lay_row(e_ref, to, s_ref, to, got[0:cols], got[cols : cols + SIDE], got[cols + SIDE : ext])
    for k in range(2):
        for to, g_ref, row in ((1 + k, g0_ref, k), (3 + k, g1_ref, rows - 2 + k)):
            side = slice(row * SIDE, (row + 1) * SIDE)
            lay_row(e_ref, to, s_ref, to, g_ref[0, k], right[side], left[side])
    z_ref[...] = jnp.zeros_like(z_ref)
    mains = {}
    for k in range(2):
        lhs = jnp.concatenate([s_ref[3 * k + r] for r in range(3)], axis=1)
        acc = jnp.dot(lhs, w1_ref[...], preferred_element_type=f32) + b1_ref[...]
        hid = silu(acc)
        z_ref[k * SLOT : (k + 1) * SLOT] = (hid[cols:] * keep_ref[...]).astype(bf16)
        q = nt(w2_ref[...], hid[0:cols].astype(bf16))
        for a in range(3):
            mains[k * (rows - 1) + 1 - a] = q[a * 3 * SLOT : (a + 1) * 3 * SLOT]
    q = nt(w2_ref[...], z_ref[...])
    sides = {a: q[a * 3 * SLOT : (a + 1) * 3 * SLOT] for a in range(3)}

    def at(row):
        k = row > rows // 2
        return k * (rows - 1) + 1 - row, k * SLOT

    mains, sides = join_taps(mains, sides, at)
    for row, own in ((0, ps0_ref[0, 0]), (1, ps0_ref[0, 1]), (rows - 2, ps1_ref[0, 2]), (rows - 1, ps1_ref[0, 3])):
        mains[row] = mains[row] + own
    for k, row in enumerate((-1, 0, 1, rows - 2, rows - 1, rows)):
        pe_ref[0, k] = mains[row]
    lane = lanes((2 * VG, WIDE))
    begin, end = lane < SLOT, lane >= WIDE - SLOT
    to_end = -2 * SLOT
    own_e = pmi_ref[0, 0] + jnp.where(begin, sides[1], 0.0) + jnp.where(end, roll(sides[2], to_end), 0.0)
    own_o = pmi_ref[0, 1] + jnp.where(begin, sides[0], 0.0) + jnp.where(end, roll(sides[1], to_end), 0.0)
    next_e = jnp.where(begin, roll(sides[0], -SLOT), 0.0)
    prev_o = jnp.where(end, roll(sides[2], -SLOT), 0.0)
    for k, x in enumerate((own_e, own_o, next_e, prev_o)):
        pm_ref[0, k] = x
    side_lo = jnp.where(lane < 2 * SLOT, own_e, jnp.where(lane < 4 * SLOT, roll(own_o, 2 * SLOT), prev_o))
    side_hi = jnp.where(lane >= WIDE - 2 * SLOT, own_e, jnp.where(lane >= WIDE - 4 * SLOT, roll(own_o, -2 * SLOT), next_e))
    out_lo = jnp.concatenate([mains[-1], mains[0], mains[1], ps0_ref[0, 2], side_lo, ps0_ref[0, 3]], axis=0)
    out_hi = jnp.concatenate([mains[rows], mains[rows - 1], mains[rows - 2], ps1_ref[0, 1], side_hi, ps1_ref[0, 0]], axis=0)
    outa_ref[0] = jnp.where(even, out_hi, out_lo).astype(bf16)
    outb_ref[0] = jnp.where(even, out_lo, out_hi).astype(bf16)


def advect_kernel(flag_ref, ps_ref, pe_ref, pm_ref, a_ref, b_ref, st8_ref, sst_ref, sa_ref, sb_ref, ha_ref, hb_ref,
                  b2_ref, lat_ref, lats_ref, vel_ref, ten_ref, x_ref, out_ref):
    rows = st8_ref.shape[1]
    nvar = ten_ref.shape[0]
    even = flag_ref[0] == 0
    lane16 = lanes((2 * VG, WIDE))
    lane = lanes((VG, WIDE))
    pair = 2 * VG

    def halos(xa, xb):
        return jnp.where(even, xb, xa), jnp.where(even, xa, xb)

    lo, hi = halos(a_ref[0].astype(f32), b_ref[0].astype(f32))
    main = {row: ps_ref[0, row] for row in range(2, rows - 2)}
    for k, row in enumerate((-1, 0, 1, rows - 2, rows - 1, rows)):
        main[row] = pe_ref[0, k]
    for k in range(REACH + 1):
        there = slice(k * pair, (k + 1) * pair) if k < REACH else slice((k + 1) * pair, (k + 2) * pair)
        for got, row in ((lo, -k), (hi, rows - 1 + k)):
            main[row] = main[row] + got[there] if row in main else got[there]
    slo, shi = (got[REACH * pair : (REACH + 1) * pair] for got in (lo, hi))
    zero = jnp.zeros((pair, WIDE), f32)
    last, front = lane16 >= WIDE - 2 * SLOT, lane16 < 2 * SLOT
    side = {
        0: pm_ref[0, 0] + jnp.where(lane16 < SLOT, slo, zero),
        1: pm_ref[0, 1] + jnp.where(lane16 >= WIDE - SLOT, shi, zero),
        2: pm_ref[0, 2] + jnp.where(last, slo, jnp.where(front, shi, zero)),
        3: pm_ref[0, 3] + jnp.where(last, roll(slo, 2 * SLOT), jnp.where(front, roll(shi, -2 * SLOT), zero)),
    }
    bias = b2_ref[...]
    main = {r: speed_cap * jnp.tanh(x + bias) for r, x in main.items()}
    side = {k: speed_cap * jnp.tanh(x + bias) * lats_ref[2:3] for k, x in side.items()}
    for part in range(2):
        for row in range(rows):
            out_ref[part, row * VG : (row + 1) * VG] = main[row][part * VG : (part + 1) * VG]
        for n in range(nvar):
            vel_ref[2 * n + part, 0] = out_ref[part, pl.ds(n, rows, stride=VG), :]

    x_ref[...] = jnp.zeros_like(x_ref)
    for n in range(nvar):
        down, up = halos(sa_ref[n, 0], sb_ref[n, 0])
        x_ref[0, pl.ds(n, REACH, stride=VG), :] = down
        x_ref[1, pl.ds(n, REACH, stride=VG), :] = up
    q0 = {row: st8_ref[0, row] for row in range(rows)}
    for k in range(REACH):
        q0[k - REACH] = x_ref[0, k * VG : (k + 1) * VG]
        q0[rows + k] = x_ref[1, k * VG : (k + 1) * VG]
    hlo, hhi = halos(ha_ref[0].astype(f32), hb_ref[0].astype(f32))
    hlo, hhi = hlo[0:VG] + hlo[VG:], hhi[0:VG] + hhi[VG:]
    last, front = lane >= WIDE - 2 * SLOT, lane < 2 * SLOT
    nil = jnp.zeros((VG, WIDE), f32)
    s0 = {
        0: sst_ref[0, 0],
        1: sst_ref[0, 1],
        2: jnp.where(last, hlo, jnp.where(front, hhi, nil)),
        3: jnp.where(last, roll(hlo, 2 * SLOT), jnp.where(front, roll(hhi, -2 * SLOT), nil)),
    }

    def at(row):
        return place(row, rows)

    def side_rows(s):
        def turned(own, halo, by, first):
            own, halo = roll(own, by), roll(halo, by)
            return jnp.where(first, halo, own), jnp.where(first, own, halo)

        odd_back = turned(s[1], s[3], SLOT, lane < SLOT)
        even_on = turned(s[0], s[2], -SLOT, lane >= WIDE - SLOT)
        before = {0: odd_back[0], 2: odd_back[1], 1: s[0], 3: s[2]}
        after = {0: s[1], 2: s[3], 1: even_on[0], 3: even_on[1]}
        return before, after

    u = {r: x[0:VG] for r, x in main.items()}
    us = {k: x[0:VG] for k, x in side.items()}
    inside = range(1 - REACH, rows + REACH - 1)
    v = {r: main[r][VG:] for r in inside}
    vs = {k: x[VG:] for k, x in side.items()}
    cosine, metric = lat_ref[0:1], lat_ref[1:2]
    cosine_s, metric_s = lats_ref[0:1], lats_ref[1:2]
    flux = {r: x * cosine for r, x in v.items()}
    flux_s = {k: x * cosine_s for k, x in vs.items()}
    fb, fbs = col_before(flux, flux_s, at)
    fa, fas = col_after(flux, flux_s, at)
    ub, ua = side_rows(us)

    def coefs(m, uu, vv, udiff, vdiff):
        div = m * (udiff * 0.5 + vdiff * 0.5)
        cl = m * jnp.maximum(uu, 0.0)
        cr = -(m * jnp.minimum(uu, 0.0))
        cd = jnp.maximum(vv, 0.0)
        cu = -jnp.minimum(vv, 0.0)
        return -(cl + cr + cd + cu + div), cl, cr, cd, cu

    cm = {r: coefs(metric, u[r], v[r], u[r + 1] - u[r - 1], fa[r] - fb[r]) for r in inside}
    cs = {k: coefs(metric_s, us[k], vs[k], ua[k] - ub[k], fas[k] - fbs[k]) for k in range(4)}

    def stencil(c, x, left, right, down, up):
        return c[0] * x + c[1] * left + c[2] * right + c[3] * down + c[4] * up

    def rate(q, s, depth):
        centre = {r: q[r] for r in range(depth - REACH, rows + REACH - depth)}
        qb, sb = col_before(centre, s, at)
        qa, sa = col_after(centre, s, at)
        rb, ra = side_rows(s)
        out = {r: stencil(cm[r], q[r], q[r - 1], q[r + 1], qb[r], qa[r]) for r in centre}
        if depth == REACH:
            return out, None
        return out, {k: stencil(cs[k], s[k], rb[k], ra[k], sb[k], sa[k]) for k in range(4)}

    def moved(rates, by):
        return {r: q0[r] + by * x for r, x in rates[0].items()}, {k: s0[k] + by * x for k, x in rates[1].items()}

    one = rate(q0, s0, 1)
    two = rate(*moved(one, 0.5 * time_step), 2)
    three = rate(*moved(two, 0.5 * time_step), 3)
    four = rate(*moved(three, time_step), 4)
    for row in range(rows):
        ten = (one[0][row] + 2.0 * two[0][row] + 2.0 * three[0][row] + four[0][row]) / 6.0
        out_ref[0, row * VG : (row + 1) * VG] = ten
    for n in range(nvar):
        ten_ref[n, 0] = out_ref[0, pl.ds(n, rows, stride=VG), :]


def full(shape):
    return pl.BlockSpec(shape, lambda *i: (0,) * len(shape))


def per_level(shape):
    return pl.BlockSpec((1,) + shape[1:], lambda i: (i,) + (0,) * (len(shape) - 1))


def level_part(shape, index):
    return pl.BlockSpec((1,) + shape, lambda i: (i, index) + (0,) * (len(shape) - 1))


def var_level(shape):
    return pl.BlockSpec((shape[0], 1) + shape[2:], lambda i: (0, i, 0, 0))


def body(hidden_in, w_conv1, b_conv1, w_conv2, b_conv2, state):
    lev, ch, rows, cols = hidden_in.shape
    nvar = state.shape[0]
    ext = cols + SLOT
    half = rows // 2
    params = pltpu.CompilerParams(vmem_limit_bytes=VMEM_LIMIT)
    smem = pl.BlockSpec(memory_space=pltpu.SMEM)
    sds = jax.ShapeDtypeStruct

    def call(kernel, ins, outs, scratch, args, cost=None):
        return pl.pallas_call(
            kernel,
            grid=(lev,),
            in_specs=ins,
            out_specs=[per_level(o.shape) if len(o.shape) == 3 or o.shape[0] == lev else var_level(o.shape) for o in outs],
            out_shape=outs,
            scratch_shapes=scratch,
            compiler_params=params,
            cost_estimate=cost,
        )(*args)

    taps = w_conv1.reshape(3, 3 * ch, ch)
    w1_pair = jnp.pad(taps.reshape(9 * ch, ch), ((0, 3 * ch), (0, 0)))
    w1_pair = jnp.concatenate([w1_pair, jnp.pad(taps.reshape(9 * ch, ch), ((3 * ch, 0), (0, 0)))], axis=1)
    w1_one = taps.reshape(9 * ch, ch)
    w2 = w_conv2.reshape(3, 3, ch, nvar, 2).transpose(0, 1, 4, 3, 2)
    w2 = jnp.pad(w2, ((0, 0), (0, 0), (0, 0), (0, VG - nvar), (0, 0))).reshape(3, 3 * SLOT, ch)
    w2_row = w2.transpose(1, 0, 2).reshape(3 * SLOT, 3 * ch)
    w2_pair = jnp.concatenate([jnp.pad(w2_row, ((0, 0), (0, ch))), jnp.pad(w2_row, ((0, 0), (ch, 0)))], axis=0)
    w2_one = w2.reshape(9 * SLOT, ch)
    b1 = b_conv1.reshape(1, ch)
    b2 = jnp.pad(b_conv2.reshape(nvar, 2).T, ((0, 0), (0, VG - nvar))).reshape(2 * VG, 1)
    b2 = jnp.broadcast_to(b2, (2 * VG, WIDE))

    n_lat = cols * lax.axis_size("lat")
    side_place = jnp.concatenate([jnp.arange(cols, cols + SIDE), jnp.arange(-SIDE, 0)]).astype(jnp.int32)

    def latitudes(place_in):
        place_in = place_in + lax.axis_index("lat") * cols
        keep = ((place_in >= 0) & (place_in < n_lat)).astype(f32)
        phi = (place_in.astype(f32) + 0.5) * (math.pi / n_lat) - 0.5 * math.pi
        cosine = jnp.maximum(jnp.cos(phi), cos_floor)
        return jnp.pad(jnp.stack([cosine, 1.0 / cosine, keep]), ((0, VG - 3), (0, 0)))

    lat_main = latitudes(jnp.arange(cols, dtype=jnp.int32))
    lat_side = latitudes(jnp.tile(side_place, WIDE // SLOT))
    keep = jnp.broadcast_to(lat_side[2, 0:SLOT].reshape(SLOT, 1), (SLOT, ch))
    is_even = lax.axis_index("lon") % 2 == 0
    flags = jnp.stack([lax.axis_index("lon") % 2, lax.axis_index("lat") % 2]).astype(jnp.int32)

    st_lo, st_hi = state[:, :, 0:REACH], state[:, :, rows - REACH :]
    state_a = swap(jnp.where(is_even, st_hi, st_lo), "lon", 0, True)
    state_b = swap(jnp.where(is_even, st_lo, st_hi), "lon", 1, True)

    lat_wire = (lev, rows * SIDE + 4 * VG, WIDE)
    g, st8, lat_a, lat_b = call(
        turn_kernel,
        [smem, per_level(hidden_in.shape), var_level(state.shape)],
        [sds((lev, rows, cols, ch), bf16), sds((lev, rows, VG, WIDE), f32), sds(lat_wire, bf16), sds(lat_wire, bf16)],
        [pltpu.VMEM((ch * rows, cols), f32), pltpu.VMEM((2, rows * SIDE, ch), f32)],
        (flags, hidden_in, state),
    )
    lat_a = swap(lat_a, "lat", 0, False)
    lat_b = swap(lat_b, "lat", 1, False)

    lon_wire = (lev, cols + 2 * SLOT, WIDE)
    lon_a, lon_b, side_state = call(
        pack_kernel,
        [smem, per_level(lat_wire), per_level(lat_wire), level_part((1, cols, ch), 0), level_part((1, cols, ch), rows - 1)],
        [sds(lon_wire, bf16), sds(lon_wire, bf16), sds((lev, 2, VG, WIDE), f32)],
        [],
        (flags, lat_a, lat_b, g, g),
    )
    lon_a = swap(lon_a, "lon", 0, True)
    lon_b = swap(lon_b, "lon", 1, True)

    ps_shape = (lev, rows, 2 * VG, WIDE)
    pm_shape = (lev, 2, 2 * VG, WIDE)
    ps, pm = call(
        inner_kernel,
        [smem, per_level(g.shape), per_level(lat_wire), per_level(lat_wire), full(w1_pair.shape), full(w2_pair.shape),
         full((1, 2 * ch)), full((SLOT, ch))],
        [sds(ps_shape, f32), sds(pm_shape, f32)],
        [
            pltpu.VMEM((rows, cols + 2 * SLOT, ch), f32),
            pltpu.VMEM((half, ext, 3 * ch), bf16),
            pltpu.VMEM((half, ext, 3 * ch), bf16),
            pltpu.VMEM((rows + 2, cols, ch), bf16),
            pltpu.VMEM((2, (half + 1) * SLOT, ch), bf16),
        ],
        (flags, g, lat_a, lat_b, w1_pair, w2_pair, jnp.concatenate([b1, b1], axis=1), keep),
        pl.CostEstimate(flops=2 * lev * rows * ext * 9 * ch * ch, bytes_accessed=8 * 2**20, transcendentals=0),
    )

    g_pair, four = (2, cols, ch), (4, 2 * VG, WIDE)
    wire = (lev, 2 * VG * (REACH + 2), WIDE)
    pe_shape = (lev, 6, 2 * VG, WIDE)
    pe, pm, out_a, out_b = call(
        edge_kernel,
        [smem, level_part(g_pair, 0), level_part(g_pair, half - 1), per_level(lat_wire), per_level(lat_wire),
         per_level(lon_wire), per_level(lon_wire), full(w1_one.shape), full(w2_one.shape), full((1, ch)), full((SLOT, ch)),
         level_part(four, 0), level_part(four, rows // 4 - 1), per_level(pm_shape)],
        [sds(pe_shape, f32), sds((lev, 4, 2 * VG, WIDE), f32), sds(wire, bf16), sds(wire, bf16)],
        [
            pltpu.VMEM((6, cols + 2 * SLOT, ch), f32),
            pltpu.VMEM((6, ext, 3 * ch), bf16),
            pltpu.VMEM((WIDE, ch), bf16),
        ],
        (flags, g, g, lat_a, lat_b, lon_a, lon_b, w1_one, w2_one, b1, keep, ps, ps, pm),
    )
    out_a = swap(out_a, "lon", 0, True)
    out_b = swap(out_b, "lon", 1, True)

    tail = level_part((SLOT, WIDE), (cols + SLOT) // SLOT)
    return call(
        advect_kernel,
        [smem, per_level(ps_shape), per_level(pe_shape), per_level((lev, 4, 2 * VG, WIDE)), per_level(wire), per_level(wire),
         per_level(st8.shape), per_level(side_state.shape), var_level(state_a.shape), var_level(state_b.shape), tail, tail,
         full(b2.shape), full(lat_main.shape), full(lat_side.shape)],
        [sds((2 * nvar, lev, rows, cols), f32), sds(state.shape, f32)],
        [pltpu.VMEM((2, REACH * VG, WIDE), f32), pltpu.VMEM((2, rows * VG, WIDE), f32)],
        (flags, ps, pe, pm, out_a, out_b, st8, side_state, state_a, state_b, lon_a, lon_b, b2, lat_main, lat_side),
    )


def solution(mesh):
    placed = (P(None, None, "lon", "lat"), P(), P(), P(), P(), P(None, None, "lon", "lat"))
    return jax.shard_map(
        body,
        mesh=mesh,
        in_specs=placed,
        out_specs=(P(None, None, "lon", "lat"), P(None, None, "lon", "lat")),
        check_vma=False,
    )
```

```python
import functools
import math

import jax
import jax.numpy as jnp
from jax import lax
from jax.experimental import pallas as pl
from jax.experimental.pallas import tpu as pltpu
from jax.sharding import PartitionSpec as P

time_step = 0.5
speed_cap = 0.6
cos_floor = 0.5

SIDE = 8
SLOT = 2 * SIDE
WIDE = 128
REACH = 4
VG = 8
VMEM_LIMIT = 24 * 2**20
EDGE_LEVELS = 4
SIDE_LEVELS = 2
PARTS = 1
f32 = jnp.float32
bf16 = jnp.bfloat16


def swap_pairs(count, first, closed):
    pairs = []
    for low in range(first, count, 2):
        high = low + 1
        if high >= count and not closed:
            continue
        pairs += [(low, high % count), (high % count, low)]
    return pairs


def swap(block, axis, first, closed):
    return lax.ppermute(block, axis, swap_pairs(lax.axis_size(axis), first, closed))


def place(row, rows):
    half, par = row // 2, row % 2
    own = 0 <= half < rows // 2
    return (0 if own else 2) + par, SLOT * (half % (rows // 2))


def lanes(shape):
    return lax.broadcasted_iota(jnp.int32, shape, len(shape) - 1)


def roll(x, by):
    by = by % WIDE
    return pltpu.roll(x, by, x.ndim - 1) if by else x


def col_before(mains, sides, at):
    lane = lanes(next(iter(mains.values())).shape)
    new_sides = {k: roll(s, 1) for k, s in sides.items()}
    new_mains = {}
    for row, main in mains.items():
        k, base = at(row)
        new_mains[row] = jnp.where(lane == 0, roll(sides[k], 1 - base - SIDE), roll(main, 1))
        new_sides[k] = jnp.where(lane == base + SIDE, roll(main, base + SIDE + 1), new_sides[k])
    return new_mains, new_sides


def col_after(mains, sides, at):
    lane = lanes(next(iter(mains.values())).shape)
    new_sides = {k: roll(s, -1) for k, s in sides.items()}
    new_mains = {}
    for row, main in mains.items():
        k, base = at(row)
        new_mains[row] = jnp.where(lane == WIDE - 1, roll(sides[k], WIDE - 1 - base - SIDE), roll(main, -1))
        new_sides[k] = jnp.where(lane == base + SIDE - 1, roll(main, base + SIDE - 1), new_sides[k])
    return new_mains, new_sides


def join_taps(x):
    return roll(x[0:SLOT], 1) + x[SLOT : 2 * SLOT] + roll(x[2 * SLOT : 3 * SLOT], -1)


def mix(first, second):
    return jnp.where(lanes(first.shape) % SLOT < SIDE, first, second)


def add_columns(main, side, base):
    lane = lanes(main.shape)
    return main + jnp.where((lane < SIDE) | (lane >= WIDE - SIDE), roll(side, -(base + SIDE)), 0.0)


def two_terms(x):
    first = x.astype(bf16)
    return [first, (x - first.astype(f32)).astype(bf16)]


def nt(lhs, rhs):
    return lax.dot_general(lhs, rhs, (((1,), (1,)), ((), ())), preferred_element_type=f32)


def silu(s):
    return s / (1.0 + jnp.exp(-s))


def shifted(e_ref, start, s_ref, to, count, first=0):
    ch = e_ref.shape[-1]
    for b in range(3):
        lane0 = first + b * ch
        s_ref[to, :, lane0 : lane0 + ch] = e_ref[pl.ds(start - 1 + b, count), :].astype(bf16)


def prep_kernel(flag_ref, n_lat, b2_ref, x_ref, st_ref, w1_ref, w2_ref, b1_ref,
                outa_ref, outb_ref, w1p_ref, w2p_ref, w2o_ref, w2e_ref, b1p_ref, b2o_ref, lat_ref, lats_ref, keep_ref,
                x32_ref, w2s_ref):
    levels, ch, rows, cols = x_ref.shape
    nvar = st_ref.shape[0]
    even = flag_ref[0] == 0

    def one(lv, carry):
        x32_ref[...] = x_ref[lv].astype(f32).reshape(ch * rows, cols)
        lo, hi = (x32_ref[pl.ds(row, ch, stride=rows), :].astype(bf16) for row in (0, rows - 1))
        outa_ref[lv, 0:ch] = jnp.where(even, hi, lo)
        outb_ref[lv, 0:ch] = jnp.where(even, lo, hi)
        x32_ref[0 : 2 * REACH * VG] = jnp.zeros((2 * REACH * VG, WIDE), f32)
        for n in range(nvar):
            x32_ref[pl.ds(n, REACH, stride=VG), :] = st_ref[n, lv, 0:REACH]
            x32_ref[pl.ds(REACH * VG + n, REACH, stride=VG), :] = st_ref[n, lv, rows - REACH :]
        lo = x32_ref[0 : REACH * VG]
        hi = x32_ref[REACH * VG : 2 * REACH * VG]
        outa_ref[lv, ch:] = jnp.concatenate(two_terms(jnp.where(even, hi, lo)), axis=0)
        outb_ref[lv, ch:] = jnp.concatenate(two_terms(jnp.where(even, lo, hi)), axis=0)
        return carry

    lax.fori_loop(0, levels, one, 0)
    size = w1_ref.shape[0]
    w1p_ref[0:size, 0:ch] = w1_ref[...]
    w1p_ref[size:, 0:ch] = jnp.zeros((3 * ch, ch), bf16)
    w1p_ref[0 : 3 * ch, ch:] = jnp.zeros((3 * ch, ch), bf16)
    w1p_ref[3 * ch :, ch:] = w1_ref[...]
    b1p_ref[:, 0:ch] = b1_ref[...]
    b1p_ref[:, ch:] = b1_ref[...]
    w2p_ref[...] = jnp.zeros_like(w2p_ref)
    w2s_ref[0 : 2 * VG] = jnp.zeros((2 * VG, ch), f32)
    for a in range(3):
        for b in range(3):
            w2s_ref[2 * VG : 2 * VG + 2 * nvar] = w2_ref[3 * a + b].astype(f32)
            for part in range(2):
                w2s_ref[part * VG : part * VG + nvar] = w2s_ref[pl.ds(2 * VG + part, nvar, stride=2), :]
            here = w2s_ref[0 : 2 * VG].astype(bf16)
            at = 3 * a + b
            w2o_ref[at * SLOT : (at + 1) * SLOT] = here
            for k in range(2):
                first = (3 * k + b) * SLOT
                w2p_ref[first : first + SLOT, (a + k) * ch : (a + k + 1) * ch] = here
            if a != 1:
                first = (3 * (a // 2) + b) * SLOT
                w2e_ref[first : first + SLOT] = here
    b2o_ref[...] = jnp.zeros_like(b2o_ref)
    for v in range(2 * nvar):
        row = (v % 2) * VG + v // 2
        b2o_ref[row : row + 1] = jnp.full((1, WIDE), b2_ref[v], f32)

    def table(place_in):
        place_in = place_in + flag_ref[2] * cols
        keep = ((place_in >= 0) & (place_in < n_lat)).astype(f32)
        phi = (place_in.astype(f32) + 0.5) * (math.pi / n_lat) - 0.5 * math.pi
        cosine = jnp.maximum(jnp.cos(phi), cos_floor)
        return cosine, 1.0 / cosine, keep

    lane = lanes((VG, WIDE))
    slot = lane % SLOT
    for ref, place_in in ((lat_ref, lane), (lats_ref, jnp.where(slot < SIDE, slot - SIDE, cols + slot - SIDE))):
        for k, x in enumerate(table(place_in)):
            ref[k] = x
    spot = lax.broadcasted_iota(jnp.int32, keep_ref.shape, 0)
    counts = ((spot > 0) & (spot <= SIDE)) | ((spot >= 3 * SIDE - 1) & (spot < 4 * SIDE - 1))
    place_in = jnp.where(spot < SLOT, spot - SIDE, cols - SIDE + spot - SLOT) + flag_ref[2] * cols
    keep_ref[...] = (counts & (place_in >= 0) & (place_in < n_lat)).astype(f32)


def main_kernel(x_ref, st_ref, w1_ref, w2_ref, b1_ref, glo_ref, ghi_ref, first_ref, last_ref, st8_ref, own_ref, ps_ref,
                x32_ref, e_ref, s_ref, h_ref):
    chans, rows, cols = x_ref.shape[1:]
    nvar = st_ref.shape[0]
    half = rows // 2
    pitch = cols + SLOT
    x32_ref[...] = x_ref[0].astype(f32).reshape(chans * rows, cols)

    @pl.when(pl.program_id(0) == 0)
    def _():
        e_ref[...] = jnp.zeros_like(e_ref)
        h_ref[...] = jnp.zeros_like(h_ref)

    sides = [[], []]
    for row in range(rows):
        block = x32_ref[pl.ds(row, chans, stride=rows), :].T
        start = row * pitch + SIDE
        e_ref[start : start + cols] = block
        for k, part in enumerate((block[0:SIDE], block[cols - SIDE :])):
            sides[k].append(part)
        if row < 2:
            glo_ref[0, row] = block.astype(bf16)
        if row >= rows - 2:
            ghi_ref[0, row - (rows - 2)] = block.astype(bf16)
        shifted(e_ref, start, s_ref, row, cols)
    first_ref[0] = jnp.concatenate(sides[0], axis=0).astype(bf16)
    last_ref[0] = jnp.concatenate(sides[1], axis=0).astype(bf16)
    place_in = lax.broadcasted_iota(jnp.int32, (cols, 2 * chans), 0)
    within = (place_in > 0) & (place_in < cols - 1)
    for m in range(half - 1):
        lhs = jnp.concatenate([s_ref[2 * m + r] for r in range(4)], axis=1)
        acc = jnp.dot(lhs, w1_ref[...], preferred_element_type=f32) + b1_ref[...]
        hid = jnp.where(within, silu(acc), 0.0).astype(bf16)
        for k in range(2):
            h_ref[2 * m + 2 + k] = hid[:, k * chans : (k + 1) * chans]
    for m in range(half):
        q = nt(w2_ref[...], jnp.concatenate([h_ref[2 * m + r] for r in range(4)], axis=1))
        for k in range(2):
            ps_ref[0, 2 * m + k] = join_taps(q[k * 3 * SLOT : (k + 1) * 3 * SLOT])
    for n in range(nvar):
        x32_ref[pl.ds(n, rows, stride=VG), :] = st_ref[n, 0]
    lane = lanes((VG, WIDE))
    own = [jnp.zeros((VG, WIDE), f32)] * 2
    for row in range(rows):
        block = x32_ref[row * VG : (row + 1) * VG]
        block = jnp.where(lax.broadcasted_iota(jnp.int32, (VG, WIDE), 0) < nvar, block, 0.0)
        st8_ref[0, row] = block
        par, base = place(row, rows)
        own[par] = jnp.where(lane // SLOT == base // SLOT, roll(block, base + SIDE), own[par])
    own_ref[0, 0], own_ref[0, 1] = own


def pack_kernel(flag_ref, a_ref, b_ref, first_ref, last_ref, own_ref, row_ref, halo_ref, own4_ref, outa_ref, outb_ref):
    cols = a_ref.shape[2]
    ch = row_ref.shape[3]
    even = flag_ref[0] == 0
    lat_even = flag_ref[1] == 0
    got_a, got_b = a_ref[0].astype(f32), b_ref[0].astype(f32)
    low, high = jnp.where(even, got_b, got_a), jnp.where(even, got_a, got_b)
    size = REACH * VG
    states = [x[ch : ch + size] + x[ch + size : ch + 2 * size] for x in (low, high)]
    low, high = low[0:ch].T, high[0:ch].T
    row_ref[0, 0] = low.astype(bf16)
    row_ref[0, 1] = high.astype(bf16)
    rows = first_ref.shape[1] // SIDE
    lane = lanes((VG, WIDE))
    own = [jnp.zeros((VG, WIDE), f32)] * 2
    for k in range(2 * REACH):
        row = k - REACH if k < REACH else rows + k - REACH
        block = states[k // REACH][(k % REACH) * VG : (k % REACH + 1) * VG]
        halo_ref[0, k] = block
        at, base = place(row, rows)
        own[at - 2] = jnp.where(lane // SLOT == base // SLOT, roll(block, base + SIDE), own[at - 2])
    own = [own_ref[0, 0], own_ref[0, 1]] + own
    terms = []
    for k in range(4):
        own4_ref[0, k] = own[k]
        terms += two_terms(own[k])
    first = [low[0:SIDE].astype(bf16), first_ref[0], high[0:SIDE].astype(bf16)]
    last = [low[cols - SIDE :].astype(bf16), last_ref[0], high[cols - SIDE :].astype(bf16)]
    first, last = jnp.concatenate(first, axis=0), jnp.concatenate(last, axis=0)
    count = first.shape[0]
    for out, pick in ((outa_ref, jnp.where(lat_even, last, first)), (outb_ref, jnp.where(lat_even, first, last))):
        out[0, 0:count] = pick
        out[0, count:] = jnp.concatenate(terms, axis=0)


def edge_kernel(row_ref, g0_ref, g1_ref, w1_ref, w2_ref, b1_ref, ps0_ref, ps1_ref, pe_ref, e_ref, s_ref, h_ref):
    levels = row_ref.shape[0]
    cols, ch = row_ref.shape[2:]
    pitch = cols + SLOT
    e_ref[...] = jnp.zeros_like(e_ref)
    for lv in range(levels):
        for k in range(2):
            part = [g0_ref[lv, 0], g0_ref[lv, 1]] if k == 0 else [g1_ref[lv, 0], g1_ref[lv, 1]]
            part = [row_ref[lv, 0]] + part if k == 0 else part + [row_ref[lv, 1]]
            for r in range(3):
                start = (6 * lv + 3 * k + r) * pitch + SIDE
                e_ref[start : start + cols] = part[r].astype(f32)
                shifted(e_ref, start, s_ref, 2 * lv + k, cols, 3 * ch * r)
    acc = jnp.dot(s_ref[...].reshape(2 * levels * cols, 9 * ch), w1_ref[...], preferred_element_type=f32) + b1_ref[...]
    place_in = lax.broadcasted_iota(jnp.int32, (cols, ch), 0)
    within = (place_in > 0) & (place_in < cols - 1)
    hid = silu(acc)
    for n in range(2 * levels):
        here = slice(n * cols, (n + 1) * cols)
        h_ref[here] = jnp.where(within, hid[here], 0.0).astype(bf16)
    q = nt(w2_ref[...], h_ref[...])
    for lv in range(levels):
        for k in range(2):
            here = slice((2 * lv + k) * cols, (2 * lv + k + 1) * cols)
            for a in range(3):
                x = join_taps(q[a * 3 * SLOT : (a + 1) * 3 * SLOT, here])
                if k == 0 and a < 2:
                    x = x + ps0_ref[lv, 1 - a]
                if k == 1 and a > 0:
                    x = x + ps1_ref[lv, 4 - a]
                pe_ref[lv, 3 * k + 2 - a] = x


def side_kernel(flag_ref, first_ref, last_ref, row_ref, la_ref, lb_ref, own_ref, w1_ref, w2_ref, w2e_ref, b1_ref, keep_ref,
                pe_ref, ps0_ref, ps1_ref, sst_ref, pm_ref, cm_ref, pec_ref, outa_ref, outb_ref, e_ref, s_ref, hs_ref, z_ref):
    levels = row_ref.shape[0]
    cols, ch = row_ref.shape[2:]
    rows = first_ref.shape[1] // SIDE
    half = rows // 2
    even = flag_ref[0] == 0
    lat_even = flag_ref[1] == 0
    wide = 2 * SLOT
    total = (rows + 2) * wide
    lane = lanes((2 * VG, WIDE))
    begin, end = lane < SLOT, lane >= WIDE - SLOT
    e_ref[...] = jnp.zeros_like(e_ref)
    hs_ref[...] = jnp.zeros_like(hs_ref)
    z_ref[...] = jnp.zeros_like(z_ref)
    for lv in range(levels):
        a, b = la_ref[lv], lb_ref[lv]
        right, left = jnp.where(lat_even, a, b), jnp.where(lat_even, b, a)
        count = (rows + 2) * SIDE
        for k in range(4):
            st = []
            for x in (left, right):
                x = x[count + 2 * k * VG : count + (2 * k + 2) * VG].astype(f32)
                st.append(x[0:VG] + x[VG:])
            sst_ref[lv, k] = mix(st[0], st[1])
        right, left = right[0:count].astype(f32), left[0:count].astype(f32)
        first, last = first_ref[lv].astype(f32), last_ref[lv].astype(f32)
        low, high = row_ref[lv, 0].astype(f32), row_ref[lv, 1].astype(f32)
        for row in range(-1, rows + 1):
            side = slice((row + 1) * SIDE, (row + 2) * SIDE)
            if 0 <= row < rows:
                own = slice(row * SIDE, (row + 1) * SIDE)
                mine = first[own], last[own]
            else:
                x = low if row < 0 else high
                mine = x[0:SIDE], x[cols - SIDE :]
            start = SIDE + (row + 1) * wide
            for k, part in enumerate((left[side], mine[0], mine[1], right[side])):
                e_ref[lv, start + k * SIDE : start + (k + 1) * SIDE] = part
        for b in range(3):
            s_ref[:, b * ch : (b + 1) * ch] = e_ref[lv, pl.ds(SIDE - 1 + b, total), :].astype(bf16)
        s = s_ref[...].reshape(half + 1, 2, wide, 3 * ch)
        part = [s[0:half, 0], s[0:half, 1], s[1:, 0], s[1:, 1]]
        lhs = jnp.concatenate([p.reshape(half * wide, 3 * ch) for p in part], axis=1)
        acc = jnp.dot(lhs, w1_ref[...], preferred_element_type=f32) + b1_ref[...]
        hid = silu(acc).reshape(half, wide, 2 * ch) * keep_ref[...]
        for m in range(half):
            for side in range(2):
                here = hid[m, side * SLOT : (side + 1) * SLOT].astype(bf16)
                hs_ref[lv, side, 0, m * SLOT : (m + 1) * SLOT] = here[:, 0:ch]
                hs_ref[lv, side, 1, (m + 1) * SLOT : (m + 2) * SLOT] = here[:, ch:]
                if m == 0:
                    z_ref[lv, side * SLOT : (side + 1) * SLOT] = here[:, 0:ch]
                if m == half - 1:
                    z_ref[lv, (2 + side) * SLOT : (3 + side) * SLOT] = here[:, ch:]
        tiles = []
        for side in range(2):
            odd, ev = hs_ref.at[lv, side, 1], hs_ref.at[lv, side, 0]
            size = half * SLOT
            rhs = [odd[0:size], ev[0:size], odd[SLOT : size + SLOT], ev[SLOT : size + SLOT]]
            q = nt(w2_ref[...], jnp.concatenate(rhs, axis=1))
            tiles.append([join_taps(q[k * 3 * SLOT : (k + 1) * 3 * SLOT]) for k in range(2)])
        q = nt(w2e_ref[...], z_ref[lv])
        prev = join_taps(q[3 * SLOT : 6 * SLOT])
        nxt = join_taps(q[0 : 3 * SLOT])
        out, inn = {}, {}
        for k in range(2):
            out[k] = mix(tiles[0][k], tiles[1][k])
            inn[k] = mix(tiles[1][k], tiles[0][k])
        for k, x, s0 in ((3, prev, 0), (2, nxt, 2)):
            spot = end if k == 3 else begin
            to = WIDE - SLOT if k == 3 else 0
            at_l, at_r = roll(x, to - s0 * SLOT), roll(x, to - (s0 + 1) * SLOT)
            out[k] = jnp.where(spot, mix(at_l, at_r), 0.0)
            inn[k] = jnp.where(spot, mix(at_r, at_l), 0.0)
        for k in range(4):
            pm_ref[lv, k] = out[k]
            cm_ref[lv, k] = inn[k]
        mains = {}
        for k, row in enumerate((-1, 0, 1, rows - 2, rows - 1, rows)):
            mains[row] = pe_ref[lv, k]
        mains[2], mains[3] = ps0_ref[lv, 2], ps0_ref[lv, 3]
        mains[rows - 4], mains[rows - 3] = ps1_ref[lv, 0], ps1_ref[lv, 1]
        for row in mains:
            k, base = place(row, rows)
            mains[row] = add_columns(mains[row], inn[k], base)
        for k, row in enumerate((-1, 0, 1, rows - 2, rows - 1, rows)):
            pec_ref[lv, k] = mains[row]
        side_lo = jnp.where(lane < 2 * SLOT, out[0], jnp.where(lane < 4 * SLOT, roll(out[1], 2 * SLOT), out[3]))
        side_hi = jnp.where(lane >= WIDE - 2 * SLOT, out[0],
                            jnp.where(lane >= WIDE - 4 * SLOT, roll(out[1], -2 * SLOT), out[2]))
        out_lo = jnp.concatenate([mains[-1], mains[0], mains[1], mains[2], side_lo, mains[3]], axis=0)
        out_hi = jnp.concatenate([mains[rows - k] for k in range(4)] + [side_hi, mains[rows - 4]], axis=0)
        outa_ref[lv] = jnp.where(even, out_hi, out_lo).astype(bf16)
        outb_ref[lv] = jnp.where(even, out_lo, out_hi).astype(bf16)


def advect_kernel(flag_ref, ps_ref, pe_ref, pm_ref, cm_ref, a_ref, b_ref, st8_ref, halo_ref, sst_ref,
                  b2_ref, lat_ref, lats_ref, *rest):
    vel_ref, ten_ref, out_ref = rest[-3:]
    rows = st8_ref.shape[1]
    nvar = ten_ref.shape[0]
    even = flag_ref[0] == 0
    lane16 = lanes((2 * VG, WIDE))
    lane = lanes((VG, WIDE))
    pair = 2 * VG

    def halos(xa, xb):
        return jnp.where(even, xb, xa), jnp.where(even, xa, xb)

    lo, hi = halos(a_ref[0].astype(f32), b_ref[0].astype(f32))
    main = {}
    for row in range(2, rows - 2):
        k, base = place(row, rows)
        main[row] = add_columns(ps_ref[0, row], cm_ref[0, k], base)
    for k, row in enumerate((-1, 0, 1, rows - 2, rows - 1, rows)):
        main[row] = pe_ref[0, k]
    for k in range(REACH + 1):
        there = slice(k * pair, (k + 1) * pair) if k < REACH else slice((k + 1) * pair, (k + 2) * pair)
        for got, row in ((lo, -k), (hi, rows - 1 + k)):
            main[row] = main[row] + got[there] if row in main else got[there]
    slo, shi = (got[REACH * pair : (REACH + 1) * pair] for got in (lo, hi))
    zero = jnp.zeros((pair, WIDE), f32)
    last, front = lane16 >= WIDE - 2 * SLOT, lane16 < 2 * SLOT
    side = {
        0: pm_ref[0, 0] + jnp.where(lane16 < SLOT, slo, zero),
        1: pm_ref[0, 1] + jnp.where(lane16 >= WIDE - SLOT, shi, zero),
        2: pm_ref[0, 2] + jnp.where(last, slo, jnp.where(front, shi, zero)),
        3: pm_ref[0, 3] + jnp.where(last, roll(slo, 2 * SLOT), jnp.where(front, roll(shi, -2 * SLOT), zero)),
    }
    bias = b2_ref[...]
    main = {r: speed_cap * jnp.tanh(x + bias) for r, x in main.items()}
    side = {k: speed_cap * jnp.tanh(x + bias) * lats_ref[2, 0:1] for k, x in side.items()}
    for part in range(2):
        for row in range(rows):
            out_ref[part, row * VG : (row + 1) * VG] = main[row][part * VG : (part + 1) * VG]
        for n in range(nvar):
            vel_ref[2 * n + part, 0] = out_ref[part, pl.ds(n, rows, stride=VG), :]

    q0 = {row: st8_ref[0, row] for row in range(rows)}
    for k in range(REACH):
        q0[k - REACH] = halo_ref[0, k]
        q0[rows + k] = halo_ref[0, REACH + k]
    s0 = {k: sst_ref[0, k] for k in range(4)}

    def at(row):
        return place(row, rows)

    def side_rows(s):
        def turned(own, halo, by, first):
            own, halo = roll(own, by), roll(halo, by)
            return jnp.where(first, halo, own), jnp.where(first, own, halo)

        odd_back = turned(s[1], s[3], SLOT, lane < SLOT)
        even_on = turned(s[0], s[2], -SLOT, lane >= WIDE - SLOT)
        before = {0: odd_back[0], 2: odd_back[1], 1: s[0], 3: s[2]}
        after = {0: s[1], 2: s[3], 1: even_on[0], 3: even_on[1]}
        return before, after

    u = {r: x[0:VG] for r, x in main.items()}
    us = {k: x[0:VG] for k, x in side.items()}
    inside = range(1 - REACH, rows + REACH - 1)
    v = {r: main[r][VG:] for r in inside}
    vs = {k: x[VG:] for k, x in side.items()}
    cosine, metric = lat_ref[0], lat_ref[1]
    cosine_s, metric_s = lats_ref[0], lats_ref[1]
    flux = {r: x * cosine for r, x in v.items()}
    flux_s = {k: x * cosine_s for k, x in vs.items()}
    fb, fbs = col_before(flux, flux_s, at)
    fa, fas = col_after(flux, flux_s, at)
    ub, ua = side_rows(us)

    def coefs(m, uu, vv, udiff, vdiff):
        div = m * (udiff * 0.5 + vdiff * 0.5)
        cl = m * jnp.maximum(uu, 0.0)
        cr = -(m * jnp.minimum(uu, 0.0))
        cd = jnp.maximum(vv, 0.0)
        cu = -jnp.minimum(vv, 0.0)
        return -(cl + cr + cd + cu + div), cl, cr, cd, cu

    cm = {r: coefs(metric, u[r], v[r], u[r + 1] - u[r - 1], fa[r] - fb[r]) for r in inside}
    cs = {k: coefs(metric_s, us[k], vs[k], ua[k] - ub[k], fas[k] - fbs[k]) for k in range(4)}

    def stencil(c, x, left, right, down, up):
        return c[0] * x + c[1] * left + c[2] * right + c[3] * down + c[4] * up

    def rate(q, s, depth):
        centre = {r: q[r] for r in range(depth - REACH, rows + REACH - depth)}
        qb, sb = col_before(centre, s, at)
        qa, sa = col_after(centre, s, at)
        rb, ra = side_rows(s)
        out = {r: stencil(cm[r], q[r], q[r - 1], q[r + 1], qb[r], qa[r]) for r in centre}
        if depth == REACH:
            return out, None
        return out, {k: stencil(cs[k], s[k], rb[k], ra[k], sb[k], sa[k]) for k in range(4)}

    def moved(rates, by):
        return {r: q0[r] + by * x for r, x in rates[0].items()}, {k: s0[k] + by * x for k, x in rates[1].items()}

    one = rate(q0, s0, 1)
    two = rate(*moved(one, 0.5 * time_step), 2)
    three = rate(*moved(two, 0.5 * time_step), 3)
    four = rate(*moved(three, time_step), 4)
    for row in range(rows):
        ten = (one[0][row] + 2.0 * two[0][row] + 2.0 * three[0][row] + four[0][row]) / 6.0
        out_ref[0, row * VG : (row + 1) * VG] = ten
    for n in range(nvar):
        ten_ref[n, 0] = out_ref[0, pl.ds(n, rows, stride=VG), :]


def full(shape):
    return pl.BlockSpec(shape, lambda *i: (0,) * len(shape))


def per_level(shape):
    return pl.BlockSpec((1,) + shape[1:], lambda i: (i,) + (0,) * (len(shape) - 1))


def level_part(shape, index, block=1, offset=0):
    return pl.BlockSpec((block,) + shape, lambda i: (i + offset, index) + (0,) * (len(shape) - 1))


def levels_of(shape, block=1, offset=0):
    return pl.BlockSpec((block,) + shape[1:], lambda i: (i + offset,) + (0,) * (len(shape) - 1))


def var_level(shape, offset=0):
    return pl.BlockSpec((shape[0], 1) + shape[2:], lambda i: (0, i + offset, 0, 0))


def body(hidden_in, w_conv1, b_conv1, w_conv2, b_conv2, state):
    lev, ch, rows, cols = hidden_in.shape
    nvar = state.shape[0]
    ext = cols + SLOT
    half = rows // 2
    params = pltpu.CompilerParams(vmem_limit_bytes=VMEM_LIMIT)
    smem = pl.BlockSpec(memory_space=pltpu.SMEM)
    sds = jax.ShapeDtypeStruct

    def call(kernel, steps, ins, outs, out_specs, scratch, args, cost=None, aliases={}):
        return pl.pallas_call(
            kernel,
            grid=(steps,),
            in_specs=ins,
            out_specs=out_specs,
            out_shape=outs,
            scratch_shapes=scratch,
            compiler_params=params,
            cost_estimate=cost,
            input_output_aliases=aliases,
        )(*args)

    flags = jnp.stack([lax.axis_index("lon") % 2, lax.axis_index("lat") % 2, lax.axis_index("lat")]).astype(jnp.int32)
    lon_wire = (lev, ch + 2 * REACH * VG, WIDE)
    shapes = [(lon_wire, bf16), (lon_wire, bf16), ((12 * ch, 2 * ch), bf16), ((6 * SLOT, 4 * ch), bf16), ((9 * SLOT, ch), bf16),
              ((6 * SLOT, ch), bf16), ((1, 2 * ch), f32), ((2 * VG, WIDE), f32), ((3, VG, WIDE), f32), ((3, VG, WIDE), f32),
              ((2 * SLOT, 2 * ch), f32)]
    vmem = pl.BlockSpec(memory_space=pltpu.VMEM)
    w1_one = w_conv1.reshape(9 * ch, ch)
    b1 = b_conv1.reshape(1, ch)
    n_lat = cols * lax.axis_size("lat")
    lon_a, lon_b, w1_pair, w2_pair, w2_one, w2_ends, b1_pair, b2, lat_main, lat_side, keep = pl.pallas_call(
        lambda flag_ref, *refs: prep_kernel(flag_ref, n_lat, *refs),
        in_specs=[smem, smem] + [vmem] * 5,
        out_specs=[vmem] * len(shapes),
        out_shape=[sds(*x) for x in shapes],
        scratch_shapes=[pltpu.VMEM((ch * rows, cols), f32), pltpu.VMEM((4 * VG, ch), f32)],
        compiler_params=params,
    )(flags, b_conv2, hidden_in, state, w1_one, w_conv2.transpose(0, 1, 3, 2).reshape(9, 2 * nvar, ch), b1)
    lon_a = swap(lon_a, "lon", 0, True)
    lon_b = swap(lon_b, "lon", 1, True)

    hbm = pl.BlockSpec(memory_space=pltpu.HBM)
    g_pair = (lev, 2, cols, ch)
    st8_shape = (lev, rows, VG, WIDE)
    cut = (lev, rows * SIDE, ch)
    ps_shape = (lev, rows, 2 * VG, WIDE)
    own_shape = (lev, 2, VG, WIDE)
    shapes = [(g_pair, bf16), (g_pair, bf16), (cut, bf16), (cut, bf16), (st8_shape, f32), (own_shape, f32), (ps_shape, f32)]
    g_lo, g_hi, first, last, st8, own, ps = call(
        main_kernel,
        lev,
        [per_level(hidden_in.shape), var_level(state.shape), full(w1_pair.shape), full(w2_pair.shape), full((1, 2 * ch))],
        [sds(*x) for x in shapes],
        [per_level(x[0]) for x in shapes],
        [
            pltpu.VMEM((ch * rows, cols), f32),
            pltpu.VMEM((rows * (cols + SLOT), ch), f32),
            pltpu.VMEM((rows, cols, 3 * ch), bf16),
            pltpu.VMEM((rows + 2, cols, ch), bf16),
        ],
        (hidden_in, state, w1_pair, w2_pair, b1_pair),
        pl.CostEstimate(flops=2 * lev * rows * ext * 9 * ch * ch, bytes_accessed=8 * 2**20, transcendentals=0),
    )

    lat_wire = (lev, (rows + 2) * SIDE + 8 * VG, WIDE)
    pair_shape = (lev, 2, cols, ch)
    halo_shape = (lev, 2 * REACH, VG, WIDE)
    own4_shape = (lev, 4, VG, WIDE)
    shapes = [(pair_shape, bf16), (halo_shape, f32), (own4_shape, f32), (lat_wire, bf16), (lat_wire, bf16)]
    row_pair, halo, own4, lat_a, lat_b = call(
        pack_kernel,
        lev,
        [smem, per_level(lon_wire), per_level(lon_wire), per_level(cut), per_level(cut), per_level(own_shape)],
        [sds(*x) for x in shapes],
        [per_level(x[0]) for x in shapes],
        [],
        (flags, lon_a, lon_b, first, last, own),
    )
    lat_a = swap(lat_a, "lat", 0, False)
    lat_b = swap(lat_b, "lat", 1, False)

    block = EDGE_LEVELS
    four = (4, 2 * VG, WIDE)
    pe_shape = (lev, 6, 2 * VG, WIDE)
    here = functools.partial(levels_of, block=block)
    (pe,) = call(
        edge_kernel,
        lev // block,
        [here(pair_shape), here(g_pair), here(g_pair), full(w1_one.shape), full(w2_one.shape), full((1, ch)),
         level_part(four, 0, block), level_part(four, rows // 4 - 1, block)],
        [sds(pe_shape, f32)],
        [here(pe_shape)],
        [
            pltpu.VMEM((6 * block * (cols + SLOT), ch), f32),
            pltpu.VMEM((2 * block, cols, 9 * ch), bf16),
            pltpu.VMEM((2 * block * cols, ch), bf16),
        ],
        (row_pair, g_lo, g_hi, w1_one, w2_one, b1, ps, ps),
        pl.CostEstimate(flops=lev * 2 * 2 * ext * 9 * ch * ch, bytes_accessed=4 * 2**20, transcendentals=0),
    )

    block = SIDE_LEVELS
    parts = PARTS
    count = lev // parts
    wire = (count, 2 * VG * (REACH + 2), WIDE)
    pec_shape = (count,) + pe_shape[1:]
    pm4_shape = (count, 4, 2 * VG, WIDE)
    sst_shape = (count, 4, VG, WIDE)
    shapes = [(sst_shape, f32), (pm4_shape, f32), (pm4_shape, f32), (pec_shape, f32), (wire, bf16), (wire, bf16)]
    sent = []
    for part in range(parts):
        off = part * count // block
        here = functools.partial(levels_of, block=block, offset=off)
        sst, pm, cm, pec, out_a, out_b = call(
            side_kernel,
            count // block,
            [smem, here(cut), here(cut), here(pair_shape), here(lat_wire), here(lat_wire), here(own4_shape),
             full(w1_pair.shape), full(w2_pair.shape), full(w2_ends.shape), full((1, 2 * ch)), full((2 * SLOT, 2 * ch)),
             here(pe_shape), level_part(four, 0, block, off), level_part(four, rows // 4 - 1, block, off)],
            [sds(*x) for x in shapes],
            [levels_of(x[0], block) for x in shapes],
            [
                pltpu.VMEM((block, (rows + 2) * 2 * SLOT + 2 * SIDE, ch), f32),
                pltpu.VMEM(((rows + 2) * 2 * SLOT, 3 * ch), bf16),
                pltpu.VMEM((block, 2, 2, (half + 1) * SLOT, ch), bf16),
                pltpu.VMEM((block, WIDE, ch), bf16),
            ],
            (flags, first, last, row_pair, lat_a, lat_b, own4, w1_pair, w2_pair, w2_ends, b1_pair, keep, pe, ps, ps),
            pl.CostEstimate(flops=count * 512 * 12 * ch * ch, bytes_accessed=4 * 2**20, transcendentals=0),
        )
        sent.append((pec, pm, cm, sst, swap(out_a, "lon", 0, True), swap(out_b, "lon", 1, True)))

    outs = [sds((2 * nvar, lev, rows, cols), f32), sds(state.shape, f32)]
    done = ()
    for part, (pec, pm, cm, sst, out_a, out_b) in enumerate(sent):
        off = part * count
        here = functools.partial(levels_of, offset=off)
        var = functools.partial(var_level, offset=off)
        done = call(
            advect_kernel,
            count,
            [smem, here(ps_shape), per_level(pec_shape), per_level(pm4_shape), per_level(pm4_shape), per_level(wire),
             per_level(wire), here(st8.shape), here(halo_shape), per_level(sst_shape),
             full(b2.shape), full(lat_main.shape), full(lat_side.shape)] + [hbm] * len(done),
            outs,
            [var(o.shape) for o in outs],
            [pltpu.VMEM((2, rows * VG, WIDE), f32)],
            (flags, ps, pec, pm, cm, out_a, out_b, st8, halo, sst, b2, lat_main, lat_side) + tuple(done),
            pl.CostEstimate(flops=count * 2**24, bytes_accessed=2 * 2**20, transcendentals=0),
            {13: 0, 14: 1} if done else {},
        )
    return tuple(done)


def solution(mesh):
    placed = (P(None, None, "lon", "lat"), P(), P(), P(), P(), P(None, None, "lon", "lat"))
    return jax.shard_map(
        body,
        mesh=mesh,
        in_specs=placed,
        out_specs=(P(None, None, "lon", "lat"), P(None, None, "lon", "lat")),
        check_vma=False,
    )
```

```python
import functools
import math

import jax
import jax.numpy as jnp
from jax import lax
from jax.experimental import pallas as pl
from jax.experimental.pallas import tpu as pltpu
from jax.sharding import PartitionSpec as P

time_step = 0.5
speed_cap = 0.6
cos_floor = 0.5

SIDE = 8
SLOT = 2 * SIDE
WIDE = 128
REACH = 4
VG = 8
VMEM_LIMIT = 24 * 2**20
ROWS_LIMIT = 50 * 2**20
EDGE_LEVELS = 4
SIDE_LEVELS = 4
PARTS = 2
f32 = jnp.float32
bf16 = jnp.bfloat16


def swap_pairs(count, first, closed):
    pairs = []
    for low in range(first, count, 2):
        high = low + 1
        if high >= count and not closed:
            continue
        pairs += [(low, high % count), (high % count, low)]
    return pairs


def swap(block, axis, first, closed):
    return lax.ppermute(block, axis, swap_pairs(lax.axis_size(axis), first, closed))


def place(row, rows):
    half, par = row // 2, row % 2
    own = 0 <= half < rows // 2
    return (0 if own else 2) + par, SLOT * (half % (rows // 2))


def lanes(shape):
    return lax.broadcasted_iota(jnp.int32, shape, len(shape) - 1)


def roll(x, by):
    by = by % WIDE
    return pltpu.roll(x, by, x.ndim - 1) if by else x


def col_before(mains, sides, at):
    lane = lanes(next(iter(mains.values())).shape)
    new_sides = {k: roll(s, 1) for k, s in sides.items()}
    new_mains = {}
    for row, main in mains.items():
        k, base = at(row)
        new_mains[row] = jnp.where(lane == 0, roll(sides[k], 1 - base - SIDE), roll(main, 1))
        new_sides[k] = jnp.where(lane == base + SIDE, roll(main, base + SIDE + 1), new_sides[k])
    return new_mains, new_sides


def col_after(mains, sides, at):
    lane = lanes(next(iter(mains.values())).shape)
    new_sides = {k: roll(s, -1) for k, s in sides.items()}
    new_mains = {}
    for row, main in mains.items():
        k, base = at(row)
        new_mains[row] = jnp.where(lane == WIDE - 1, roll(sides[k], WIDE - 1 - base - SIDE), roll(main, -1))
        new_sides[k] = jnp.where(lane == base + SIDE - 1, roll(main, base + SIDE - 1), new_sides[k])
    return new_mains, new_sides


def join_taps(x):
    return roll(x[0:SLOT], 1) + x[SLOT : 2 * SLOT] + roll(x[2 * SLOT : 3 * SLOT], -1)


def mix(first, second):
    return jnp.where(lanes(first.shape) % SLOT < SIDE, first, second)


def add_columns(main, side, base):
    lane = lanes(main.shape)
    return main + jnp.where((lane < SIDE) | (lane >= WIDE - SIDE), roll(side, -(base + SIDE)), 0.0)


def two_terms(x):
    first = x.astype(bf16)
    return [first, (x - first.astype(f32)).astype(bf16)]


def nt(lhs, rhs):
    return lax.dot_general(lhs, rhs, (((1,), (1,)), ((), ())), preferred_element_type=f32)


def silu(s):
    return s / (1.0 + jnp.exp(-s))


def shifted(e_ref, start, s_ref, to, count, first=0):
    ch = e_ref.shape[-1]
    for b in range(3):
        lane0 = first + b * ch
        s_ref[to, :, lane0 : lane0 + ch] = e_ref[pl.ds(start - 1 + b, count), :].astype(bf16)


def rows_kernel(flag_ref, x_hbm, st_hbm, outa_ref, outb_ref, x32_ref, x_ref, st_ref, sem):
    levels, ch, rows, cols = x_hbm.shape
    nvar = st_hbm.shape[0]
    size = nvar * REACH
    even = flag_ref[0] == 0

    def level_copy(lv):
        return pltpu.make_async_copy(x_hbm.at[lv], x_ref.at[lv], sem.at[lv])

    state_copy = pltpu.make_async_copy(st_hbm, st_ref, sem.at[levels])
    level_copy(0).start()
    state_copy.start()
    for lv in range(1, levels):
        level_copy(lv).start()
    state_copy.wait()

    def one(lv, carry):
        level_copy(lv).wait()
        x32_ref[...] = x_ref[lv].astype(f32).reshape(ch * rows, cols)
        lo, hi = (x32_ref[pl.ds(row, ch, stride=rows), :].astype(bf16) for row in (0, rows - 1))
        outa_ref[lv, 0:ch] = jnp.where(even, hi, lo)
        outb_ref[lv, 0:ch] = jnp.where(even, lo, hi)
        for n in range(nvar):
            x32_ref[n * REACH : (n + 1) * REACH] = st_ref[n, lv, 0:REACH]
            x32_ref[size + n * REACH : size + (n + 1) * REACH] = st_ref[n, lv, rows - REACH :]
        lo, hi = x32_ref[0:size], x32_ref[size : 2 * size]
        outa_ref[lv, ch:] = jnp.concatenate(two_terms(jnp.where(even, hi, lo)), axis=0)
        outb_ref[lv, ch:] = jnp.concatenate(two_terms(jnp.where(even, lo, hi)), axis=0)
        return carry

    lax.fori_loop(0, levels, one, 0)


def prep_kernel(flag_ref, n_lat, cols, b2_ref, w1_ref, w2_ref, b1_ref,
                w1p_ref, w2p_ref, w2o_ref, w2e_ref, b1p_ref, b2o_ref, lat_ref, lats_ref, keep_ref, w2s_ref):
    size, ch = w1_ref.shape
    nvar = w2_ref.shape[1] // 2
    w1p_ref[0:size, 0:ch] = w1_ref[...]
    w1p_ref[size:, 0:ch] = jnp.zeros((3 * ch, ch), bf16)
    w1p_ref[0 : 3 * ch, ch:] = jnp.zeros((3 * ch, ch), bf16)
    w1p_ref[3 * ch :, ch:] = w1_ref[...]
    b1p_ref[:, 0:ch] = b1_ref[...]
    b1p_ref[:, ch:] = b1_ref[...]
    w2p_ref[...] = jnp.zeros_like(w2p_ref)
    w2s_ref[0 : 2 * VG] = jnp.zeros((2 * VG, ch), f32)
    for a in range(3):
        for b in range(3):
            w2s_ref[2 * VG : 2 * VG + 2 * nvar] = w2_ref[3 * a + b].astype(f32)
            for part in range(2):
                w2s_ref[part * VG : part * VG + nvar] = w2s_ref[pl.ds(2 * VG + part, nvar, stride=2), :]
            here = w2s_ref[0 : 2 * VG].astype(bf16)
            at = 3 * a + b
            w2o_ref[at * SLOT : (at + 1) * SLOT] = here
            for k in range(2):
                first = (3 * k + b) * SLOT
                w2p_ref[first : first + SLOT, (a + k) * ch : (a + k + 1) * ch] = here
            if a != 1:
                first = (3 * (a // 2) + b) * SLOT
                w2e_ref[first : first + SLOT] = here
    b2o_ref[...] = jnp.zeros_like(b2o_ref)
    for v in range(2 * nvar):
        row = (v % 2) * VG + v // 2
        b2o_ref[row : row + 1] = jnp.full((1, WIDE), b2_ref[v], f32)

    def table(place_in):
        place_in = place_in + flag_ref[2] * cols
        keep = ((place_in >= 0) & (place_in < n_lat)).astype(f32)
        phi = (place_in.astype(f32) + 0.5) * (math.pi / n_lat) - 0.5 * math.pi
        cosine = jnp.maximum(jnp.cos(phi), cos_floor)
        return cosine, 1.0 / cosine, keep

    lane = lanes((VG, WIDE))
    slot = lane % SLOT
    beyond = jnp.where(slot < SIDE, slot - SIDE, cols + slot - SIDE)
    ends = jnp.where(slot < SIDE, cols - SIDE + slot, slot - SIDE)
    for ref, first, place_in in ((lat_ref, 0, lane), (lats_ref, 0, beyond), (lats_ref, 3, ends)):
        for k, x in enumerate(table(place_in)):
            ref[first + k] = x
    spot = lax.broadcasted_iota(jnp.int32, keep_ref.shape, 0)
    counts = ((spot > 0) & (spot <= SIDE)) | ((spot >= 3 * SIDE - 1) & (spot < 4 * SIDE - 1))
    place_in = jnp.where(spot < SLOT, spot - SIDE, cols - SIDE + spot - SLOT) + flag_ref[2] * cols
    keep_ref[...] = (counts & (place_in >= 0) & (place_in < n_lat)).astype(f32)


def main_kernel(x_ref, st_ref, w1_ref, w2_ref, b1_ref, glo_ref, ghi_ref, first_ref, last_ref, st8_ref, own_ref, ps_ref,
                x32_ref, e_ref, s_ref, h_ref):
    chans, rows, cols = x_ref.shape[1:]
    nvar = st_ref.shape[0]
    half = rows // 2
    pitch = cols + SLOT
    step = rows + VG
    x32_ref.reshape(chans, step, cols)[:, 0:rows] = x_ref[0].astype(f32)

    @pl.when(pl.program_id(0) == 0)
    def _():
        e_ref[...] = jnp.zeros_like(e_ref)
        h_ref[...] = jnp.zeros_like(h_ref)

    sides = [[], []]
    for row in range(rows):
        block = x32_ref[pl.ds(row, chans, stride=step), :].T
        start = row * pitch + SIDE
        e_ref[start : start + cols] = block
        for k, part in enumerate((block[0:SIDE], block[cols - SIDE :])):
            sides[k].append(part)
        if row < 2:
            glo_ref[0, row] = block.astype(bf16)
        if row >= rows - 2:
            ghi_ref[0, row - (rows - 2)] = block.astype(bf16)
        shifted(e_ref, start, s_ref, row, cols)
    first_ref[0] = jnp.concatenate(sides[0], axis=0).astype(bf16)
    last_ref[0] = jnp.concatenate(sides[1], axis=0).astype(bf16)
    place_in = lax.broadcasted_iota(jnp.int32, (cols, 2 * chans), 0)
    within = (place_in > 0) & (place_in < cols - 1)
    for m in range(half - 1):
        lhs = jnp.concatenate([s_ref[2 * m + r] for r in range(4)], axis=1)
        acc = jnp.dot(lhs, w1_ref[...], preferred_element_type=f32) + b1_ref[...]
        hid = jnp.where(within, silu(acc), 0.0).astype(bf16)
        for k in range(2):
            h_ref[2 * m + 2 + k] = hid[:, k * chans : (k + 1) * chans]
    for m in range(half):
        q = nt(w2_ref[...], jnp.concatenate([h_ref[2 * m + r] for r in range(4)], axis=1))
        for k in range(2):
            ps_ref[0, 2 * m + k] = join_taps(q[k * 3 * SLOT : (k + 1) * 3 * SLOT])
    for n in range(nvar):
        x32_ref[pl.ds(n, rows, stride=VG), :] = st_ref[n, 0]
    lane = lanes((VG, WIDE))
    own = [jnp.zeros((VG, WIDE), f32)] * 2
    for row in range(rows):
        block = x32_ref[row * VG : (row + 1) * VG]
        block = jnp.where(lax.broadcasted_iota(jnp.int32, (VG, WIDE), 0) < nvar, block, 0.0)
        st8_ref[0, row] = block
        par, base = place(row, rows)
        own[par] = jnp.where(lane // SLOT == base // SLOT, roll(block, base + SIDE), own[par])
    own_ref[0, 0], own_ref[0, 1] = own


def pack_kernel(flag_ref, a_ref, b_ref, first_ref, last_ref, own_ref, row_ref, halo_ref, outa_ref, outb_ref, x_ref):
    cols = a_ref.shape[2]
    ch = row_ref.shape[3]
    size = (a_ref.shape[1] - ch) // 2
    nvar = size // REACH
    even = flag_ref[0] == 0
    lat_even = flag_ref[1] == 0
    got_a, got_b = a_ref[0].astype(f32), b_ref[0].astype(f32)
    low, high = jnp.where(even, got_b, got_a), jnp.where(even, got_a, got_b)
    halo_ref[...] = jnp.zeros_like(halo_ref)
    for k, x in enumerate((low, high)):
        x_ref[...] = x[ch : ch + size] + x[ch + size :]
        for r in range(REACH):
            halo_ref[0, k * REACH + r, 0:nvar] = x_ref[pl.ds(r, nvar, stride=REACH), :]
    low, high = low[0:ch].T, high[0:ch].T
    row_ref[0, 0] = low.astype(bf16)
    row_ref[0, 1] = high.astype(bf16)
    terms = two_terms(own_ref[0, 0]) + two_terms(own_ref[0, 1])
    first = [low[0:SIDE].astype(bf16), first_ref[0], high[0:SIDE].astype(bf16)]
    last = [low[cols - SIDE :].astype(bf16), last_ref[0], high[cols - SIDE :].astype(bf16)]
    first, last = jnp.concatenate(first, axis=0), jnp.concatenate(last, axis=0)
    count = first.shape[0]
    for out, pick in ((outa_ref, jnp.where(lat_even, last, first)), (outb_ref, jnp.where(lat_even, first, last))):
        out[0, 0:count] = pick
        out[0, count:] = jnp.concatenate(terms, axis=0)


def edge_kernel(row_ref, g0_ref, g1_ref, w1_ref, w2_ref, b1_ref, ps0_ref, ps1_ref, pe_ref, e_ref, s_ref, h_ref):
    levels = row_ref.shape[0]
    cols, ch = row_ref.shape[2:]
    pitch = cols + SLOT
    e_ref[...] = jnp.zeros_like(e_ref)
    for lv in range(levels):
        for k in range(2):
            part = [g0_ref[lv, 0], g0_ref[lv, 1]] if k == 0 else [g1_ref[lv, 0], g1_ref[lv, 1]]
            part = [row_ref[lv, 0]] + part if k == 0 else part + [row_ref[lv, 1]]
            for r in range(3):
                start = (6 * lv + 3 * k + r) * pitch + SIDE
                e_ref[start : start + cols] = part[r].astype(f32)
                shifted(e_ref, start, s_ref, 2 * lv + k, cols, 3 * ch * r)
    acc = jnp.dot(s_ref[...].reshape(2 * levels * cols, 9 * ch), w1_ref[...], preferred_element_type=f32) + b1_ref[...]
    place_in = lax.broadcasted_iota(jnp.int32, (cols, ch), 0)
    within = (place_in > 0) & (place_in < cols - 1)
    hid = silu(acc)
    for n in range(2 * levels):
        here = slice(n * cols, (n + 1) * cols)
        h_ref[here] = jnp.where(within, hid[here], 0.0).astype(bf16)
    q = nt(w2_ref[...], h_ref[...])
    for lv in range(levels):
        for k in range(2):
            here = slice((2 * lv + k) * cols, (2 * lv + k + 1) * cols)
            for a in range(3):
                x = join_taps(q[a * 3 * SLOT : (a + 1) * 3 * SLOT, here])
                if k == 0 and a < 2:
                    x = x + ps0_ref[lv, 1 - a]
                if k == 1 and a > 0:
                    x = x + ps1_ref[lv, 4 - a]
                pe_ref[lv, 3 * k + 2 - a] = x


def side_kernel(flag_ref, first_ref, last_ref, row_ref, la_ref, lb_ref, w1_ref, w2_ref, w2e_ref, b1_ref, keep_ref,
                pe_ref, ps0_ref, ps1_ref, sst_ref, pm_ref, cm_ref, pec_ref, outa_ref, outb_ref, e_ref, s_ref, hs_ref, z_ref):
    levels = row_ref.shape[0]
    cols, ch = row_ref.shape[2:]
    rows = first_ref.shape[1] // SIDE
    half = rows // 2
    even = flag_ref[0] == 0
    lat_even = flag_ref[1] == 0
    wide = 2 * SLOT
    total = (rows + 2) * wide
    lane = lanes((2 * VG, WIDE))
    begin, end = lane < SLOT, lane >= WIDE - SLOT
    e_ref[...] = jnp.zeros_like(e_ref)
    hs_ref[...] = jnp.zeros_like(hs_ref)
    z_ref[...] = jnp.zeros_like(z_ref)
    for lv in range(levels):
        a, b = la_ref[lv], lb_ref[lv]
        right, left = jnp.where(lat_even, a, b), jnp.where(lat_even, b, a)
        count = (rows + 2) * SIDE
        for k in range(2):
            st = []
            for x in (left, right):
                x = x[count + 2 * k * VG : count + (2 * k + 2) * VG].astype(f32)
                st.append(x[0:VG] + x[VG:])
            sst_ref[lv, k] = mix(st[0], st[1])
        right, left = right[0:count].astype(f32), left[0:count].astype(f32)
        first, last = first_ref[lv].astype(f32), last_ref[lv].astype(f32)
        low, high = row_ref[lv, 0].astype(f32), row_ref[lv, 1].astype(f32)
        for row in range(-1, rows + 1):
            side = slice((row + 1) * SIDE, (row + 2) * SIDE)
            if 0 <= row < rows:
                own = slice(row * SIDE, (row + 1) * SIDE)
                mine = first[own], last[own]
            else:
                x = low if row < 0 else high
                mine = x[0:SIDE], x[cols - SIDE :]
            start = SIDE + (row + 1) * wide
            for k, part in enumerate((left[side], mine[0], mine[1], right[side])):
                e_ref[lv, start + k * SIDE : start + (k + 1) * SIDE] = part
        for b in range(3):
            s_ref[lv, :, b * ch : (b + 1) * ch] = e_ref[lv, pl.ds(SIDE - 1 + b, total), :].astype(bf16)
    s = s_ref[...].reshape(levels, half + 1, 2, wide, 3 * ch)
    part = [s[:, 0:half, 0], s[:, 0:half, 1], s[:, 1:, 0], s[:, 1:, 1]]
    lhs = jnp.concatenate([p.reshape(levels * half * wide, 3 * ch) for p in part], axis=1)
    acc = jnp.dot(lhs, w1_ref[...], preferred_element_type=f32) + b1_ref[...]
    hid = silu(acc).reshape(levels, half, wide, 2 * ch) * keep_ref[...]
    for lv in range(levels):
        for m in range(half):
            for side in range(2):
                here = hid[lv, m, side * SLOT : (side + 1) * SLOT].astype(bf16)
                hs_ref[lv, side, 0, m * SLOT : (m + 1) * SLOT] = here[:, 0:ch]
                hs_ref[lv, side, 1, (m + 1) * SLOT : (m + 2) * SLOT] = here[:, ch:]
                at = (4 * lv + side) * SLOT
                if m == 0:
                    z_ref[at : at + SLOT] = here[:, 0:ch]
                if m == half - 1:
                    z_ref[at + 2 * SLOT : at + 3 * SLOT] = here[:, ch:]
    size = half * SLOT
    rhs = []
    for lv in range(levels):
        for side in range(2):
            odd, ev = hs_ref.at[lv, side, 1], hs_ref.at[lv, side, 0]
            rhs.append(jnp.concatenate([odd[0:size], ev[0:size], odd[SLOT : size + SLOT], ev[SLOT : size + SLOT]], axis=1))
    q_side = nt(w2_ref[...], jnp.concatenate(rhs, axis=0))
    q_ends = nt(w2e_ref[...], z_ref[...])
    for lv in range(levels):
        tiles = []
        for side in range(2):
            q = q_side[:, (2 * lv + side) * size : (2 * lv + side + 1) * size]
            tiles.append([join_taps(q[k * 3 * SLOT : (k + 1) * 3 * SLOT]) for k in range(2)])
        per = WIDE // (4 * SLOT)
        q = roll(q_ends[:, (lv // per) * WIDE : (lv // per + 1) * WIDE], -(lv % per) * 4 * SLOT)
        prev = join_taps(q[3 * SLOT : 6 * SLOT])
        nxt = join_taps(q[0 : 3 * SLOT])
        out, inn = {}, {}
        for k in range(2):
            out[k] = mix(tiles[0][k], tiles[1][k])
            inn[k] = mix(tiles[1][k], tiles[0][k])
        for k, x, s0 in ((3, prev, 0), (2, nxt, 2)):
            spot = end if k == 3 else begin
            to = WIDE - SLOT if k == 3 else 0
            at_l, at_r = roll(x, to - s0 * SLOT), roll(x, to - (s0 + 1) * SLOT)
            out[k] = jnp.where(spot, mix(at_l, at_r), 0.0)
            inn[k] = jnp.where(spot, mix(at_r, at_l), 0.0)
        for k in range(4):
            pm_ref[lv, k] = out[k]
            cm_ref[lv, k] = inn[k]
        mains = {}
        for k, row in enumerate((-1, 0, 1, rows - 2, rows - 1, rows)):
            mains[row] = pe_ref[lv, k]
        mains[2], mains[3] = ps0_ref[lv, 2], ps0_ref[lv, 3]
        mains[rows - 4], mains[rows - 3] = ps1_ref[lv, 0], ps1_ref[lv, 1]
        for row in mains:
            k, base = place(row, rows)
            mains[row] = add_columns(mains[row], inn[k], base)
        for k, row in enumerate((-1, 0, 1, rows - 2, rows - 1, rows)):
            pec_ref[lv, k] = mains[row]
        lane8 = lanes((VG, WIDE))
        st = sst_ref[lv, 0], sst_ref[lv, 1]
        st_lo = two_terms(jnp.where(lane8 < 2 * SLOT, st[0], roll(st[1], 2 * SLOT)))
        st_hi = two_terms(jnp.where(lane8 >= WIDE - 2 * SLOT, st[0], roll(st[1], -2 * SLOT)))
        side_lo = jnp.where(lane < 2 * SLOT, out[0], jnp.where(lane < 4 * SLOT, roll(out[1], 2 * SLOT), out[3]))
        side_hi = jnp.where(lane >= WIDE - 2 * SLOT, out[0],
                            jnp.where(lane >= WIDE - 4 * SLOT, roll(out[1], -2 * SLOT), out[2]))
        out_lo = jnp.concatenate([mains[-1], mains[0], mains[1], mains[2], side_lo, mains[3]], axis=0)
        out_hi = jnp.concatenate([mains[rows - k] for k in range(4)] + [side_hi, mains[rows - 4]], axis=0)
        main_rows = out_lo.shape[0]
        outa_ref[lv, 0:main_rows] = jnp.where(even, out_hi, out_lo).astype(bf16)
        outb_ref[lv, 0:main_rows] = jnp.where(even, out_lo, out_hi).astype(bf16)
        outa_ref[lv, main_rows:] = jnp.concatenate([jnp.where(even, h, l) for h, l in zip(st_hi, st_lo)], axis=0)
        outb_ref[lv, main_rows:] = jnp.concatenate([jnp.where(even, l, h) for h, l in zip(st_hi, st_lo)], axis=0)


def advect_kernel(flag_ref, ps_ref, pe_ref, pm_ref, cm_ref, a_ref, b_ref, st8_ref, halo_ref, sst_ref, own_ref,
                  b2_ref, lat_ref, lats_ref, *rest):
    vel_ref, ten_ref, out_ref = rest[-3:]
    rows = st8_ref.shape[1]
    nvar = ten_ref.shape[0]
    even = flag_ref[0] == 0
    lane16 = lanes((2 * VG, WIDE))
    lane = lanes((VG, WIDE))
    pair = 2 * VG

    def halos(xa, xb):
        return jnp.where(even, xb, xa), jnp.where(even, xa, xb)

    lo, hi = halos(a_ref[0].astype(f32), b_ref[0].astype(f32))
    main = {}
    for row in range(2, rows - 2):
        k, base = place(row, rows)
        main[row] = add_columns(ps_ref[0, row], cm_ref[0, k], base)
    for k, row in enumerate((-1, 0, 1, rows - 2, rows - 1, rows)):
        main[row] = pe_ref[0, k]
    for k in range(REACH + 1):
        there = slice(k * pair, (k + 1) * pair) if k < REACH else slice((k + 1) * pair, (k + 2) * pair)
        for got, row in ((lo, -k), (hi, rows - 1 + k)):
            main[row] = main[row] + got[there] if row in main else got[there]
    slo, shi = (got[REACH * pair : (REACH + 1) * pair] for got in (lo, hi))
    zero = jnp.zeros((pair, WIDE), f32)
    last, front = lane16 >= WIDE - 2 * SLOT, lane16 < 2 * SLOT
    side = {
        0: pm_ref[0, 0] + jnp.where(lane16 < SLOT, slo, zero),
        1: pm_ref[0, 1] + jnp.where(lane16 >= WIDE - SLOT, shi, zero),
        2: pm_ref[0, 2] + jnp.where(last, slo, jnp.where(front, shi, zero)),
        3: pm_ref[0, 3] + jnp.where(last, roll(slo, 2 * SLOT), jnp.where(front, roll(shi, -2 * SLOT), zero)),
    }
    bias = b2_ref[...]
    main = {r: speed_cap * jnp.tanh(x + bias) for r, x in main.items()}
    side = {k: speed_cap * jnp.tanh(x + bias) * lats_ref[2, 0:1] for k, x in side.items()}
    for part in range(2):
        for row in range(rows):
            out_ref[part, row * VG : (row + 1) * VG] = main[row][part * VG : (part + 1) * VG]
        for n in range(nvar):
            vel_ref[2 * n + part, 0] = out_ref[part, pl.ds(n, rows, stride=VG), :]

    q0 = {row: st8_ref[0, row] for row in range(rows)}
    for k in range(REACH):
        q0[k - REACH], q0[rows + k] = halo_ref[0, k], halo_ref[0, REACH + k]
    hlo, hhi = (x[(REACH + 1) * pair + pair :] for x in (lo, hi))
    hlo, hhi = hlo[0:VG] + hlo[VG:], hhi[0:VG] + hhi[VG:]
    last, front = lane >= WIDE - 2 * SLOT, lane < 2 * SLOT
    nil = jnp.zeros((VG, WIDE), f32)
    out_q = {
        0: sst_ref[0, 0],
        1: sst_ref[0, 1],
        2: jnp.where(last, hlo, jnp.where(front, hhi, nil)),
        3: jnp.where(last, roll(hlo, 2 * SLOT), jnp.where(front, roll(hhi, -2 * SLOT), nil)),
    }
    own_q = {0: own_ref[0, 0], 1: own_ref[0, 1], 2: nil, 3: nil}
    for row in list(range(-REACH, 0)) + list(range(rows, rows + REACH)):
        k, base = place(row, rows)
        own_q[k] = jnp.where(lane // SLOT == base // SLOT, roll(q0[row], base + SIDE), own_q[k])

    everywhere = range(-REACH, rows + REACH)
    own = {k: jnp.zeros((pair, WIDE), f32) for k in range(4)}
    for row in everywhere:
        k, base = place(row, rows)
        own[k] = jnp.where(lane16 // SLOT == base // SLOT, roll(main[row], base + SIDE), own[k])

    def tiles(out, inner):
        return {**{k: mix(out[k], inner[k]) for k in range(4)}, **{4 + k: mix(inner[k], out[k]) for k in range(4)}}

    s0 = tiles(out_q, own_q)
    vel_s = tiles(side, own)

    def tile_rows(s):
        def turned(own, halo, by, first):
            own, halo = roll(own, by), roll(halo, by)
            return jnp.where(first, halo, own), jnp.where(first, own, halo)

        before, after = {}, {}
        for t in (0, 4):
            before[t + 1], before[t + 3], after[t], after[t + 2] = s[t], s[t + 2], s[t + 1], s[t + 3]
            before[t], before[t + 2] = turned(s[t + 1], s[t + 3], SLOT, lane < SLOT)
            after[t + 1], after[t + 3] = turned(s[t], s[t + 2], -SLOT, lane >= WIDE - SLOT)
        return before, after

    u = {r: x[0:VG] for r, x in main.items()}
    us = {k: x[0:VG] for k, x in vel_s.items()}
    inside = range(1 - REACH, rows + REACH - 1)
    v = {r: main[r][VG:] for r in inside}
    vs = {k: x[VG:] for k, x in vel_s.items()}
    cosine, metric = lat_ref[0], lat_ref[1]

    def side_table(n, k):
        return mix(lats_ref[n], lats_ref[n + 3]) if k < 4 else mix(lats_ref[n + 3], lats_ref[n])

    cosine_s, metric_s = ([side_table(n, k) for k in range(8)] for n in range(2))
    flux = {r: x * cosine for r, x in v.items()}
    flux_s = {k: x * cosine_s[k] for k, x in vs.items()}
    ub, ua = tile_rows(us)

    def coefs(m, uu, vv, udiff, vdiff):
        div = m * (udiff * 0.5 + vdiff * 0.5)
        cl = m * jnp.maximum(uu, 0.0)
        cr = -(m * jnp.minimum(uu, 0.0))
        cd = jnp.maximum(vv, 0.0)
        cu = -jnp.minimum(vv, 0.0)
        return -(cl + cr + cd + cu + div), cl, cr, cd, cu

    cm = {r: coefs(metric, u[r], v[r], u[r + 1] - u[r - 1], roll(flux[r], -1) - roll(flux[r], 1)) for r in inside}
    cs = {k: coefs(metric_s[k], us[k], vs[k], ua[k] - ub[k], roll(flux_s[k], -1) - roll(flux_s[k], 1)) for k in range(8)}

    def stencil(c, x, left, right):
        return c[0] * x + c[1] * left + c[2] * right + c[3] * roll(x, 1) + c[4] * roll(x, -1)

    def rate(q, s, depth):
        rb, ra = tile_rows(s)
        inner = range(depth - REACH, rows + REACH - depth)
        wanted = [k for k in range(8) if depth < REACH or k % 4 < 2]
        return ({r: stencil(cm[r], q[r], q[r - 1], q[r + 1]) for r in inner},
                {k: stencil(cs[k], s[k], rb[k], ra[k]) for k in wanted})

    def moved(rates, by):
        return {r: q0[r] + by * x for r, x in rates[0].items()}, {k: s0[k] + by * x for k, x in rates[1].items()}

    one = rate(q0, s0, 1)
    two = rate(*moved(one, 0.5 * time_step), 2)
    three = rate(*moved(two, 0.5 * time_step), 3)
    four = rate(*moved(three, time_step), 4)

    def mean(n, k):
        return (one[n][k] + 2.0 * two[n][k] + 2.0 * three[n][k] + four[n][k]) / 6.0

    ends = {k: mix(mean(1, 4 + k), mean(1, k)) for k in range(2)}
    for row in range(rows):
        k, base = place(row, rows)
        at_end = (lane < REACH) | (lane >= WIDE - REACH)
        out_ref[0, row * VG : (row + 1) * VG] = jnp.where(at_end, roll(ends[k], -(base + SIDE)), mean(0, row))
    for n in range(nvar):
        ten_ref[n, 0] = out_ref[0, pl.ds(n, rows, stride=VG), :]


def full(shape):
    return pl.BlockSpec(shape, lambda *i: (0,) * len(shape))


def per_level(shape):
    return pl.BlockSpec((1,) + shape[1:], lambda i: (i,) + (0,) * (len(shape) - 1))


def level_part(shape, index, block=1, offset=0):
    return pl.BlockSpec((block,) + shape, lambda i: (i + offset, index) + (0,) * (len(shape) - 1))


def levels_of(shape, block=1, offset=0):
    return pl.BlockSpec((block,) + shape[1:], lambda i: (i + offset,) + (0,) * (len(shape) - 1))


def var_level(shape, offset=0):
    return pl.BlockSpec((shape[0], 1) + shape[2:], lambda i: (0, i + offset, 0, 0))


def body(hidden_in, w_conv1, b_conv1, w_conv2, b_conv2, state):
    lev, ch, rows, cols = hidden_in.shape
    nvar = state.shape[0]
    ext = cols + SLOT
    half = rows // 2
    params = pltpu.CompilerParams(vmem_limit_bytes=VMEM_LIMIT)
    smem = pl.BlockSpec(memory_space=pltpu.SMEM)
    sds = jax.ShapeDtypeStruct

    def call(kernel, steps, ins, outs, out_specs, scratch, args, cost=None, aliases={}):
        return pl.pallas_call(
            kernel,
            grid=(steps,),
            in_specs=ins,
            out_specs=out_specs,
            out_shape=outs,
            scratch_shapes=scratch,
            compiler_params=params,
            cost_estimate=cost,
            input_output_aliases=aliases,
        )(*args)

    flags = jnp.stack([lax.axis_index("lon") % 2, lax.axis_index("lat") % 2, lax.axis_index("lat")]).astype(jnp.int32)
    lon_wire = (lev, ch + 2 * nvar * REACH, cols)
    vmem = pl.BlockSpec(memory_space=pltpu.VMEM)
    lon_a, lon_b = pl.pallas_call(
        rows_kernel,
        in_specs=[smem] + [pl.BlockSpec(memory_space=pltpu.HBM)] * 2,
        out_specs=[vmem] * 2,
        out_shape=[sds(lon_wire, bf16)] * 2,
        scratch_shapes=[
            pltpu.VMEM((ch * rows, cols), f32),
            pltpu.VMEM(hidden_in.shape, bf16),
            pltpu.VMEM(state.shape, f32),
            pltpu.SemaphoreType.DMA((lev + 1,)),
        ],
        compiler_params=pltpu.CompilerParams(vmem_limit_bytes=ROWS_LIMIT),
    )(flags, hidden_in, state)
    shapes = [((12 * ch, 2 * ch), bf16), ((6 * SLOT, 4 * ch), bf16), ((9 * SLOT, ch), bf16),
              ((6 * SLOT, ch), bf16), ((1, 2 * ch), f32), ((2 * VG, WIDE), f32), ((3, VG, WIDE), f32), ((6, VG, WIDE), f32),
              ((2 * SLOT, 2 * ch), f32)]
    w1_one = w_conv1.reshape(9 * ch, ch)
    b1 = b_conv1.reshape(1, ch)
    n_lat = cols * lax.axis_size("lat")
    w1_pair, w2_pair, w2_one, w2_ends, b1_pair, b2, lat_main, lat_side, keep = pl.pallas_call(
        lambda flag_ref, *refs: prep_kernel(flag_ref, n_lat, cols, *refs),
        in_specs=[smem, smem] + [vmem] * 3,
        out_specs=[vmem] * len(shapes),
        out_shape=[sds(*x) for x in shapes],
        scratch_shapes=[pltpu.VMEM((4 * VG, ch), f32)],
        compiler_params=params,
    )(flags, b_conv2, w1_one, w_conv2.transpose(0, 1, 3, 2).reshape(9, 2 * nvar, ch), b1)
    lon_a = swap(lon_a, "lon", 0, True)
    lon_b = swap(lon_b, "lon", 1, True)

    hbm = pl.BlockSpec(memory_space=pltpu.HBM)
    g_pair = (lev, 2, cols, ch)
    st8_shape = (lev, rows, VG, WIDE)
    cut = (lev, rows * SIDE, ch)
    ps_shape = (lev, rows, 2 * VG, WIDE)
    own_shape = (lev, 2, VG, WIDE)
    halo_shape = (lev, 2 * REACH, VG, WIDE)
    shapes = [(g_pair, bf16), (g_pair, bf16), (cut, bf16), (cut, bf16), (st8_shape, f32), (own_shape, f32), (ps_shape, f32)]
    g_lo, g_hi, first, last, st8, own, ps = call(
        main_kernel,
        lev,
        [per_level(hidden_in.shape), var_level(state.shape), full(w1_pair.shape), full(w2_pair.shape), full((1, 2 * ch))],
        [sds(*x) for x in shapes],
        [per_level(x[0]) for x in shapes],
        [
            pltpu.VMEM((ch * (rows + VG), cols), f32),
            pltpu.VMEM((rows * (cols + SLOT), ch), f32),
            pltpu.VMEM((rows, cols, 3 * ch), bf16),
            pltpu.VMEM((rows + 2, cols, ch), bf16),
        ],
        (hidden_in, state, w1_pair, w2_pair, b1_pair),
        pl.CostEstimate(flops=2 * lev * rows * ext * 9 * ch * ch, bytes_accessed=8 * 2**20, transcendentals=0),
    )

    lat_wire = (lev, (rows + 2) * SIDE + 4 * VG, WIDE)
    pair_shape = (lev, 2, cols, ch)
    shapes = [(pair_shape, bf16), (halo_shape, f32), (lat_wire, bf16), (lat_wire, bf16)]
    row_pair, halo, lat_a, lat_b = call(
        pack_kernel,
        lev,
        [smem, per_level(lon_wire), per_level(lon_wire), per_level(cut), per_level(cut), per_level(own_shape)],
        [sds(*x) for x in shapes],
        [per_level(x[0]) for x in shapes],
        [pltpu.VMEM((nvar * REACH, WIDE), f32)],
        (flags, lon_a, lon_b, first, last, own),
    )
    lat_a = swap(lat_a, "lat", 0, False)
    lat_b = swap(lat_b, "lat", 1, False)

    block = EDGE_LEVELS
    four = (4, 2 * VG, WIDE)
    pe_shape = (lev, 6, 2 * VG, WIDE)
    here = functools.partial(levels_of, block=block)
    (pe,) = call(
        edge_kernel,
        lev // block,
        [here(pair_shape), here(g_pair), here(g_pair), full(w1_one.shape), full(w2_one.shape), full((1, ch)),
         level_part(four, 0, block), level_part(four, rows // 4 - 1, block)],
        [sds(pe_shape, f32)],
        [here(pe_shape)],
        [
            pltpu.VMEM((6 * block * (cols + SLOT), ch), f32),
            pltpu.VMEM((2 * block, cols, 9 * ch), bf16),
            pltpu.VMEM((2 * block * cols, ch), bf16),
        ],
        (row_pair, g_lo, g_hi, w1_one, w2_one, b1, ps, ps),
        pl.CostEstimate(flops=lev * 2 * 2 * ext * 9 * ch * ch, bytes_accessed=4 * 2**20, transcendentals=0),
    )

    block = SIDE_LEVELS
    parts = PARTS
    count = lev // parts
    wire = (count, 2 * VG * (REACH + 3), WIDE)
    pec_shape = (count,) + pe_shape[1:]
    pm4_shape = (count, 4, 2 * VG, WIDE)
    sst_shape = (count, 2, VG, WIDE)
    shapes = [(sst_shape, f32), (pm4_shape, f32), (pm4_shape, f32), (pec_shape, f32), (wire, bf16), (wire, bf16)]
    sent = []
    for part in range(parts):
        off = part * count // block
        here = functools.partial(levels_of, block=block, offset=off)
        sst, pm, cm, pec, out_a, out_b = call(
            side_kernel,
            count // block,
            [smem, here(cut), here(cut), here(pair_shape), here(lat_wire), here(lat_wire),
             full(w1_pair.shape), full(w2_pair.shape), full(w2_ends.shape), full((1, 2 * ch)), full((2 * SLOT, 2 * ch)),
             here(pe_shape), level_part(four, 0, block, off), level_part(four, rows // 4 - 1, block, off)],
            [sds(*x) for x in shapes],
            [levels_of(x[0], block) for x in shapes],
            [
                pltpu.VMEM((block, (rows + 2) * 2 * SLOT + 2 * SIDE, ch), f32),
                pltpu.VMEM((block, (rows + 2) * 2 * SLOT, 3 * ch), bf16),
                pltpu.VMEM((block, 2, 2, (half + 1) * SLOT, ch), bf16),
                pltpu.VMEM((max(WIDE, block * 4 * SLOT), ch), bf16),
            ],
            (flags, first, last, row_pair, lat_a, lat_b, w1_pair, w2_pair, w2_ends, b1_pair, keep, pe, ps, ps),
            pl.CostEstimate(flops=count * 512 * 12 * ch * ch, bytes_accessed=4 * 2**20, transcendentals=0),
        )
        sent.append((pec, pm, cm, sst, swap(out_a, "lon", 0, True), swap(out_b, "lon", 1, True)))

    outs = [sds((2 * nvar, lev, rows, cols), f32), sds(state.shape, f32)]
    done = ()
    for part, (pec, pm, cm, sst, out_a, out_b) in enumerate(sent):
        off = part * count
        here = functools.partial(levels_of, offset=off)
        var = functools.partial(var_level, offset=off)
        done = call(
            advect_kernel,
            count,
            [smem, here(ps_shape), per_level(pec_shape), per_level(pm4_shape), per_level(pm4_shape), per_level(wire),
             per_level(wire), here(st8.shape), here(halo_shape), per_level(sst_shape), here(own_shape),
             full(b2.shape), full(lat_main.shape), full(lat_side.shape)] + [hbm] * len(done),
            outs,
            [var(o.shape) for o in outs],
            [pltpu.VMEM((2, rows * VG, WIDE), f32)],
            (flags, ps, pec, pm, cm, out_a, out_b, st8, halo, sst, own, b2, lat_main, lat_side) + tuple(done),
            pl.CostEstimate(flops=count * 2**24, bytes_accessed=2 * 2**20, transcendentals=0),
            {14: 0, 15: 1} if done else {},
        )
    return tuple(done)


def solution(mesh):
    placed = (P(None, None, "lon", "lat"), P(), P(), P(), P(), P(None, None, "lon", "lat"))
    return jax.shard_map(
        body,
        mesh=mesh,
        in_specs=placed,
        out_specs=(P(None, None, "lon", "lat"), P(None, None, "lon", "lat")),
        check_vma=False,
    )
```

```python
import functools
import math

import jax
import jax.numpy as jnp
from jax import lax
from jax.experimental import pallas as pl
from jax.experimental.pallas import tpu as pltpu
from jax.sharding import PartitionSpec as P

time_step = 0.5
speed_cap = 0.6
cos_floor = 0.5

SIDE = 8
SLOT = 2 * SIDE
WIDE = 128
REACH = 4
VG = 8
VMEM_LIMIT = 24 * 2**20
ROWS_LIMIT = 50 * 2**20
EDGE_LEVELS = 8
ADVECT_UNROLL = 2
SIDE_LEVELS = 4
PARTS = 2
PACK_UNROLL = 4
f32 = jnp.float32
bf16 = jnp.bfloat16


def swap_pairs(count, first, closed):
    pairs = []
    for low in range(first, count, 2):
        high = low + 1
        if high >= count and not closed:
            continue
        pairs += [(low, high % count), (high % count, low)]
    return pairs


def swap(block, axis, first, closed):
    return lax.ppermute(block, axis, swap_pairs(lax.axis_size(axis), first, closed))


def place(row, rows):
    half, par = row // 2, row % 2
    own = 0 <= half < rows // 2
    return (0 if own else 2) + par, SLOT * (half % (rows // 2))


def lanes(shape):
    return lax.broadcasted_iota(jnp.int32, shape, len(shape) - 1)


def roll(x, by):
    by = by % WIDE
    return pltpu.roll(x, by, x.ndim - 1) if by else x


def col_before(mains, sides, at):
    lane = lanes(next(iter(mains.values())).shape)
    new_sides = {k: roll(s, 1) for k, s in sides.items()}
    new_mains = {}
    for row, main in mains.items():
        k, base = at(row)
        new_mains[row] = jnp.where(lane == 0, roll(sides[k], 1 - base - SIDE), roll(main, 1))
        new_sides[k] = jnp.where(lane == base + SIDE, roll(main, base + SIDE + 1), new_sides[k])
    return new_mains, new_sides


def col_after(mains, sides, at):
    lane = lanes(next(iter(mains.values())).shape)
    new_sides = {k: roll(s, -1) for k, s in sides.items()}
    new_mains = {}
    for row, main in mains.items():
        k, base = at(row)
        new_mains[row] = jnp.where(lane == WIDE - 1, roll(sides[k], WIDE - 1 - base - SIDE), roll(main, -1))
        new_sides[k] = jnp.where(lane == base + SIDE - 1, roll(main, base + SIDE - 1), new_sides[k])
    return new_mains, new_sides


def join_taps(x):
    return roll(x[0:SLOT], 1) + x[SLOT : 2 * SLOT] + roll(x[2 * SLOT : 3 * SLOT], -1)


def mix(first, second):
    return jnp.where(lanes(first.shape) % SLOT < SIDE, first, second)


def add_columns(main, side, base):
    lane = lanes(main.shape)
    return main + jnp.where((lane < SIDE) | (lane >= WIDE - SIDE), roll(side, -(base + SIDE)), 0.0)


def two_terms(x):
    first = x.astype(bf16)
    return [first, (x - first.astype(f32)).astype(bf16)]


def nt(lhs, rhs):
    return lax.dot_general(lhs, rhs, (((1,), (1,)), ((), ())), preferred_element_type=f32)


def silu(s):
    return s / (1.0 + jnp.exp(-s))


def shifted(e_ref, start, s_ref, to, count, first=0):
    ch = e_ref.shape[-1]
    for b in range(3):
        lane0 = first + b * ch
        s_ref[to, :, lane0 : lane0 + ch] = e_ref[pl.ds(start - 1 + b, count), :].astype(bf16)


def rows_kernel(flag_ref, x_hbm, st_hbm, outa_ref, outb_ref, x32_ref, x_ref, st_ref, sem):
    levels, ch, rows, cols = x_hbm.shape
    nvar = st_hbm.shape[0]
    size = nvar * REACH
    even = flag_ref[0] == 0

    def level_copy(lv):
        return pltpu.make_async_copy(x_hbm.at[lv], x_ref.at[lv], sem.at[lv])

    state_copy = pltpu.make_async_copy(st_hbm, st_ref, sem.at[levels])
    level_copy(0).start()
    state_copy.start()
    for lv in range(1, levels):
        level_copy(lv).start()
    state_copy.wait()

    def one(lv, carry):
        level_copy(lv).wait()
        x32_ref[...] = x_ref[lv].astype(f32).reshape(ch * rows, cols)
        lo, hi = (x32_ref[pl.ds(row, ch, stride=rows), :].astype(bf16) for row in (0, rows - 1))
        outa_ref[lv, 0:ch] = jnp.where(even, hi, lo)
        outb_ref[lv, 0:ch] = jnp.where(even, lo, hi)
        for n in range(nvar):
            x32_ref[n * REACH : (n + 1) * REACH] = st_ref[n, lv, 0:REACH]
            x32_ref[size + n * REACH : size + (n + 1) * REACH] = st_ref[n, lv, rows - REACH :]
        lo, hi = x32_ref[0:size], x32_ref[size : 2 * size]
        outa_ref[lv, ch:] = jnp.concatenate(two_terms(jnp.where(even, hi, lo)), axis=0)
        outb_ref[lv, ch:] = jnp.concatenate(two_terms(jnp.where(even, lo, hi)), axis=0)
        return carry

    lax.fori_loop(0, levels, one, 0)


def prep_kernel(flag_ref, n_lat, cols, b2_ref, w1_ref, w2_ref, b1_ref,
                w1p_ref, w2p_ref, w2o_ref, w2e_ref, b1p_ref, b2o_ref, lat_ref, lats_ref, keep_ref, w2s_ref):
    size, ch = w1_ref.shape
    nvar = w2_ref.shape[1] // 2
    w1p_ref[0:size, 0:ch] = w1_ref[...]
    w1p_ref[size:, 0:ch] = jnp.zeros((3 * ch, ch), bf16)
    w1p_ref[0 : 3 * ch, ch:] = jnp.zeros((3 * ch, ch), bf16)
    w1p_ref[3 * ch :, ch:] = w1_ref[...]
    b1p_ref[:, 0:ch] = b1_ref[...]
    b1p_ref[:, ch:] = b1_ref[...]
    w2p_ref[...] = jnp.zeros_like(w2p_ref)
    w2s_ref[0 : 2 * VG] = jnp.zeros((2 * VG, ch), f32)
    for a in range(3):
        for b in range(3):
            w2s_ref[2 * VG : 2 * VG + 2 * nvar] = w2_ref[3 * a + b].astype(f32)
            for part in range(2):
                w2s_ref[part * VG : part * VG + nvar] = w2s_ref[pl.ds(2 * VG + part, nvar, stride=2), :]
            here = w2s_ref[0 : 2 * VG].astype(bf16)
            at = 3 * a + b
            w2o_ref[at * SLOT : (at + 1) * SLOT] = here
            for k in range(2):
                first = (3 * k + b) * SLOT
                w2p_ref[first : first + SLOT, (a + k) * ch : (a + k + 1) * ch] = here
            if a != 1:
                first = (3 * (a // 2) + b) * SLOT
                w2e_ref[first : first + SLOT] = here
    b2o_ref[...] = jnp.zeros_like(b2o_ref)
    for v in range(2 * nvar):
        row = (v % 2) * VG + v // 2
        b2o_ref[row : row + 1] = jnp.full((1, WIDE), b2_ref[v], f32)

    def table(place_in):
        place_in = place_in + flag_ref[2] * cols
        keep = ((place_in >= 0) & (place_in < n_lat)).astype(f32)
        phi = (place_in.astype(f32) + 0.5) * (math.pi / n_lat) - 0.5 * math.pi
        cosine = jnp.maximum(jnp.cos(phi), cos_floor)
        return cosine, 1.0 / cosine, keep

    lane = lanes((VG, WIDE))
    slot = lane % SLOT
    beyond = jnp.where(slot < SIDE, slot - SIDE, cols + slot - SIDE)
    ends = jnp.where(slot < SIDE, cols - SIDE + slot, slot - SIDE)
    for ref, first, place_in in ((lat_ref, 0, lane), (lats_ref, 0, beyond), (lats_ref, 3, ends)):
        for k, x in enumerate(table(place_in)):
            ref[first + k] = x
    spot = lax.broadcasted_iota(jnp.int32, keep_ref.shape, 0)
    place_in = jnp.where(spot < SIDE, spot - SIDE + 1, cols - SIDE - 1 + spot) + flag_ref[2] * cols
    keep_ref[...] = ((place_in >= 0) & (place_in < n_lat)).astype(f32)


def main_kernel(x_ref, st_ref, w1_ref, w2_ref, b1_ref, glo_ref, ghi_ref, first_ref, last_ref, st8_ref, own_ref, ps_ref,
                x32_ref, e_ref, s_ref, h_ref):
    chans, rows, cols = x_ref.shape[1:]
    nvar = st_ref.shape[0]
    half = rows // 2
    pitch = cols + SLOT
    step = rows + VG
    x32_ref.reshape(chans, step, cols)[:, 0:rows] = x_ref[0].astype(f32)

    @pl.when(pl.program_id(0) == 0)
    def _():
        e_ref[...] = jnp.zeros_like(e_ref)
        h_ref[...] = jnp.zeros_like(h_ref)

    place_in = lax.broadcasted_iota(jnp.int32, (cols, 2 * chans), 0)
    within = (place_in > 0) & (place_in < cols - 1)

    def hidden_pair(m):
        lhs = jnp.concatenate([s_ref[2 * m + r] for r in range(4)], axis=1)
        acc = jnp.dot(lhs, w1_ref[...], preferred_element_type=f32) + b1_ref[...]
        hid = jnp.where(within, silu(acc), 0.0).astype(bf16)
        for k in range(2):
            h_ref[2 * m + 2 + k] = hid[:, k * chans : (k + 1) * chans]

    def sum_pair(m):
        q = nt(w2_ref[...], jnp.concatenate([h_ref[2 * m + r] for r in range(4)], axis=1))
        for k in range(2):
            ps_ref[0, 2 * m + k] = join_taps(q[k * 3 * SLOT : (k + 1) * 3 * SLOT])

    sides = [[], []]
    for row in range(rows):
        block = x32_ref[pl.ds(row, chans, stride=step), :].T
        start = row * pitch + SIDE
        e_ref[start : start + cols] = block
        for k, part in enumerate((block[0:SIDE], block[cols - SIDE :])):
            sides[k].append(part)
        if row < 2:
            glo_ref[0, row] = block.astype(bf16)
        if row >= rows - 2:
            ghi_ref[0, row - (rows - 2)] = block.astype(bf16)
        shifted(e_ref, start, s_ref, row, cols)
    first_ref[0] = jnp.concatenate(sides[0], axis=0).astype(bf16)
    last_ref[0] = jnp.concatenate(sides[1], axis=0).astype(bf16)
    for m in range(half - 1):
        hidden_pair(m)
    for m in range(half):
        sum_pair(m)
    for n in range(nvar):
        x32_ref[pl.ds(n, rows, stride=VG), :] = st_ref[n, 0]
    lane = lanes((VG, WIDE))
    own = [jnp.zeros((VG, WIDE), f32)] * 2
    for row in range(rows):
        block = x32_ref[row * VG : (row + 1) * VG]
        block = jnp.where(lax.broadcasted_iota(jnp.int32, (VG, WIDE), 0) < nvar, block, 0.0)
        st8_ref[0, row] = block
        par, base = place(row, rows)
        own[par] = jnp.where(lane // SLOT == base // SLOT, roll(block, base + SIDE), own[par])
    own_ref[0, 0], own_ref[0, 1] = own


def pack_kernel(flag_ref, a_ref, b_ref, first_ref, last_ref, own_ref, row_ref, halo_ref, outa_ref, outb_ref, x_ref):
    cols = a_ref.shape[2]
    ch = row_ref.shape[3]
    size = (a_ref.shape[1] - ch) // 2
    nvar = size // REACH
    even = flag_ref[0] == 0
    lat_even = flag_ref[1] == 0
    got_a, got_b = a_ref[0].astype(f32), b_ref[0].astype(f32)
    low, high = jnp.where(even, got_b, got_a), jnp.where(even, got_a, got_b)
    halo_ref[...] = jnp.zeros_like(halo_ref)
    for k, x in enumerate((low, high)):
        x_ref[...] = x[ch : ch + size] + x[ch + size :]
        for r in range(REACH):
            halo_ref[0, k * REACH + r, 0:nvar] = x_ref[pl.ds(r, nvar, stride=REACH), :]
    low, high = low[0:ch].T, high[0:ch].T
    row_ref[0, 0] = low.astype(bf16)
    row_ref[0, 1] = high.astype(bf16)
    terms = two_terms(own_ref[0, 0]) + two_terms(own_ref[0, 1])
    first = [low[0:SIDE].astype(bf16), first_ref[0], high[0:SIDE].astype(bf16)]
    last = [low[cols - SIDE :].astype(bf16), last_ref[0], high[cols - SIDE :].astype(bf16)]
    first, last = jnp.concatenate(first, axis=0), jnp.concatenate(last, axis=0)
    count = first.shape[0]
    for out, pick in ((outa_ref, jnp.where(lat_even, last, first)), (outb_ref, jnp.where(lat_even, first, last))):
        out[0, 0:count] = pick
        out[0, count:] = jnp.concatenate(terms, axis=0)


def edge_kernel(row_ref, g0_ref, g1_ref, w1_ref, w2_ref, b1_ref, ps0_ref, ps1_ref, pe_ref, e_ref, s_ref, h_ref):
    levels = row_ref.shape[0]
    cols, ch = row_ref.shape[2:]
    pitch = cols + SLOT
    e_ref[...] = jnp.zeros_like(e_ref)
    for lv in range(levels):
        for k in range(2):
            part = [g0_ref[lv, 0], g0_ref[lv, 1]] if k == 0 else [g1_ref[lv, 0], g1_ref[lv, 1]]
            part = [row_ref[lv, 0]] + part if k == 0 else part + [row_ref[lv, 1]]
            for r in range(3):
                start = (6 * lv + 3 * k + r) * pitch + SIDE
                e_ref[start : start + cols] = part[r].astype(f32)
                shifted(e_ref, start, s_ref, 2 * lv + k, cols, 3 * ch * r)
    acc = jnp.dot(s_ref[...].reshape(2 * levels * cols, 9 * ch), w1_ref[...], preferred_element_type=f32) + b1_ref[...]
    place_in = lax.broadcasted_iota(jnp.int32, (cols, ch), 0)
    within = (place_in > 0) & (place_in < cols - 1)
    hid = silu(acc)
    for n in range(2 * levels):
        here = slice(n * cols, (n + 1) * cols)
        h_ref[here] = jnp.where(within, hid[here], 0.0).astype(bf16)
    q = nt(w2_ref[...], h_ref[...])
    for lv in range(levels):
        for k in range(2):
            here = slice((2 * lv + k) * cols, (2 * lv + k + 1) * cols)
            for a in range(3):
                x = join_taps(q[a * 3 * SLOT : (a + 1) * 3 * SLOT, here])
                if k == 0 and a < 2:
                    x = x + ps0_ref[lv, 1 - a]
                if k == 1 and a > 0:
                    x = x + ps1_ref[lv, 4 - a]
                pe_ref[lv, 3 * k + 2 - a] = x


def side_kernel(flag_ref, first_ref, last_ref, row_ref, la_ref, lb_ref, w1_ref, w2_ref, w2e_ref, b1_ref, keep_ref,
                pe_ref, ps0_ref, ps1_ref, sst_ref, pm_ref, cm_ref, pec_ref, outa_ref, outb_ref, e_ref, s_ref, hs_ref, z_ref):
    levels = row_ref.shape[0]
    cols, ch = row_ref.shape[2:]
    rows = first_ref.shape[1] // SIDE
    half = rows // 2
    even = flag_ref[0] == 0
    lat_even = flag_ref[1] == 0
    wide = 2 * SLOT
    lane = lanes((2 * VG, WIDE))
    begin, end = lane < SLOT, lane >= WIDE - SLOT
    e_ref[...] = jnp.zeros_like(e_ref)
    hs_ref[...] = jnp.zeros_like(hs_ref)
    z_ref[...] = jnp.zeros_like(z_ref)
    for lv in range(levels):
        a, b = la_ref[lv], lb_ref[lv]
        right, left = jnp.where(lat_even, a, b), jnp.where(lat_even, b, a)
        count = (rows + 2) * SIDE
        for k in range(2):
            st = []
            for x in (left, right):
                x = x[count + 2 * k * VG : count + (2 * k + 2) * VG].astype(f32)
                st.append(x[0:VG] + x[VG:])
            sst_ref[lv, k] = mix(st[0], st[1])
        right, left = right[0:count].astype(f32), left[0:count].astype(f32)
        first, last = first_ref[lv].astype(f32), last_ref[lv].astype(f32)
        low, high = row_ref[lv, 0].astype(f32), row_ref[lv, 1].astype(f32)
        for row in range(-1, rows + 1):
            side = slice((row + 1) * SIDE, (row + 2) * SIDE)
            if 0 <= row < rows:
                own = slice(row * SIDE, (row + 1) * SIDE)
                mine = first[own], last[own]
            else:
                x = low if row < 0 else high
                mine = x[0:SIDE], x[cols - SIDE :]
            start = SIDE + (row + 1) * wide
            for k, part in enumerate((left[side], mine[0], mine[1], right[side])):
                e_ref[lv, start + k * SIDE : start + (k + 1) * SIDE] = part
        for row in range(rows + 2):
            for b in range(3):
                start = SIDE + row * wide + b
                x = [e_ref[lv, pl.ds(start, SIDE), :], e_ref[lv, pl.ds(start + 3 * SIDE - 2, SIDE), :]]
                x = jnp.concatenate(x, axis=0).astype(bf16)
                s_ref[lv, row * SLOT : (row + 1) * SLOT, b * ch : (b + 1) * ch] = x
    s = s_ref[...].reshape(levels, half + 1, 2, SLOT, 3 * ch)
    part = [s[:, 0:half, 0], s[:, 0:half, 1], s[:, 1:, 0], s[:, 1:, 1]]
    lhs = jnp.concatenate([p.reshape(levels * half * SLOT, 3 * ch) for p in part], axis=1)
    acc = jnp.dot(lhs, w1_ref[...], preferred_element_type=f32) + b1_ref[...]
    hid = silu(acc).reshape(levels, half, SLOT, 2 * ch) * keep_ref[...]
    for lv in range(levels):
        for m in range(half):
            here = hid[lv, m].astype(bf16)
            hs_ref[lv, 0, m * SLOT : (m + 1) * SLOT] = here[:, 0:ch]
            hs_ref[lv, 1, (m + 1) * SLOT : (m + 2) * SLOT] = here[:, ch:]
            if m == 0:
                z_ref[2 * lv * SLOT : (2 * lv + 1) * SLOT] = here[:, 0:ch]
            if m == half - 1:
                z_ref[(2 * lv + 1) * SLOT : (2 * lv + 2) * SLOT] = here[:, ch:]
    size = half * SLOT
    rhs = []
    for lv in range(levels):
        odd, ev = hs_ref.at[lv, 1], hs_ref.at[lv, 0]
        rhs.append(jnp.concatenate([odd[0:size], ev[0:size], odd[SLOT : size + SLOT], ev[SLOT : size + SLOT]], axis=1))
    q_side = nt(w2_ref[...], jnp.concatenate(rhs, axis=0))
    q_ends = nt(w2e_ref[...], z_ref[...])
    in_left = lanes((SLOT, WIDE)) % SLOT < SIDE

    def join_sides(q):
        taps = [q[b * SLOT : (b + 1) * SLOT] for b in range(3)]
        l = [jnp.where(in_left, x, 0.0) for x in taps]
        r = [jnp.where(in_left, 0.0, x) for x in taps]
        l = roll(l[0], 2) + roll(l[1], 1) + l[2]
        r = r[0] + roll(r[1], -1) + roll(r[2], -2)
        return mix(l, r), mix(r, l)

    for lv in range(levels):
        out, inn = {}, {}
        q = q_side[:, lv * size : (lv + 1) * size]
        for k in range(2):
            out[k], inn[k] = join_sides(q[k * 3 * SLOT : (k + 1) * 3 * SLOT])
        per = WIDE // (2 * SLOT)
        q = roll(q_ends[:, (lv // per) * WIDE : (lv // per + 1) * WIDE], -(lv % per) * 2 * SLOT)
        prev = join_sides(q[3 * SLOT : 6 * SLOT])
        nxt = join_sides(q[0 : 3 * SLOT])
        for k, x, spot, by in ((3, prev, end, WIDE - SLOT), (2, nxt, begin, -SLOT)):
            out[k], inn[k] = (jnp.where(spot, roll(y, by), 0.0) for y in x)
        for k in range(4):
            pm_ref[lv, k] = out[k]
            cm_ref[lv, k] = inn[k]
        mains = {}
        for k, row in enumerate((-1, 0, 1, rows - 2, rows - 1, rows)):
            mains[row] = pe_ref[lv, k]
        mains[2], mains[3] = ps0_ref[lv, 2], ps0_ref[lv, 3]
        mains[rows - 4], mains[rows - 3] = ps1_ref[lv, 0], ps1_ref[lv, 1]
        for row in mains:
            k, base = place(row, rows)
            mains[row] = add_columns(mains[row], inn[k], base)
        for k, row in enumerate((-1, 0, 1, rows - 2, rows - 1, rows)):
            pec_ref[lv, k] = mains[row]
        lane8 = lanes((VG, WIDE))
        st = sst_ref[lv, 0], sst_ref[lv, 1]
        st_lo = two_terms(jnp.where(lane8 < 2 * SLOT, st[0], roll(st[1], 2 * SLOT)))
        st_hi = two_terms(jnp.where(lane8 >= WIDE - 2 * SLOT, st[0], roll(st[1], -2 * SLOT)))
        side_lo = jnp.where(lane < 2 * SLOT, out[0], jnp.where(lane < 4 * SLOT, roll(out[1], 2 * SLOT), out[3]))
        side_hi = jnp.where(lane >= WIDE - 2 * SLOT, out[0],
                            jnp.where(lane >= WIDE - 4 * SLOT, roll(out[1], -2 * SLOT), out[2]))
        out_lo = jnp.concatenate([mains[-1], mains[0], mains[1], mains[2], side_lo, mains[3]], axis=0)
        out_hi = jnp.concatenate([mains[rows - k] for k in range(4)] + [side_hi, mains[rows - 4]], axis=0)
        main_rows = out_lo.shape[0]
        outa_ref[lv, 0:main_rows] = jnp.where(even, out_hi, out_lo).astype(bf16)
        outb_ref[lv, 0:main_rows] = jnp.where(even, out_lo, out_hi).astype(bf16)
        outa_ref[lv, main_rows:] = jnp.concatenate([jnp.where(even, h, l) for h, l in zip(st_hi, st_lo)], axis=0)
        outb_ref[lv, main_rows:] = jnp.concatenate([jnp.where(even, l, h) for h, l in zip(st_hi, st_lo)], axis=0)


def advect_kernel(flag_ref, ps_ref, pe_ref, pm_ref, cm_ref, a_ref, b_ref, st8_ref, halo_ref, sst_ref, own_ref,
                  b2_ref, lat_ref, lats_ref, *rest):
    vel_ref, ten_ref, out_ref = rest[-3:]
    rows = st8_ref.shape[1]
    nvar = ten_ref.shape[0]
    even = flag_ref[0] == 0
    lane16 = lanes((2 * VG, WIDE))
    lane = lanes((VG, WIDE))
    pair = 2 * VG

    def halos(xa, xb):
        return jnp.where(even, xb, xa), jnp.where(even, xa, xb)

    lo, hi = halos(a_ref[0].astype(f32), b_ref[0].astype(f32))
    main = {}
    for row in range(2, rows - 2):
        k, base = place(row, rows)
        main[row] = add_columns(ps_ref[0, row], cm_ref[0, k], base)
    for k, row in enumerate((-1, 0, 1, rows - 2, rows - 1, rows)):
        main[row] = pe_ref[0, k]
    for k in range(REACH + 1):
        there = slice(k * pair, (k + 1) * pair) if k < REACH else slice((k + 1) * pair, (k + 2) * pair)
        for got, row in ((lo, -k), (hi, rows - 1 + k)):
            main[row] = main[row] + got[there] if row in main else got[there]
    slo, shi = (got[REACH * pair : (REACH + 1) * pair] for got in (lo, hi))
    zero = jnp.zeros((pair, WIDE), f32)
    last, front = lane16 >= WIDE - 2 * SLOT, lane16 < 2 * SLOT
    side = {
        0: pm_ref[0, 0] + jnp.where(lane16 < SLOT, slo, zero),
        1: pm_ref[0, 1] + jnp.where(lane16 >= WIDE - SLOT, shi, zero),
        2: pm_ref[0, 2] + jnp.where(last, slo, jnp.where(front, shi, zero)),
        3: pm_ref[0, 3] + jnp.where(last, roll(slo, 2 * SLOT), jnp.where(front, roll(shi, -2 * SLOT), zero)),
    }
    bias = b2_ref[...]
    main = {r: speed_cap * jnp.tanh(x + bias) for r, x in main.items()}
    side = {k: speed_cap * jnp.tanh(x + bias) * lats_ref[2, 0:1] for k, x in side.items()}
    for part in range(2):
        for row in range(rows):
            out_ref[part, row * VG : (row + 1) * VG] = main[row][part * VG : (part + 1) * VG]
        for n in range(nvar):
            vel_ref[2 * n + part, 0] = out_ref[part, pl.ds(n, rows, stride=VG), :]

    q0 = {row: st8_ref[0, row] for row in range(rows)}
    for k in range(REACH):
        q0[k - REACH], q0[rows + k] = halo_ref[0, k], halo_ref[0, REACH + k]
    hlo, hhi = (x[(REACH + 1) * pair + pair :] for x in (lo, hi))
    hlo, hhi = hlo[0:VG] + hlo[VG:], hhi[0:VG] + hhi[VG:]
    last, front = lane >= WIDE - 2 * SLOT, lane < 2 * SLOT
    nil = jnp.zeros((VG, WIDE), f32)
    out_q = {
        0: sst_ref[0, 0],
        1: sst_ref[0, 1],
        2: jnp.where(last, hlo, jnp.where(front, hhi, nil)),
        3: jnp.where(last, roll(hlo, 2 * SLOT), jnp.where(front, roll(hhi, -2 * SLOT), nil)),
    }
    own_q = {0: own_ref[0, 0], 1: own_ref[0, 1], 2: nil, 3: nil}
    for row in list(range(-REACH, 0)) + list(range(rows, rows + REACH)):
        k, base = place(row, rows)
        own_q[k] = jnp.where(lane // SLOT == base // SLOT, roll(q0[row], base + SIDE), own_q[k])

    everywhere = range(-REACH, rows + REACH)
    own = {k: jnp.zeros((pair, WIDE), f32) for k in range(4)}
    for row in everywhere:
        k, base = place(row, rows)
        own[k] = jnp.where(lane16 // SLOT == base // SLOT, roll(main[row], base + SIDE), own[k])

    def tiles(out, inner):
        return {**{k: mix(out[k], inner[k]) for k in range(4)}, **{4 + k: mix(inner[k], out[k]) for k in range(4)}}

    s0 = tiles(out_q, own_q)
    vel_s = tiles(side, own)

    def tile_rows(s):
        def turned(own, halo, by, first):
            own, halo = roll(own, by), roll(halo, by)
            return jnp.where(first, halo, own), jnp.where(first, own, halo)

        before, after = {}, {}
        for t in (0, 4):
            before[t + 1], before[t + 3], after[t], after[t + 2] = s[t], s[t + 2], s[t + 1], s[t + 3]
            before[t], before[t + 2] = turned(s[t + 1], s[t + 3], SLOT, lane < SLOT)
            after[t + 1], after[t + 3] = turned(s[t], s[t + 2], -SLOT, lane >= WIDE - SLOT)
        return before, after

    u = {r: x[0:VG] for r, x in main.items()}
    us = {k: x[0:VG] for k, x in vel_s.items()}
    inside = range(1 - REACH, rows + REACH - 1)
    v = {r: main[r][VG:] for r in inside}
    vs = {k: x[VG:] for k, x in vel_s.items()}
    cosine, metric = lat_ref[0], lat_ref[1]

    def side_table(n, k):
        return mix(lats_ref[n], lats_ref[n + 3]) if k < 4 else mix(lats_ref[n + 3], lats_ref[n])

    cosine_s, metric_s = ([side_table(n, k) for k in range(8)] for n in range(2))
    flux = {r: x * cosine for r, x in v.items()}
    flux_s = {k: x * cosine_s[k] for k, x in vs.items()}
    ub, ua = tile_rows(us)

    def coefs(m, uu, vv, udiff, vdiff):
        flow = m * uu
        cl = jnp.maximum(flow, 0.0)
        cr = cl - flow
        cd = jnp.maximum(vv, 0.0)
        cu = cd - vv
        div = (0.5 * m) * (udiff + vdiff)
        return -((cl + cr) + (cd + cu) + div), cl, cr, cd, cu

    cm = {r: coefs(metric, u[r], v[r], u[r + 1] - u[r - 1], roll(flux[r], -1) - roll(flux[r], 1)) for r in inside}
    cs = {k: coefs(metric_s[k], us[k], vs[k], ua[k] - ub[k], roll(flux_s[k], -1) - roll(flux_s[k], 1)) for k in range(8)}

    def stencil(c, x, left, right):
        return c[0] * x + c[1] * left + c[2] * right + c[3] * roll(x, 1) + c[4] * roll(x, -1)

    def rate(q, s, depth):
        rb, ra = tile_rows(s)
        inner = range(depth - REACH, rows + REACH - depth)
        wanted = [k for k in range(8) if depth < REACH or k % 4 < 2]
        return ({r: stencil(cm[r], q[r], q[r - 1], q[r + 1]) for r in inner},
                {k: stencil(cs[k], s[k], rb[k], ra[k]) for k in wanted})

    def moved(rates, by):
        return {r: q0[r] + by * x for r, x in rates[0].items()}, {k: s0[k] + by * x for k, x in rates[1].items()}

    one = rate(q0, s0, 1)
    two = rate(*moved(one, 0.5 * time_step), 2)
    three = rate(*moved(two, 0.5 * time_step), 3)
    four = rate(*moved(three, time_step), 4)

    def mean(n, k):
        return (one[n][k] + four[n][k] + 2.0 * (two[n][k] + three[n][k])) * (1.0 / 6.0)

    ends = {k: mix(mean(1, 4 + k), mean(1, k)) for k in range(2)}
    for row in range(rows):
        k, base = place(row, rows)
        at_end = (lane < REACH) | (lane >= WIDE - REACH)
        out_ref[0, row * VG : (row + 1) * VG] = jnp.where(at_end, roll(ends[k], -(base + SIDE)), mean(0, row))
    for n in range(nvar):
        ten_ref[n, 0] = out_ref[0, pl.ds(n, rows, stride=VG), :]


def full(shape):
    return pl.BlockSpec(shape, lambda *i: (0,) * len(shape))


def per_level(shape):
    return pl.BlockSpec((1,) + shape[1:], lambda i: (i,) + (0,) * (len(shape) - 1))


def level_part(shape, index, block=1, offset=0):
    return pl.BlockSpec((block,) + shape, lambda i: (i + offset, index) + (0,) * (len(shape) - 1))


def levels_of(shape, block=1, offset=0):
    return pl.BlockSpec((block,) + shape[1:], lambda i: (i + offset,) + (0,) * (len(shape) - 1))


def var_level(shape, offset=0):
    return pl.BlockSpec((shape[0], 1) + shape[2:], lambda i: (0, i + offset, 0, 0))


def body(hidden_in, w_conv1, b_conv1, w_conv2, b_conv2, state):
    lev, ch, rows, cols = hidden_in.shape
    nvar = state.shape[0]
    ext = cols + SLOT
    half = rows // 2
    params = pltpu.CompilerParams(vmem_limit_bytes=VMEM_LIMIT)
    smem = pl.BlockSpec(memory_space=pltpu.SMEM)
    sds = jax.ShapeDtypeStruct

    def call(kernel, steps, ins, outs, out_specs, scratch, args, cost=None, aliases={}):
        return pl.pallas_call(
            kernel,
            grid=(steps,),
            in_specs=ins,
            out_specs=out_specs,
            out_shape=outs,
            scratch_shapes=scratch,
            compiler_params=params,
            cost_estimate=cost,
            input_output_aliases=aliases,
        )(*args)

    vmem = pl.BlockSpec(memory_space=pltpu.VMEM)

    def levels(block=1, off=0, first=None, size=None):
        def view(ref, i):
            here = pl.ds(off + i * block, block)
            return ref.at[here] if first is None else ref.at[here, first : first + size]

        return view

    def whole(kernel, steps, ins, outs, scratch, cost, unroll=1):
        views = [v for _, v in ins] + [v for _, v in outs]

        def run(*refs):
            def one(i, carry):
                kernel(*[v(r, i) if v else r for v, r in zip(views, refs)], *refs[len(views) :])
                return carry

            if steps == 1:
                one(0, 0)
            else:
                lax.fori_loop(0, steps, one, 0, unroll=unroll)

        return pl.pallas_call(
            run,
            in_specs=[smem if x is flags else vmem for x, _ in ins],
            out_specs=[vmem] * len(outs),
            out_shape=[x for x, _ in outs],
            scratch_shapes=scratch,
            compiler_params=params,
            cost_estimate=pl.CostEstimate(flops=cost, bytes_accessed=2**20, transcendentals=0),
        )(*[x for x, _ in ins])

    flags = jnp.stack([lax.axis_index("lon") % 2, lax.axis_index("lat") % 2, lax.axis_index("lat")]).astype(jnp.int32)
    lon_wire = (lev, ch + 2 * nvar * REACH, cols)
    lon_a, lon_b = pl.pallas_call(
        rows_kernel,
        in_specs=[smem] + [pl.BlockSpec(memory_space=pltpu.HBM)] * 2,
        out_specs=[vmem] * 2,
        out_shape=[sds(lon_wire, bf16)] * 2,
        scratch_shapes=[
            pltpu.VMEM((ch * rows, cols), f32),
            pltpu.VMEM(hidden_in.shape, bf16),
            pltpu.VMEM(state.shape, f32),
            pltpu.SemaphoreType.DMA((lev + 1,)),
        ],
        compiler_params=pltpu.CompilerParams(vmem_limit_bytes=ROWS_LIMIT),
    )(flags, hidden_in, state)
    shapes = [((12 * ch, 2 * ch), bf16), ((6 * SLOT, 4 * ch), bf16), ((9 * SLOT, ch), bf16),
              ((6 * SLOT, ch), bf16), ((1, 2 * ch), f32), ((2 * VG, WIDE), f32), ((3, VG, WIDE), f32), ((6, VG, WIDE), f32),
              ((SLOT, 2 * ch), f32)]
    w1_one = w_conv1.reshape(9 * ch, ch)
    b1 = b_conv1.reshape(1, ch)
    n_lat = cols * lax.axis_size("lat")
    w1_pair, w2_pair, w2_one, w2_ends, b1_pair, b2, lat_main, lat_side, keep = pl.pallas_call(
        lambda flag_ref, *refs: prep_kernel(flag_ref, n_lat, cols, *refs),
        in_specs=[smem, smem] + [vmem] * 3,
        out_specs=[vmem] * len(shapes),
        out_shape=[sds(*x) for x in shapes],
        scratch_shapes=[pltpu.VMEM((4 * VG, ch), f32)],
        compiler_params=params,
    )(flags, b_conv2, w1_one, w_conv2.transpose(0, 1, 3, 2).reshape(9, 2 * nvar, ch), b1)
    lon_a = swap(lon_a, "lon", 0, True)
    lon_b = swap(lon_b, "lon", 1, True)

    hbm = pl.BlockSpec(memory_space=pltpu.HBM)
    g_pair = (lev, 2, cols, ch)
    st8_shape = (lev, rows, VG, WIDE)
    cut = (lev, rows * SIDE, ch)
    ps_shape = (lev, rows, 2 * VG, WIDE)
    own_shape = (lev, 2, VG, WIDE)
    halo_shape = (lev, 2 * REACH, VG, WIDE)
    shapes = [(g_pair, bf16), (g_pair, bf16), (cut, bf16), (cut, bf16), (st8_shape, f32), (own_shape, f32), (ps_shape, f32)]
    g_lo, g_hi, first, last, st8, own, ps = call(
        main_kernel,
        lev,
        [per_level(hidden_in.shape), var_level(state.shape), full(w1_pair.shape), full(w2_pair.shape), full((1, 2 * ch))],
        [sds(*x) for x in shapes],
        [per_level(x[0]) for x in shapes],
        [
            pltpu.VMEM((ch * (rows + VG), cols), f32),
            pltpu.VMEM((rows * (cols + SLOT), ch), f32),
            pltpu.VMEM((rows, cols, 3 * ch), bf16),
            pltpu.VMEM((rows + 2, cols, ch), bf16),
        ],
        (hidden_in, state, w1_pair, w2_pair, b1_pair),
        pl.CostEstimate(flops=2 * lev * rows * ext * 9 * ch * ch, bytes_accessed=8 * 2**20, transcendentals=0),
    )

    lat_wire = (lev, (rows + 2) * SIDE + 4 * VG, WIDE)
    pair_shape = (lev, 2, cols, ch)
    shapes = [(pair_shape, bf16), (halo_shape, f32), (lat_wire, bf16), (lat_wire, bf16)]
    each = levels()
    row_pair, halo, lat_a, lat_b = whole(
        pack_kernel,
        lev,
        [(flags, None)] + [(x, each) for x in (lon_a, lon_b, first, last, own)],
        [(sds(*x), each) for x in shapes],
        [pltpu.VMEM((nvar * REACH, WIDE), f32)],
        2**22,
        PACK_UNROLL,
    )
    lat_a = swap(lat_a, "lat", 0, False)
    lat_b = swap(lat_b, "lat", 1, False)

    block = EDGE_LEVELS
    pe_shape = (lev, 6, 2 * VG, WIDE)
    each = levels(block)
    (pe,) = whole(
        edge_kernel,
        lev // block,
        [(row_pair, each), (g_lo, each), (g_hi, each), (w1_one, None), (w2_one, None), (b1, None),
         (ps, levels(block, 0, 0, 4)), (ps, levels(block, 0, rows - 4, 4))],
        [(sds(pe_shape, f32), each)],
        [
            pltpu.VMEM((6 * block * (cols + SLOT), ch), f32),
            pltpu.VMEM((2 * block, cols, 9 * ch), bf16),
            pltpu.VMEM((2 * block * cols, ch), bf16),
        ],
        lev * 4 * ext * 9 * ch * ch,
    )

    block = SIDE_LEVELS
    parts = PARTS
    count = lev // parts
    wire = (count, 2 * VG * (REACH + 3), WIDE)
    pec_shape = (count,) + pe_shape[1:]
    pm4_shape = (count, 4, 2 * VG, WIDE)
    sst_shape = (count, 2, VG, WIDE)
    shapes = [(sst_shape, f32), (pm4_shape, f32), (pm4_shape, f32), (pec_shape, f32), (wire, bf16), (wire, bf16)]
    sent = []
    for part in range(parts):
        here = levels(block, part * count)
        each = levels(block)
        sst, pm, cm, pec, out_a, out_b = whole(
            side_kernel,
            count // block,
            [(flags, None)] + [(x, here) for x in (first, last, row_pair, lat_a, lat_b)]
            + [(x, None) for x in (w1_pair, w2_pair, w2_ends, b1_pair, keep)]
            + [(pe, here), (ps, levels(block, part * count, 0, 4)), (ps, levels(block, part * count, rows - 4, 4))],
            [(sds(*x), each) for x in shapes],
            [
                pltpu.VMEM((block, (rows + 2) * 2 * SLOT + 2 * SIDE, ch), f32),
                pltpu.VMEM((block, (rows + 2) * SLOT, 3 * ch), bf16),
                pltpu.VMEM((block, 2, (half + 1) * SLOT, ch), bf16),
                pltpu.VMEM((max(WIDE, block * 2 * SLOT), ch), bf16),
            ],
            count * 512 * 12 * ch * ch,
        )
        sent.append((pec, pm, cm, sst, swap(out_a, "lon", 0, True), swap(out_b, "lon", 1, True)))

    outs = [sds((2 * nvar, lev, rows, cols), f32), sds(state.shape, f32)]
    done = ()
    for part, (pec, pm, cm, sst, out_a, out_b) in enumerate(sent):
        off = part * count
        here, each = levels(1, off), levels()
        ins = [(flags, None), (ps, here)] + [(x, each) for x in (pec, pm, cm, out_a, out_b)]
        ins += [(st8, here), (halo, here), (sst, each), (own, here)] + [(x, None) for x in (b2, lat_main, lat_side)]

        def run(*refs, off=off, ins=ins, given=len(done)):
            sources = [functools.partial(v, r) if v else (lambda i, r=r: r) for (_, v), r in zip(ins, refs)]
            vel_hbm, ten_hbm, vel_ref, ten_ref, out_ref, sem = refs[len(ins) + given :]

            def copies(i):
                at, to = pl.ds(i, 1), pl.ds(off + i, 1)
                return [
                    pltpu.make_async_copy(src.at[:, at], dst.at[:, to], sem.at[i, k])
                    for k, (src, dst) in enumerate(((vel_ref, vel_hbm), (ten_ref, ten_hbm)))
                ]

            def one(i, carry):
                at = pl.ds(i, 1)
                advect_kernel(*[f(i) for f in sources], vel_ref.at[:, at], ten_ref.at[:, at], out_ref.at[i])
                for copy in copies(i):
                    copy.start()
                return carry

            lax.fori_loop(0, count, one, 0, unroll=ADVECT_UNROLL)
            for i in range(count):
                for copy in copies(i):
                    copy.wait()

        done = pl.pallas_call(
            run,
            in_specs=[smem if x is flags else vmem for x, _ in ins] + [hbm] * len(done),
            out_specs=[hbm] * 2,
            out_shape=outs,
            scratch_shapes=[
                pltpu.VMEM((2 * nvar, count, rows, cols), f32),
                pltpu.VMEM((nvar, count, rows, cols), f32),
                pltpu.VMEM((count, 2, rows * VG, WIDE), f32),
                pltpu.SemaphoreType.DMA((count, 2)),
            ],
            compiler_params=params,
            cost_estimate=pl.CostEstimate(flops=count * 2**24, bytes_accessed=2 * 2**20, transcendentals=0),
            input_output_aliases={len(ins): 0, len(ins) + 1: 1} if done else {},
        )(*[x for x, _ in ins], *done)
    return tuple(done)


def solution(mesh):
    placed = (P(None, None, "lon", "lat"), P(), P(), P(), P(), P(None, None, "lon", "lat"))
    return jax.shard_map(
        body,
        mesh=mesh,
        in_specs=placed,
        out_specs=(P(None, None, "lon", "lat"), P(None, None, "lon", "lat")),
        check_vma=False,
    )
```

```python
import functools
import math

import jax
import jax.numpy as jnp
from jax import lax
from jax.experimental import pallas as pl
from jax.experimental.pallas import tpu as pltpu
from jax.sharding import PartitionSpec as P

time_step = 0.5
speed_cap = 0.6
cos_floor = 0.5

SIDE = 8
SLOT = 2 * SIDE
SENT = 6
WIDE = 128
REACH = 4
VG = 8
VMEM_LIMIT = 24 * 2**20
ROWS_LIMIT = 50 * 2**20
EDGE_LEVELS = 8
ADVECT_UNROLL = 2
SIDE_LEVELS = 4
PARTS = 2
PACK_UNROLL = 4
f32 = jnp.float32
bf16 = jnp.bfloat16


def swap_pairs(count, first, closed):
    pairs = []
    for low in range(first, count, 2):
        high = low + 1
        if high >= count and not closed:
            continue
        pairs += [(low, high % count), (high % count, low)]
    return pairs


def swap(block, axis, first, closed):
    return lax.ppermute(block, axis, swap_pairs(lax.axis_size(axis), first, closed))


def place(row, rows):
    half, par = row // 2, row % 2
    own = 0 <= half < rows // 2
    return (0 if own else 2) + par, SLOT * (half % (rows // 2))


def lanes(shape):
    return lax.broadcasted_iota(jnp.int32, shape, len(shape) - 1)


def roll(x, by):
    by = by % WIDE
    return pltpu.roll(x, by, x.ndim - 1) if by else x


def col_before(mains, sides, at):
    lane = lanes(next(iter(mains.values())).shape)
    new_sides = {k: roll(s, 1) for k, s in sides.items()}
    new_mains = {}
    for row, main in mains.items():
        k, base = at(row)
        new_mains[row] = jnp.where(lane == 0, roll(sides[k], 1 - base - SIDE), roll(main, 1))
        new_sides[k] = jnp.where(lane == base + SIDE, roll(main, base + SIDE + 1), new_sides[k])
    return new_mains, new_sides


def col_after(mains, sides, at):
    lane = lanes(next(iter(mains.values())).shape)
    new_sides = {k: roll(s, -1) for k, s in sides.items()}
    new_mains = {}
    for row, main in mains.items():
        k, base = at(row)
        new_mains[row] = jnp.where(lane == WIDE - 1, roll(sides[k], WIDE - 1 - base - SIDE), roll(main, -1))
        new_sides[k] = jnp.where(lane == base + SIDE - 1, roll(main, base + SIDE - 1), new_sides[k])
    return new_mains, new_sides


def join_taps(x):
    return roll(x[0:SLOT], 1) + x[SLOT : 2 * SLOT] + roll(x[2 * SLOT : 3 * SLOT], -1)


def mix(first, second):
    return jnp.where(lanes(first.shape) % SLOT < SIDE, first, second)


def add_columns(main, side, base):
    lane = lanes(main.shape)
    return main + jnp.where((lane < SIDE) | (lane >= WIDE - SIDE), roll(side, -(base + SIDE)), 0.0)


def two_terms(x):
    first = x.astype(bf16)
    return [first, (x - first.astype(f32)).astype(bf16)]


def nt(lhs, rhs):
    return lax.dot_general(lhs, rhs, (((1,), (1,)), ((), ())), preferred_element_type=f32)


def silu(s):
    return s / (1.0 + jnp.exp(-s))


def shifted(e_ref, start, s_ref, to, count, first=0):
    ch = e_ref.shape[-1]
    for b in range(3):
        lane0 = first + b * ch
        s_ref[to, :, lane0 : lane0 + ch] = e_ref[pl.ds(start - 1 + b, count), :].astype(bf16)


def rows_kernel(flag_ref, x_hbm, st_hbm, outa_ref, outb_ref, x32_ref, x_ref, st_ref, sem):
    levels, ch, rows, cols = x_hbm.shape
    nvar = st_hbm.shape[0]
    size = nvar * REACH
    even = flag_ref[0] == 0

    def level_copy(lv):
        return pltpu.make_async_copy(x_hbm.at[lv], x_ref.at[lv], sem.at[lv])

    state_copy = pltpu.make_async_copy(st_hbm, st_ref, sem.at[levels])
    level_copy(0).start()
    state_copy.start()
    for lv in range(1, levels):
        level_copy(lv).start()
    state_copy.wait()

    def one(lv, carry):
        level_copy(lv).wait()
        x32_ref[...] = x_ref[lv].astype(f32).reshape(ch * rows, cols)
        lo, hi = (x32_ref[pl.ds(row, ch, stride=rows), :].astype(bf16) for row in (0, rows - 1))
        outa_ref[lv, 0:ch] = jnp.where(even, hi, lo)
        outb_ref[lv, 0:ch] = jnp.where(even, lo, hi)
        for n in range(nvar):
            x32_ref[n * REACH : (n + 1) * REACH] = st_ref[n, lv, 0:REACH]
            x32_ref[size + n * REACH : size + (n + 1) * REACH] = st_ref[n, lv, rows - REACH :]
        lo, hi = x32_ref[0:size], x32_ref[size : 2 * size]
        outa_ref[lv, ch:] = jnp.concatenate(two_terms(jnp.where(even, hi, lo)), axis=0)
        outb_ref[lv, ch:] = jnp.concatenate(two_terms(jnp.where(even, lo, hi)), axis=0)
        return carry

    lax.fori_loop(0, levels, one, 0)


def prep_kernel(flag_ref, n_lat, cols, b2_ref, w1_ref, w2_ref, b1_ref,
                w1p_ref, w2p_ref, w2o_ref, w2e_ref, b1p_ref, b2o_ref, lat_ref, lats_ref, keep_ref, w2s_ref):
    size, ch = w1_ref.shape
    nvar = w2_ref.shape[1] // 2
    w1p_ref[0:size, 0:ch] = w1_ref[...]
    w1p_ref[size:, 0:ch] = jnp.zeros((3 * ch, ch), bf16)
    w1p_ref[0 : 3 * ch, ch:] = jnp.zeros((3 * ch, ch), bf16)
    w1p_ref[3 * ch :, ch:] = w1_ref[...]
    b1p_ref[:, 0:ch] = b1_ref[...]
    b1p_ref[:, ch:] = b1_ref[...]
    w2p_ref[...] = jnp.zeros_like(w2p_ref)
    w2s_ref[0 : 2 * VG] = jnp.zeros((2 * VG, ch), f32)
    for a in range(3):
        for b in range(3):
            w2s_ref[2 * VG : 2 * VG + 2 * nvar] = w2_ref[3 * a + b].astype(f32)
            for part in range(2):
                w2s_ref[part * VG : part * VG + nvar] = w2s_ref[pl.ds(2 * VG + part, nvar, stride=2), :]
            here = w2s_ref[0 : 2 * VG].astype(bf16)
            at = 3 * a + b
            w2o_ref[at * SLOT : (at + 1) * SLOT] = here
            for k in range(2):
                first = (3 * k + b) * SLOT
                w2p_ref[first : first + SLOT, (a + k) * ch : (a + k + 1) * ch] = here
            if a != 1:
                first = (3 * (a // 2) + b) * SLOT
                w2e_ref[first : first + SLOT] = here
    b2o_ref[...] = jnp.zeros_like(b2o_ref)
    for v in range(2 * nvar):
        row = (v % 2) * VG + v // 2
        b2o_ref[row : row + 1] = jnp.full((1, WIDE), b2_ref[v], f32)

    def table(place_in):
        place_in = place_in + flag_ref[2] * cols
        keep = ((place_in >= 0) & (place_in < n_lat)).astype(f32)
        phi = (place_in.astype(f32) + 0.5) * (math.pi / n_lat) - 0.5 * math.pi
        cosine = jnp.maximum(jnp.cos(phi), cos_floor)
        return cosine, 1.0 / cosine, keep

    lane = lanes((VG, WIDE))
    slot = lane % SLOT
    beyond = jnp.where(slot < SIDE, slot - SIDE, cols + slot - SIDE)
    ends = jnp.where(slot < SIDE, cols - SIDE + slot, slot - SIDE)
    for ref, first, place_in in ((lat_ref, 0, lane), (lats_ref, 0, beyond), (lats_ref, 3, ends)):
        for k, x in enumerate(table(place_in)):
            ref[first + k] = x
    spot = lax.broadcasted_iota(jnp.int32, keep_ref.shape, 0)
    place_in = jnp.where(spot < SIDE, spot - SIDE + 1, cols - SIDE - 1 + spot) + flag_ref[2] * cols
    keep_ref[...] = ((place_in >= 0) & (place_in < n_lat)).astype(f32)


def main_kernel(x_ref, st_ref, w1_ref, w2_ref, b1_ref, glo_ref, ghi_ref, first_ref, last_ref, st8_ref, own_ref, ps_ref,
                x32_ref, e_ref, s_ref, h_ref):
    chans, rows, cols = x_ref.shape[1:]
    nvar = st_ref.shape[0]
    half = rows // 2
    pitch = cols + SLOT
    step = rows + VG
    x32_ref.reshape(chans, step, cols)[:, 0:rows] = x_ref[0].astype(f32)

    @pl.when(pl.program_id(0) == 0)
    def _():
        e_ref[...] = jnp.zeros_like(e_ref)
        h_ref[...] = jnp.zeros_like(h_ref)

    place_in = lax.broadcasted_iota(jnp.int32, (cols, 2 * chans), 0)
    within = (place_in > 0) & (place_in < cols - 1)

    def hidden_pair(m):
        lhs = jnp.concatenate([s_ref[2 * m + r] for r in range(4)], axis=1)
        acc = jnp.dot(lhs, w1_ref[...], preferred_element_type=f32) + b1_ref[...]
        hid = jnp.where(within, silu(acc), 0.0).astype(bf16)
        for k in range(2):
            h_ref[2 * m + 2 + k] = hid[:, k * chans : (k + 1) * chans]

    def sum_pair(m):
        q = nt(w2_ref[...], jnp.concatenate([h_ref[2 * m + r] for r in range(4)], axis=1))
        for k in range(2):
            ps_ref[0, 2 * m + k] = join_taps(q[k * 3 * SLOT : (k + 1) * 3 * SLOT])

    sides = [[], []]
    for row in range(rows):
        block = x32_ref[pl.ds(row, chans, stride=step), :].T
        start = row * pitch + SIDE
        e_ref[start : start + cols] = block
        for k, part in enumerate((block[0:SIDE], block[cols - SIDE :])):
            sides[k].append(part)
        if row < 2:
            glo_ref[0, row] = block.astype(bf16)
        if row >= rows - 2:
            ghi_ref[0, row - (rows - 2)] = block.astype(bf16)
        shifted(e_ref, start, s_ref, row, cols)
    first_ref[0] = jnp.concatenate(sides[0], axis=0).astype(bf16)
    last_ref[0] = jnp.concatenate(sides[1], axis=0).astype(bf16)
    for m in range(half - 1):
        hidden_pair(m)
    for m in range(half):
        sum_pair(m)
    for n in range(nvar):
        x32_ref[pl.ds(n, rows, stride=VG), :] = st_ref[n, 0]
    lane = lanes((VG, WIDE))
    own = [jnp.zeros((VG, WIDE), f32)] * 2
    for row in range(rows):
        block = x32_ref[row * VG : (row + 1) * VG]
        block = jnp.where(lax.broadcasted_iota(jnp.int32, (VG, WIDE), 0) < nvar, block, 0.0)
        st8_ref[0, row] = block
        par, base = place(row, rows)
        own[par] = jnp.where(lane // SLOT == base // SLOT, roll(block, base + SIDE), own[par])
    own_ref[0, 0], own_ref[0, 1] = own


def pack_kernel(flag_ref, a_ref, b_ref, first_ref, last_ref, own_ref, row_ref, halo_ref, outa_ref, outb_ref, w_ref, x_ref):
    cols = a_ref.shape[2]
    rows = first_ref.shape[1] // SIDE
    ch = row_ref.shape[3]
    size = (a_ref.shape[1] - ch) // 2
    nvar = size // REACH
    even = flag_ref[0] == 0
    lat_even = flag_ref[1] == 0
    got_a, got_b = a_ref[0].astype(f32), b_ref[0].astype(f32)
    low, high = jnp.where(even, got_b, got_a), jnp.where(even, got_a, got_b)
    halo_ref[...] = jnp.zeros_like(halo_ref)
    for k, x in enumerate((low, high)):
        x_ref[...] = x[ch : ch + size] + x[ch + size :]
        for r in range(REACH):
            halo_ref[0, k * REACH + r, 0:nvar] = x_ref[pl.ds(r, nvar, stride=REACH), :]
    low, high = low[0:ch].T, high[0:ch].T
    row_ref[0, 0] = low.astype(bf16)
    row_ref[0, 1] = high.astype(bf16)
    spot = lanes((VG, WIDE)) % SLOT
    near = (spot >= SIDE - REACH) & (spot < SIDE + REACH)
    terms = two_terms(jnp.where(near, own_ref[0, 0], roll(own_ref[0, 1], SIDE)))
    firsts = [low[0:SIDE]] + [first_ref[0, r * SIDE : (r + 1) * SIDE].astype(f32) for r in range(rows)] + [high[0:SIDE]]
    lasts = [low[cols - SIDE :]] + [last_ref[0, r * SIDE : (r + 1) * SIDE].astype(f32) for r in range(rows)]
    lasts += [high[cols - SIDE :]]
    for r in range(rows + 2):
        w_ref[0, 0, r * SENT : r * SENT + SIDE] = firsts[r]
    for r in reversed(range(rows + 2)):
        w_ref[0, 1, r * SENT : r * SENT + SIDE] = lasts[r]
    count = w_ref.shape[2]
    first, last = w_ref[0, 0].astype(bf16), w_ref[0, 1].astype(bf16)
    for out, pick in ((outa_ref, jnp.where(lat_even, last, first)), (outb_ref, jnp.where(lat_even, first, last))):
        out[0, 0:count] = pick
        out[0, count:] = jnp.concatenate(terms, axis=0)


def edge_kernel(row_ref, g0_ref, g1_ref, w1_ref, w2_ref, b1_ref, ps0_ref, ps1_ref, pe_ref, e_ref, s_ref, h_ref):
    levels = row_ref.shape[0]
    cols, ch = row_ref.shape[2:]
    pitch = cols + SLOT
    e_ref[...] = jnp.zeros_like(e_ref)
    for lv in range(levels):
        for k in range(2):
            part = [g0_ref[lv, 0], g0_ref[lv, 1]] if k == 0 else [g1_ref[lv, 0], g1_ref[lv, 1]]
            part = [row_ref[lv, 0]] + part if k == 0 else part + [row_ref[lv, 1]]
            for r in range(3):
                start = (6 * lv + 3 * k + r) * pitch + SIDE
                e_ref[start : start + cols] = part[r].astype(f32)
                shifted(e_ref, start, s_ref, 2 * lv + k, cols, 3 * ch * r)
    acc = jnp.dot(s_ref[...].reshape(2 * levels * cols, 9 * ch), w1_ref[...], preferred_element_type=f32) + b1_ref[...]
    place_in = lax.broadcasted_iota(jnp.int32, (cols, ch), 0)
    within = (place_in > 0) & (place_in < cols - 1)
    hid = silu(acc)
    for n in range(2 * levels):
        here = slice(n * cols, (n + 1) * cols)
        h_ref[here] = jnp.where(within, hid[here], 0.0).astype(bf16)
    q = nt(w2_ref[...], h_ref[...])
    for lv in range(levels):
        for k in range(2):
            here = slice((2 * lv + k) * cols, (2 * lv + k + 1) * cols)
            for a in range(3):
                x = join_taps(q[a * 3 * SLOT : (a + 1) * 3 * SLOT, here])
                if k == 0 and a < 2:
                    x = x + ps0_ref[lv, 1 - a]
                if k == 1 and a > 0:
                    x = x + ps1_ref[lv, 4 - a]
                pe_ref[lv, 3 * k + 2 - a] = x


def side_kernel(flag_ref, first_ref, last_ref, row_ref, la_ref, lb_ref, w1_ref, w2_ref, w2e_ref, b1_ref, keep_ref,
                pe_ref, ps0_ref, ps1_ref, sst_ref, pm_ref, cm_ref, pec_ref, outa_ref, outb_ref, e_ref, s_ref, hs_ref, z_ref, w_ref):
    levels = row_ref.shape[0]
    cols, ch = row_ref.shape[2:]
    rows = first_ref.shape[1] // SIDE
    half = rows // 2
    even = flag_ref[0] == 0
    lat_even = flag_ref[1] == 0
    wide = 2 * SLOT
    lane = lanes((2 * VG, WIDE))
    begin, end = lane < SLOT, lane >= WIDE - SLOT
    e_ref[...] = jnp.zeros_like(e_ref)
    hs_ref[...] = jnp.zeros_like(hs_ref)
    z_ref[...] = jnp.zeros_like(z_ref)
    for lv in range(levels):
        a, b = la_ref[lv], lb_ref[lv]
        right, left = jnp.where(lat_even, a, b), jnp.where(lat_even, b, a)
        count = la_ref.shape[1] - 2 * VG
        st = []
        for x in (left, right):
            x = x[count:].astype(f32)
            st.append(x[0:VG] + x[VG:])
        sst_ref[lv, 0] = mix(st[0], st[1])
        sst_ref[lv, 1] = mix(roll(st[0], -SIDE), roll(st[1], -SIDE))
        w_ref[lv, 0], w_ref[lv, 1] = left[0:count].astype(f32), right[0:count].astype(f32)
        first, last = first_ref[lv].astype(f32), last_ref[lv].astype(f32)
        low, high = row_ref[lv, 0].astype(f32), row_ref[lv, 1].astype(f32)
        for row in range(-1, rows + 1):
            far = [w_ref[lv, k, pl.ds((row + 1) * SENT, SIDE), :] for k in range(2)]
            if 0 <= row < rows:
                own = slice(row * SIDE, (row + 1) * SIDE)
                mine = first[own], last[own]
            else:
                x = low if row < 0 else high
                mine = x[0:SIDE], x[cols - SIDE :]
            start = SIDE + (row + 1) * wide
            for k, part in enumerate((far[0], mine[0], mine[1], far[1])):
                e_ref[lv, start + k * SIDE : start + (k + 1) * SIDE] = part
        for row in range(rows + 2):
            for b in range(3):
                start = SIDE + row * wide + b
                x = [e_ref[lv, pl.ds(start, SIDE), :], e_ref[lv, pl.ds(start + 3 * SIDE - 2, SIDE), :]]
                x = jnp.concatenate(x, axis=0).astype(bf16)
                s_ref[lv, row * SLOT : (row + 1) * SLOT, b * ch : (b + 1) * ch] = x
    s = s_ref[...].reshape(levels, half + 1, 2, SLOT, 3 * ch)
    part = [s[:, 0:half, 0], s[:, 0:half, 1], s[:, 1:, 0], s[:, 1:, 1]]
    lhs = jnp.concatenate([p.reshape(levels * half * SLOT, 3 * ch) for p in part], axis=1)
    acc = jnp.dot(lhs, w1_ref[...], preferred_element_type=f32) + b1_ref[...]
    hid = silu(acc).reshape(levels, half, SLOT, 2 * ch) * keep_ref[...]
    for lv in range(levels):
        for m in range(half):
            here = hid[lv, m].astype(bf16)
            hs_ref[lv, 0, m * SLOT : (m + 1) * SLOT] = here[:, 0:ch]
            hs_ref[lv, 1, (m + 1) * SLOT : (m + 2) * SLOT] = here[:, ch:]
            if m == 0:
                z_ref[2 * lv * SLOT : (2 * lv + 1) * SLOT] = here[:, 0:ch]
            if m == half - 1:
                z_ref[(2 * lv + 1) * SLOT : (2 * lv + 2) * SLOT] = here[:, ch:]
    size = half * SLOT
    rhs = []
    for lv in range(levels):
        odd, ev = hs_ref.at[lv, 1], hs_ref.at[lv, 0]
        rhs.append(jnp.concatenate([odd[0:size], ev[0:size], odd[SLOT : size + SLOT], ev[SLOT : size + SLOT]], axis=1))
    q_side = nt(w2_ref[...], jnp.concatenate(rhs, axis=0))
    q_ends = nt(w2e_ref[...], z_ref[...])
    in_left = lanes((SLOT, WIDE)) % SLOT < SIDE

    def join_sides(q):
        taps = [q[b * SLOT : (b + 1) * SLOT] for b in range(3)]
        l = [jnp.where(in_left, x, 0.0) for x in taps]
        r = [jnp.where(in_left, 0.0, x) for x in taps]
        l = roll(l[0], 2) + roll(l[1], 1) + l[2]
        r = r[0] + roll(r[1], -1) + roll(r[2], -2)
        return mix(l, r), mix(r, l)

    for lv in range(levels):
        out, inn = {}, {}
        q = q_side[:, lv * size : (lv + 1) * size]
        for k in range(2):
            out[k], inn[k] = join_sides(q[k * 3 * SLOT : (k + 1) * 3 * SLOT])
        per = WIDE // (2 * SLOT)
        q = roll(q_ends[:, (lv // per) * WIDE : (lv // per + 1) * WIDE], -(lv % per) * 2 * SLOT)
        prev = join_sides(q[3 * SLOT : 6 * SLOT])
        nxt = join_sides(q[0 : 3 * SLOT])
        for k, x, spot, by in ((3, prev, end, WIDE - SLOT), (2, nxt, begin, -SLOT)):
            out[k], inn[k] = (jnp.where(spot, roll(y, by), 0.0) for y in x)
        for k in range(4):
            pm_ref[lv, k] = out[k]
            cm_ref[lv, k] = inn[k]
        mains = {}
        for k, row in enumerate((-1, 0, 1, rows - 2, rows - 1, rows)):
            mains[row] = pe_ref[lv, k]
        mains[2], mains[3] = ps0_ref[lv, 2], ps0_ref[lv, 3]
        mains[rows - 4], mains[rows - 3] = ps1_ref[lv, 0], ps1_ref[lv, 1]
        for row in mains:
            k, base = place(row, rows)
            mains[row] = add_columns(mains[row], inn[k], base)
        for k, row in enumerate((-1, 0, 1, rows - 2, rows - 1, rows)):
            pec_ref[lv, k] = mains[row]
        lane8 = lanes((VG, WIDE))
        st = sst_ref[lv, 0], sst_ref[lv, 1]

        def terms_of(x, here):
            first = x.astype(bf16).astype(f32)
            return jnp.where(here, first, roll(x - first, WIDE // 2))

        st_lo = terms_of(jnp.where(lane8 < 2 * SLOT, st[0], roll(st[1], 2 * SLOT)), lane8 < WIDE // 2)
        st_hi = terms_of(jnp.where(lane8 >= WIDE - 2 * SLOT, st[0], roll(st[1], -2 * SLOT)), lane8 >= WIDE // 2)
        side_lo = jnp.where(lane < 2 * SLOT, out[0], jnp.where(lane < 4 * SLOT, roll(out[1], 2 * SLOT), out[3]))
        side_hi = jnp.where(lane >= WIDE - 2 * SLOT, out[0],
                            jnp.where(lane >= WIDE - 4 * SLOT, roll(out[1], -2 * SLOT), out[2]))
        out_lo = jnp.concatenate([mains[k - 1] for k in range(4)] + [side_lo, mains[3][0:VG], st_lo], axis=0)
        out_hi = jnp.concatenate([mains[rows - k] for k in range(4)] + [side_hi, mains[rows - 4][0:VG], st_hi], axis=0)
        outa_ref[lv] = jnp.where(even, out_hi, out_lo).astype(bf16)
        outb_ref[lv] = jnp.where(even, out_lo, out_hi).astype(bf16)


def advect_kernel(flag_ref, ps_ref, pe_ref, pm_ref, cm_ref, a_ref, b_ref, st8_ref, halo_ref, sst_ref, own_ref,
                  b2_ref, lat_ref, lats_ref, *rest):
    vel_ref, ten_ref, out_ref = rest[-3:]
    rows = st8_ref.shape[1]
    nvar = ten_ref.shape[0]
    even = flag_ref[0] == 0
    lane16 = lanes((2 * VG, WIDE))
    lane = lanes((VG, WIDE))
    pair = 2 * VG

    def halos(xa, xb):
        return jnp.where(even, xb, xa), jnp.where(even, xa, xb)

    lo, hi = halos(a_ref[0].astype(f32), b_ref[0].astype(f32))
    main = {}
    for row in range(2, rows - 2):
        k, base = place(row, rows)
        main[row] = add_columns(ps_ref[0, row], cm_ref[0, k], base)
    for k, row in enumerate((-1, 0, 1, rows - 2, rows - 1, rows)):
        main[row] = pe_ref[0, k]
    for k in range(REACH + 1):
        there = slice(k * pair, (k + 1) * pair) if k < REACH else slice((k + 1) * pair, (k + 2) * pair)
        for got, row in ((lo, -k), (hi, rows - 1 + k)):
            main[row] = main[row] + got[there] if row in main else got[there]
    slo, shi = (got[REACH * pair : (REACH + 1) * pair] for got in (lo, hi))
    zero = jnp.zeros((pair, WIDE), f32)
    last, front = lane16 >= WIDE - 2 * SLOT, lane16 < 2 * SLOT
    side = {
        0: pm_ref[0, 0] + jnp.where(lane16 < SLOT, slo, zero),
        1: pm_ref[0, 1] + jnp.where(lane16 >= WIDE - SLOT, shi, zero),
        2: pm_ref[0, 2] + jnp.where(last, slo, jnp.where(front, shi, zero)),
        3: pm_ref[0, 3] + jnp.where(last, roll(slo, 2 * SLOT), jnp.where(front, roll(shi, -2 * SLOT), zero)),
    }
    bias = b2_ref[...]
    main = {r: speed_cap * jnp.tanh(x + bias) for r, x in main.items()}
    side = {k: speed_cap * jnp.tanh(x + bias) * lats_ref[2, 0:1] for k, x in side.items()}
    for part in range(2):
        for row in range(rows):
            out_ref[part, row * VG : (row + 1) * VG] = main[row][part * VG : (part + 1) * VG]
        for n in range(nvar):
            vel_ref[2 * n + part, 0] = out_ref[part, pl.ds(n, rows, stride=VG), :]

    q0 = {row: st8_ref[0, row] for row in range(rows)}
    for k in range(REACH):
        q0[k - REACH], q0[rows + k] = halo_ref[0, k], halo_ref[0, REACH + k]
    hlo, hhi = (x[(REACH + 1) * pair + VG :] for x in (lo, hi))
    hlo, hhi = hlo + roll(hlo, WIDE // 2), hhi + roll(hhi, WIDE // 2)
    last, front = lane >= WIDE - 2 * SLOT, lane < 2 * SLOT
    nil = jnp.zeros((VG, WIDE), f32)
    out_q = {
        0: sst_ref[0, 0],
        1: sst_ref[0, 1],
        2: jnp.where(last, hlo, jnp.where(front, hhi, nil)),
        3: jnp.where(last, roll(hlo, 2 * SLOT), jnp.where(front, roll(hhi, -2 * SLOT), nil)),
    }
    own_q = {0: own_ref[0, 0], 1: own_ref[0, 1], 2: nil, 3: nil}
    for row in list(range(-REACH, 0)) + list(range(rows, rows + REACH)):
        k, base = place(row, rows)
        own_q[k] = jnp.where(lane // SLOT == base // SLOT, roll(q0[row], base + SIDE), own_q[k])

    everywhere = range(-REACH, rows + REACH)
    own = {k: jnp.zeros((pair, WIDE), f32) for k in range(4)}
    for row in everywhere:
        k, base = place(row, rows)
        own[k] = jnp.where(lane16 // SLOT == base // SLOT, roll(main[row], base + SIDE), own[k])

    def tiles(out, inner):
        return {**{k: mix(out[k], inner[k]) for k in range(4)}, **{4 + k: mix(inner[k], out[k]) for k in range(4)}}

    s0 = tiles(out_q, own_q)
    vel_s = tiles(side, own)

    def tile_rows(s):
        def turned(own, halo, by, first):
            own, halo = roll(own, by), roll(halo, by)
            return jnp.where(first, halo, own), jnp.where(first, own, halo)

        before, after = {}, {}
        for t in (0, 4):
            before[t + 1], before[t + 3], after[t], after[t + 2] = s[t], s[t + 2], s[t + 1], s[t + 3]
            before[t], before[t + 2] = turned(s[t + 1], s[t + 3], SLOT, lane < SLOT)
            after[t + 1], after[t + 3] = turned(s[t], s[t + 2], -SLOT, lane >= WIDE - SLOT)
        return before, after

    u = {r: x[0:VG] for r, x in main.items()}
    us = {k: x[0:VG] for k, x in vel_s.items()}
    inside = range(1 - REACH, rows + REACH - 1)
    v = {r: main[r][VG:] for r in inside}
    vs = {k: x[VG:] for k, x in vel_s.items()}
    cosine, metric = lat_ref[0], lat_ref[1]

    def side_table(n, k):
        return mix(lats_ref[n], lats_ref[n + 3]) if k < 4 else mix(lats_ref[n + 3], lats_ref[n])

    cosine_s, metric_s = ([side_table(n, k) for k in range(8)] for n in range(2))
    flux = {r: x * cosine for r, x in v.items()}
    flux_s = {k: x * cosine_s[k] for k, x in vs.items()}
    ub, ua = tile_rows(us)

    def coefs(m, uu, vv, udiff, vdiff):
        flow = m * uu
        cl = jnp.maximum(flow, 0.0)
        cr = cl - flow
        cd = jnp.maximum(vv, 0.0)
        cu = cd - vv
        div = (0.5 * m) * (udiff + vdiff)
        return -((cl + cr) + (cd + cu) + div), cl, cr, cd, cu

    cm = {r: coefs(metric, u[r], v[r], u[r + 1] - u[r - 1], roll(flux[r], -1) - roll(flux[r], 1)) for r in inside}
    cs = {k: coefs(metric_s[k], us[k], vs[k], ua[k] - ub[k], roll(flux_s[k], -1) - roll(flux_s[k], 1)) for k in range(8)}

    def stencil(c, x, left, right):
        return c[0] * x + c[1] * left + c[2] * right + c[3] * roll(x, 1) + c[4] * roll(x, -1)

    def rate(q, s, depth):
        rb, ra = tile_rows(s)
        inner = range(depth - REACH, rows + REACH - depth)
        wanted = [k for k in range(8) if depth < REACH or k % 4 < 2]
        return ({r: stencil(cm[r], q[r], q[r - 1], q[r + 1]) for r in inner},
                {k: stencil(cs[k], s[k], rb[k], ra[k]) for k in wanted})

    def moved(rates, by):
        return {r: q0[r] + by * x for r, x in rates[0].items()}, {k: s0[k] + by * x for k, x in rates[1].items()}

    one = rate(q0, s0, 1)
    two = rate(*moved(one, 0.5 * time_step), 2)
    three = rate(*moved(two, 0.5 * time_step), 3)
    four = rate(*moved(three, time_step), 4)

    def mean(n, k):
        return (one[n][k] + four[n][k] + 2.0 * (two[n][k] + three[n][k])) * (1.0 / 6.0)

    ends = {k: mix(mean(1, 4 + k), mean(1, k)) for k in range(2)}
    for row in range(rows):
        k, base = place(row, rows)
        at_end = (lane < REACH) | (lane >= WIDE - REACH)
        out_ref[0, row * VG : (row + 1) * VG] = jnp.where(at_end, roll(ends[k], -(base + SIDE)), mean(0, row))
    for n in range(nvar):
        ten_ref[n, 0] = out_ref[0, pl.ds(n, rows, stride=VG), :]


def full(shape):
    return pl.BlockSpec(shape, lambda *i: (0,) * len(shape))


def per_level(shape):
    return pl.BlockSpec((1,) + shape[1:], lambda i: (i,) + (0,) * (len(shape) - 1))


def level_part(shape, index, block=1, offset=0):
    return pl.BlockSpec((block,) + shape, lambda i: (i + offset, index) + (0,) * (len(shape) - 1))


def levels_of(shape, block=1, offset=0):
    return pl.BlockSpec((block,) + shape[1:], lambda i: (i + offset,) + (0,) * (len(shape) - 1))


def var_level(shape, offset=0):
    return pl.BlockSpec((shape[0], 1) + shape[2:], lambda i: (0, i + offset, 0, 0))


def body(hidden_in, w_conv1, b_conv1, w_conv2, b_conv2, state):
    lev, ch, rows, cols = hidden_in.shape
    nvar = state.shape[0]
    ext = cols + SLOT
    half = rows // 2
    params = pltpu.CompilerParams(vmem_limit_bytes=VMEM_LIMIT)
    smem = pl.BlockSpec(memory_space=pltpu.SMEM)
    sds = jax.ShapeDtypeStruct

    def call(kernel, steps, ins, outs, out_specs, scratch, args, cost=None, aliases={}):
        return pl.pallas_call(
            kernel,
            grid=(steps,),
            in_specs=ins,
            out_specs=out_specs,
            out_shape=outs,
            scratch_shapes=scratch,
            compiler_params=params,
            cost_estimate=cost,
            input_output_aliases=aliases,
        )(*args)

    vmem = pl.BlockSpec(memory_space=pltpu.VMEM)

    def levels(block=1, off=0, first=None, size=None):
        def view(ref, i):
            here = pl.ds(off + i * block, block)
            return ref.at[here] if first is None else ref.at[here, first : first + size]

        return view

    def whole(kernel, steps, ins, outs, scratch, cost, unroll=1, scratch_views=()):
        views = [v for _, v in ins] + [v for _, v in outs] + list(scratch_views)

        def run(*refs):
            def one(i, carry):
                kernel(*[v(r, i) if v else r for v, r in zip(views, refs)], *refs[len(views) :])
                return carry

            if steps == 1:
                one(0, 0)
            else:
                lax.fori_loop(0, steps, one, 0, unroll=unroll)

        return pl.pallas_call(
            run,
            in_specs=[smem if x is flags else vmem for x, _ in ins],
            out_specs=[vmem] * len(outs),
            out_shape=[x for x, _ in outs],
            scratch_shapes=scratch,
            compiler_params=params,
            cost_estimate=pl.CostEstimate(flops=cost, bytes_accessed=2**20, transcendentals=0),
        )(*[x for x, _ in ins])

    flags = jnp.stack([lax.axis_index("lon") % 2, lax.axis_index("lat") % 2, lax.axis_index("lat")]).astype(jnp.int32)
    lon_wire = (lev, ch + 2 * nvar * REACH, cols)
    lon_a, lon_b = pl.pallas_call(
        rows_kernel,
        in_specs=[smem] + [pl.BlockSpec(memory_space=pltpu.HBM)] * 2,
        out_specs=[vmem] * 2,
        out_shape=[sds(lon_wire, bf16)] * 2,
        scratch_shapes=[
            pltpu.VMEM((ch * rows, cols), f32),
            pltpu.VMEM(hidden_in.shape, bf16),
            pltpu.VMEM(state.shape, f32),
            pltpu.SemaphoreType.DMA((lev + 1,)),
        ],
        compiler_params=pltpu.CompilerParams(vmem_limit_bytes=ROWS_LIMIT),
    )(flags, hidden_in, state)
    shapes = [((12 * ch, 2 * ch), bf16), ((6 * SLOT, 4 * ch), bf16), ((9 * SLOT, ch), bf16),
              ((6 * SLOT, ch), bf16), ((1, 2 * ch), f32), ((2 * VG, WIDE), f32), ((3, VG, WIDE), f32), ((6, VG, WIDE), f32),
              ((SLOT, 2 * ch), f32)]
    w1_one = w_conv1.reshape(9 * ch, ch)
    b1 = b_conv1.reshape(1, ch)
    n_lat = cols * lax.axis_size("lat")
    w1_pair, w2_pair, w2_one, w2_ends, b1_pair, b2, lat_main, lat_side, keep = pl.pallas_call(
        lambda flag_ref, *refs: prep_kernel(flag_ref, n_lat, cols, *refs),
        in_specs=[smem, smem] + [vmem] * 3,
        out_specs=[vmem] * len(shapes),
        out_shape=[sds(*x) for x in shapes],
        scratch_shapes=[pltpu.VMEM((4 * VG, ch), f32)],
        compiler_params=params,
    )(flags, b_conv2, w1_one, w_conv2.transpose(0, 1, 3, 2).reshape(9, 2 * nvar, ch), b1)
    lon_a = swap(lon_a, "lon", 0, True)
    lon_b = swap(lon_b, "lon", 1, True)

    hbm = pl.BlockSpec(memory_space=pltpu.HBM)
    g_pair = (lev, 2, cols, ch)
    st8_shape = (lev, rows, VG, WIDE)
    cut = (lev, rows * SIDE, ch)
    ps_shape = (lev, rows, 2 * VG, WIDE)
    own_shape = (lev, 2, VG, WIDE)
    halo_shape = (lev, 2 * REACH, VG, WIDE)
    shapes = [(g_pair, bf16), (g_pair, bf16), (cut, bf16), (cut, bf16), (st8_shape, f32), (own_shape, f32), (ps_shape, f32)]
    g_lo, g_hi, first, last, st8, own, ps = call(
        main_kernel,
        lev,
        [per_level(hidden_in.shape), var_level(state.shape), full(w1_pair.shape), full(w2_pair.shape), full((1, 2 * ch))],
        [sds(*x) for x in shapes],
        [per_level(x[0]) for x in shapes],
        [
            pltpu.VMEM((ch * (rows + VG), cols), f32),
            pltpu.VMEM((rows * (cols + SLOT), ch), f32),
            pltpu.VMEM((rows, cols, 3 * ch), bf16),
            pltpu.VMEM((rows + 2, cols, ch), bf16),
        ],
        (hidden_in, state, w1_pair, w2_pair, b1_pair),
        pl.CostEstimate(flops=2 * lev * rows * ext * 9 * ch * ch, bytes_accessed=8 * 2**20, transcendentals=0),
    )

    sent_rows = -(-((rows + 1) * SENT + SIDE) // SLOT) * SLOT
    lat_wire = (lev, sent_rows + 2 * VG, WIDE)
    pair_shape = (lev, 2, cols, ch)
    shapes = [(pair_shape, bf16), (halo_shape, f32), (lat_wire, bf16), (lat_wire, bf16)]
    each = levels()
    row_pair, halo, lat_a, lat_b = whole(
        pack_kernel,
        lev,
        [(flags, None)] + [(x, each) for x in (lon_a, lon_b, first, last, own)],
        [(sds(*x), each) for x in shapes],
        [pltpu.VMEM((lev, 2, sent_rows, ch), f32), pltpu.VMEM((nvar * REACH, WIDE), f32)],
        2**22,
        PACK_UNROLL,
        [each],
    )
    lat_a = swap(lat_a, "lat", 0, False)
    lat_b = swap(lat_b, "lat", 1, False)

    block = EDGE_LEVELS
    pe_shape = (lev, 6, 2 * VG, WIDE)
    each = levels(block)
    (pe,) = whole(
        edge_kernel,
        lev // block,
        [(row_pair, each), (g_lo, each), (g_hi, each), (w1_one, None), (w2_one, None), (b1, None),
         (ps, levels(block, 0, 0, 4)), (ps, levels(block, 0, rows - 4, 4))],
        [(sds(pe_shape, f32), each)],
        [
            pltpu.VMEM((6 * block * (cols + SLOT), ch), f32),
            pltpu.VMEM((2 * block, cols, 9 * ch), bf16),
            pltpu.VMEM((2 * block * cols, ch), bf16),
        ],
        lev * 4 * ext * 9 * ch * ch,
    )

    block = SIDE_LEVELS
    parts = PARTS
    count = lev // parts
    wire = (count, 2 * VG * (REACH + 2), WIDE)
    pec_shape = (count,) + pe_shape[1:]
    pm4_shape = (count, 4, 2 * VG, WIDE)
    sst_shape = (count, 2, VG, WIDE)
    shapes = [(sst_shape, f32), (pm4_shape, f32), (pm4_shape, f32), (pec_shape, f32), (wire, bf16), (wire, bf16)]
    sent = []
    for part in range(parts):
        here = levels(block, part * count)
        each = levels(block)
        sst, pm, cm, pec, out_a, out_b = whole(
            side_kernel,
            count // block,
            [(flags, None)] + [(x, here) for x in (first, last, row_pair, lat_a, lat_b)]
            + [(x, None) for x in (w1_pair, w2_pair, w2_ends, b1_pair, keep)]
            + [(pe, here), (ps, levels(block, part * count, 0, 4)), (ps, levels(block, part * count, rows - 4, 4))],
            [(sds(*x), each) for x in shapes],
            [
                pltpu.VMEM((block, (rows + 2) * 2 * SLOT + 2 * SIDE, ch), f32),
                pltpu.VMEM((block, (rows + 2) * SLOT, 3 * ch), bf16),
                pltpu.VMEM((block, 2, (half + 1) * SLOT, ch), bf16),
                pltpu.VMEM((max(WIDE, block * 2 * SLOT), ch), bf16),
                pltpu.VMEM((block, 2, sent_rows, ch), f32),
            ],
            count * 512 * 12 * ch * ch,
        )
        sent.append((pec, pm, cm, sst, swap(out_a, "lon", 0, True), swap(out_b, "lon", 1, True)))

    outs = [sds((2 * nvar, lev, rows, cols), f32), sds(state.shape, f32)]
    done = ()
    for part, (pec, pm, cm, sst, out_a, out_b) in enumerate(sent):
        off = part * count
        here, each = levels(1, off), levels()
        ins = [(flags, None), (ps, here)] + [(x, each) for x in (pec, pm, cm, out_a, out_b)]
        ins += [(st8, here), (halo, here), (sst, each), (own, here)] + [(x, None) for x in (b2, lat_main, lat_side)]

        def run(*refs, off=off, ins=ins, given=len(done)):
            sources = [functools.partial(v, r) if v else (lambda i, r=r: r) for (_, v), r in zip(ins, refs)]
            vel_hbm, ten_hbm, vel_ref, ten_ref, out_ref, sem = refs[len(ins) + given :]

            def copies(i):
                at, to = pl.ds(i, 1), pl.ds(off + i, 1)
                return [
                    pltpu.make_async_copy(src.at[:, at], dst.at[:, to], sem.at[i, k])
                    for k, (src, dst) in enumerate(((vel_ref, vel_hbm), (ten_ref, ten_hbm)))
                ]

            def one(i, carry):
                at = pl.ds(i, 1)
                advect_kernel(*[f(i) for f in sources], vel_ref.at[:, at], ten_ref.at[:, at], out_ref.at[i])
                for copy in copies(i):
                    copy.start()
                return carry

            lax.fori_loop(0, count, one, 0, unroll=ADVECT_UNROLL)
            for i in range(count):
                for copy in copies(i):
                    copy.wait()

        done = pl.pallas_call(
            run,
            in_specs=[smem if x is flags else vmem for x, _ in ins] + [hbm] * len(done),
            out_specs=[hbm] * 2,
            out_shape=outs,
            scratch_shapes=[
                pltpu.VMEM((2 * nvar, count, rows, cols), f32),
                pltpu.VMEM((nvar, count, rows, cols), f32),
                pltpu.VMEM((count, 2, rows * VG, WIDE), f32),
                pltpu.SemaphoreType.DMA((count, 2)),
            ],
            compiler_params=params,
            cost_estimate=pl.CostEstimate(flops=count * 2**24, bytes_accessed=2 * 2**20, transcendentals=0),
            input_output_aliases={len(ins): 0, len(ins) + 1: 1} if done else {},
        )(*[x for x, _ in ins], *done)
    return tuple(done)


def solution(mesh):
    placed = (P(None, None, "lon", "lat"), P(), P(), P(), P(), P(None, None, "lon", "lat"))
    return jax.shard_map(
        body,
        mesh=mesh,
        in_specs=placed,
        out_specs=(P(None, None, "lon", "lat"), P(None, None, "lon", "lat")),
        check_vma=False,
    )
```

```python
import functools
import math

import jax
import jax.numpy as jnp
from jax import lax
from jax.experimental import pallas as pl
from jax.experimental.pallas import tpu as pltpu
from jax.sharding import PartitionSpec as P

time_step = 0.5
speed_cap = 0.6
cos_floor = 0.5

SIDE = 8
SLOT = 2 * SIDE
SENT = 6
FINE = 32
WIDE = 128
REACH = 4
VG = 8
VMEM_LIMIT = 24 * 2**20
ROWS_LIMIT = 50 * 2**20
EDGE_LEVELS = 8
ADVECT_UNROLL = 2
SIDE_LEVELS = 4
PARTS = 2
PACK_UNROLL = 4
f32 = jnp.float32
bf16 = jnp.bfloat16


def swap_pairs(count, first, closed):
    pairs = []
    for low in range(first, count, 2):
        high = low + 1
        if high >= count and not closed:
            continue
        pairs += [(low, high % count), (high % count, low)]
    return pairs


def swap(block, axis, first, closed):
    return lax.ppermute(block, axis, swap_pairs(lax.axis_size(axis), first, closed))


def place(row, rows):
    half, par = row // 2, row % 2
    own = 0 <= half < rows // 2
    return (0 if own else 2) + par, SLOT * (half % (rows // 2))


def lanes(shape):
    return lax.broadcasted_iota(jnp.int32, shape, len(shape) - 1)


def roll(x, by):
    by = by % WIDE
    return pltpu.roll(x, by, x.ndim - 1) if by else x


def col_before(mains, sides, at):
    lane = lanes(next(iter(mains.values())).shape)
    new_sides = {k: roll(s, 1) for k, s in sides.items()}
    new_mains = {}
    for row, main in mains.items():
        k, base = at(row)
        new_mains[row] = jnp.where(lane == 0, roll(sides[k], 1 - base - SIDE), roll(main, 1))
        new_sides[k] = jnp.where(lane == base + SIDE, roll(main, base + SIDE + 1), new_sides[k])
    return new_mains, new_sides


def col_after(mains, sides, at):
    lane = lanes(next(iter(mains.values())).shape)
    new_sides = {k: roll(s, -1) for k, s in sides.items()}
    new_mains = {}
    for row, main in mains.items():
        k, base = at(row)
        new_mains[row] = jnp.where(lane == WIDE - 1, roll(sides[k], WIDE - 1 - base - SIDE), roll(main, -1))
        new_sides[k] = jnp.where(lane == base + SIDE - 1, roll(main, base + SIDE - 1), new_sides[k])
    return new_mains, new_sides


def join_taps(x):
    return roll(x[0:SLOT], 1) + x[SLOT : 2 * SLOT] + roll(x[2 * SLOT : 3 * SLOT], -1)


def mix(first, second):
    return jnp.where(lanes(first.shape) % SLOT < SIDE, first, second)


def add_columns(main, side, base):
    lane = lanes(main.shape)
    return main + jnp.where((lane < SIDE) | (lane >= WIDE - SIDE), roll(side, -(base + SIDE)), 0.0)


def two_terms(x):
    first = x.astype(bf16)
    return [first, (x - first.astype(f32)).astype(bf16)]


def nt(lhs, rhs):
    return lax.dot_general(lhs, rhs, (((1,), (1,)), ((), ())), preferred_element_type=f32)


def silu(s):
    return s / (1.0 + jnp.exp(-s))


def shifted(e_ref, start, s_ref, to, count, first=0):
    ch = e_ref.shape[-1]
    for b in range(3):
        lane0 = first + b * ch
        s_ref[to, :, lane0 : lane0 + ch] = e_ref[pl.ds(start - 1 + b, count), :].astype(bf16)


def rows_kernel(flag_ref, x_hbm, st_hbm, outa_ref, outb_ref, x32_ref, x_ref, st_ref, sem):
    levels, ch, rows, cols = x_hbm.shape
    nvar = st_hbm.shape[0]
    size = nvar * REACH
    even = flag_ref[0] == 0

    def level_copy(lv):
        return pltpu.make_async_copy(x_hbm.at[lv], x_ref.at[lv], sem.at[lv])

    state_copy = pltpu.make_async_copy(st_hbm, st_ref, sem.at[levels])
    level_copy(0).start()
    state_copy.start()
    for lv in range(1, levels):
        level_copy(lv).start()
    state_copy.wait()

    def one(lv, carry):
        level_copy(lv).wait()
        x32_ref[...] = x_ref[lv].astype(f32).reshape(ch * rows, cols)
        lo, hi = (x32_ref[pl.ds(row, ch, stride=rows), :].astype(bf16) for row in (0, rows - 1))
        outa_ref[lv, 0:ch] = jnp.where(even, hi, lo)
        outb_ref[lv, 0:ch] = jnp.where(even, lo, hi)
        for n in range(nvar):
            x32_ref[n * REACH : (n + 1) * REACH] = st_ref[n, lv, 0:REACH]
            x32_ref[size + n * REACH : size + (n + 1) * REACH] = st_ref[n, lv, rows - REACH :]
        lo, hi = x32_ref[0:size], x32_ref[size : 2 * size]
        outa_ref[lv, ch:] = jnp.concatenate(two_terms(jnp.where(even, hi, lo)), axis=0)
        outb_ref[lv, ch:] = jnp.concatenate(two_terms(jnp.where(even, lo, hi)), axis=0)
        return carry

    lax.fori_loop(0, levels, one, 0)


def prep_kernel(flag_ref, n_lat, cols, b2_ref, w1_ref, w2_ref, b1_ref,
                w1p_ref, w2p_ref, w2o_ref, w2e_ref, b1p_ref, b2o_ref, lat_ref, lats_ref, keep_ref, w2s_ref):
    size, ch = w1_ref.shape
    nvar = w2_ref.shape[1] // 2
    w1p_ref[0:size, 0:ch] = w1_ref[...]
    w1p_ref[size:, 0:ch] = jnp.zeros((3 * ch, ch), bf16)
    w1p_ref[0 : 3 * ch, ch:] = jnp.zeros((3 * ch, ch), bf16)
    w1p_ref[3 * ch :, ch:] = w1_ref[...]
    b1p_ref[:, 0:ch] = b1_ref[...]
    b1p_ref[:, ch:] = b1_ref[...]
    w2p_ref[...] = jnp.zeros_like(w2p_ref)
    w2s_ref[0 : 2 * VG] = jnp.zeros((2 * VG, ch), f32)
    for a in range(3):
        for b in range(3):
            w2s_ref[2 * VG : 2 * VG + 2 * nvar] = w2_ref[3 * a + b].astype(f32)
            for part in range(2):
                w2s_ref[part * VG : part * VG + nvar] = w2s_ref[pl.ds(2 * VG + part, nvar, stride=2), :]
            here = w2s_ref[0 : 2 * VG].astype(bf16)
            at = 3 * a + b
            w2o_ref[at * SLOT : (at + 1) * SLOT] = here
            for k in range(2):
                first = (3 * k + b) * SLOT
                w2p_ref[first : first + SLOT, (a + k) * ch : (a + k + 1) * ch] = here
            if a != 1:
                first = (3 * (a // 2) + b) * SLOT
                w2e_ref[first : first + SLOT] = here
    b2o_ref[...] = jnp.zeros_like(b2o_ref)
    for v in range(2 * nvar):
        row = (v % 2) * VG + v // 2
        b2o_ref[row : row + 1] = jnp.full((1, WIDE), b2_ref[v], f32)

    def table(place_in):
        place_in = place_in + flag_ref[2] * cols
        keep = ((place_in >= 0) & (place_in < n_lat)).astype(f32)
        phi = (place_in.astype(f32) + 0.5) * (math.pi / n_lat) - 0.5 * math.pi
        cosine = jnp.maximum(jnp.cos(phi), cos_floor)
        return cosine, 1.0 / cosine, keep

    lane = lanes((VG, WIDE))
    slot = lane % SLOT
    beyond = jnp.where(slot < SIDE, slot - SIDE, cols + slot - SIDE)
    ends = jnp.where(slot < SIDE, cols - SIDE + slot, slot - SIDE)
    for ref, first, place_in in ((lat_ref, 0, lane), (lats_ref, 0, beyond), (lats_ref, 3, ends)):
        for k, x in enumerate(table(place_in)):
            ref[first + k] = x
    spot = lax.broadcasted_iota(jnp.int32, keep_ref.shape, 0)
    place_in = jnp.where(spot < SIDE, spot - SIDE + 1, cols - SIDE - 1 + spot) + flag_ref[2] * cols
    keep_ref[...] = ((place_in >= 0) & (place_in < n_lat)).astype(f32)


def main_kernel(x_ref, st_ref, w1_ref, w2_ref, b1_ref, glo_ref, ghi_ref, first_ref, last_ref, st8_ref, own_ref, ps_ref,
                x32_ref, e_ref, s_ref, h_ref):
    chans, rows, cols = x_ref.shape[1:]
    nvar = st_ref.shape[0]
    half = rows // 2
    pitch = cols + SLOT
    step = rows + VG
    x32_ref.reshape(chans, step, cols)[:, 0:rows] = x_ref[0].astype(f32)

    place_in = lax.broadcasted_iota(jnp.int32, (cols, 2 * chans), 0)
    within = (place_in > 0) & (place_in < cols - 1)

    def hidden_pair(m):
        lhs = jnp.concatenate([s_ref[2 * m + r] for r in range(4)], axis=1)
        acc = jnp.dot(lhs, w1_ref[...], preferred_element_type=f32) + b1_ref[...]
        hid = jnp.where(within, silu(acc), 0.0).astype(bf16)
        for k in range(2):
            h_ref[2 * m + 2 + k] = hid[:, k * chans : (k + 1) * chans]

    def sum_pair(m):
        q = nt(w2_ref[...], jnp.concatenate([h_ref[2 * m + r] for r in range(4)], axis=1))
        for k in range(2):
            ps_ref[0, 2 * m + k] = join_taps(q[k * 3 * SLOT : (k + 1) * 3 * SLOT])

    sides = [[], []]
    for row in range(rows):
        block = x32_ref[pl.ds(row, chans, stride=step), :].T
        start = row * pitch + SIDE
        e_ref[start : start + cols] = block
        for k, part in enumerate((block[0:SIDE], block[cols - SIDE :])):
            sides[k].append(part)
        if row < 2:
            glo_ref[0, row] = block.astype(bf16)
        if row >= rows - 2:
            ghi_ref[0, row - (rows - 2)] = block.astype(bf16)
        shifted(e_ref, start, s_ref, row, cols)
    first_ref[0] = jnp.concatenate(sides[0], axis=0).astype(bf16)
    last_ref[0] = jnp.concatenate(sides[1], axis=0).astype(bf16)
    for m in range(half - 1):
        hidden_pair(m)
    for m in range(half):
        sum_pair(m)
    for n in range(nvar):
        x32_ref[pl.ds(n, rows, stride=VG), :] = st_ref[n, 0]
    lane = lanes((VG, WIDE))
    own = [jnp.zeros((VG, WIDE), f32)] * 2
    for row in range(rows):
        block = x32_ref[row * VG : (row + 1) * VG]
        block = jnp.where(lax.broadcasted_iota(jnp.int32, (VG, WIDE), 0) < nvar, block, 0.0)
        st8_ref[0, row] = block
        par, base = place(row, rows)
        own[par] = jnp.where(lane // SLOT == base // SLOT, roll(block, base + SIDE), own[par])
    own_ref[0, 0], own_ref[0, 1] = own


def main_start(x32_ref, e_ref, s_ref, h_ref):
    e_ref[...] = jnp.zeros_like(e_ref)
    h_ref[...] = jnp.zeros_like(h_ref)


def pack_kernel(flag_ref, a_ref, b_ref, first_ref, last_ref, own_ref, row_ref, halo_ref, outa_ref, outb_ref, w_ref, x_ref):
    cols = a_ref.shape[2]
    rows = first_ref.shape[1] // SIDE
    ch = row_ref.shape[3]
    size = (a_ref.shape[1] - ch) // 2
    nvar = size // REACH
    even = flag_ref[0] == 0
    lat_even = flag_ref[1] == 0
    got_a, got_b = a_ref[0].astype(f32), b_ref[0].astype(f32)
    low, high = jnp.where(even, got_b, got_a), jnp.where(even, got_a, got_b)
    halo_ref[...] = jnp.zeros_like(halo_ref)
    for k, x in enumerate((low, high)):
        x_ref[...] = x[ch : ch + size] + x[ch + size :]
        for r in range(REACH):
            halo_ref[0, k * REACH + r, 0:nvar] = x_ref[pl.ds(r, nvar, stride=REACH), :]
    low, high = low[0:ch].T, high[0:ch].T
    row_ref[0, 0] = low.astype(bf16)
    row_ref[0, 1] = high.astype(bf16)
    spot = lanes((VG, WIDE)) % SLOT
    near = (spot >= SIDE - REACH) & (spot < SIDE + REACH)
    terms = two_terms(jnp.where(near, own_ref[0, 0], roll(own_ref[0, 1], SIDE)))
    firsts = [low[0:SIDE]] + [first_ref[0, r * SIDE : (r + 1) * SIDE].astype(f32) for r in range(rows)] + [high[0:SIDE]]
    lasts = [low[cols - SIDE :]] + [last_ref[0, r * SIDE : (r + 1) * SIDE].astype(f32) for r in range(rows)]
    lasts += [high[cols - SIDE :]]
    for r in range(rows + 2):
        w_ref[0, 0, r * SENT : r * SENT + SIDE] = firsts[r]
    for r in reversed(range(rows + 2)):
        w_ref[0, 1, r * SENT : r * SENT + SIDE] = lasts[r]
    count = w_ref.shape[2]
    first, last = w_ref[0, 0].astype(bf16), w_ref[0, 1].astype(bf16)
    for out, pick in ((outa_ref, jnp.where(lat_even, last, first)), (outb_ref, jnp.where(lat_even, first, last))):
        out[0, 0:count] = pick
        out[0, count:] = jnp.concatenate(terms, axis=0)


def edge_kernel(row_ref, g0_ref, g1_ref, w1_ref, w2_ref, b1_ref, ps0_ref, ps1_ref, pe_ref, e_ref, s_ref, h_ref):
    levels = row_ref.shape[0]
    cols, ch = row_ref.shape[2:]
    pitch = cols + SLOT
    e_ref[...] = jnp.zeros_like(e_ref)
    for lv in range(levels):
        for k in range(2):
            part = [g0_ref[lv, 0], g0_ref[lv, 1]] if k == 0 else [g1_ref[lv, 0], g1_ref[lv, 1]]
            part = [row_ref[lv, 0]] + part if k == 0 else part + [row_ref[lv, 1]]
            for r in range(3):
                start = (6 * lv + 3 * k + r) * pitch + SIDE
                e_ref[start : start + cols] = part[r].astype(f32)
                shifted(e_ref, start, s_ref, 2 * lv + k, cols, 3 * ch * r)
    acc = jnp.dot(s_ref[...].reshape(2 * levels * cols, 9 * ch), w1_ref[...], preferred_element_type=f32) + b1_ref[...]
    place_in = lax.broadcasted_iota(jnp.int32, (cols, ch), 0)
    within = (place_in > 0) & (place_in < cols - 1)
    hid = silu(acc)
    for n in range(2 * levels):
        here = slice(n * cols, (n + 1) * cols)
        h_ref[here] = jnp.where(within, hid[here], 0.0).astype(bf16)
    q = nt(w2_ref[...], h_ref[...])
    for lv in range(levels):
        for k in range(2):
            here = slice((2 * lv + k) * cols, (2 * lv + k + 1) * cols)
            for a in range(3):
                x = join_taps(q[a * 3 * SLOT : (a + 1) * 3 * SLOT, here])
                if k == 0 and a < 2:
                    x = x + ps0_ref[lv, 1 - a]
                if k == 1 and a > 0:
                    x = x + ps1_ref[lv, 4 - a]
                pe_ref[lv, 3 * k + 2 - a] = x


def side_kernel(flag_ref, first_ref, last_ref, row_ref, la_ref, lb_ref, w1_ref, w2_ref, w2e_ref, b1_ref, keep_ref,
                pe_ref, ps0_ref, ps1_ref, sst_ref, pm_ref, cm_ref, pec_ref, outa_ref, outb_ref, e_ref, s_ref, hs_ref, z_ref, w_ref):
    levels = row_ref.shape[0]
    cols, ch = row_ref.shape[2:]
    rows = first_ref.shape[1] // SIDE
    half = rows // 2
    even = flag_ref[0] == 0
    lat_even = flag_ref[1] == 0
    wide = 2 * SLOT
    lane = lanes((2 * VG, WIDE))
    begin, end = lane < SLOT, lane >= WIDE - SLOT
    if z_ref.shape[0] > 2 * levels * SLOT:
        z_ref[...] = jnp.zeros_like(z_ref)
    for lv in range(levels):
        hs_ref[lv, 0, half * SLOT :] = jnp.zeros((SLOT, ch), bf16)
        hs_ref[lv, 1, 0:SLOT] = jnp.zeros((SLOT, ch), bf16)
    for lv in range(levels):
        a, b = la_ref[lv], lb_ref[lv]
        right, left = jnp.where(lat_even, a, b), jnp.where(lat_even, b, a)
        count = la_ref.shape[1] - 2 * VG
        st = []
        for x in (left, right):
            x = x[count:].astype(f32)
            st.append(x[0:VG] + x[VG:])
        sst_ref[lv, 0] = mix(st[0], st[1])
        sst_ref[lv, 1] = mix(roll(st[0], -SIDE), roll(st[1], -SIDE))
        w_ref[lv, 0], w_ref[lv, 1] = left[0:count].astype(f32), right[0:count].astype(f32)
        first, last = first_ref[lv].astype(f32), last_ref[lv].astype(f32)
        low, high = row_ref[lv, 0].astype(f32), row_ref[lv, 1].astype(f32)
        for row in range(-1, rows + 1):
            far = [w_ref[lv, k, pl.ds((row + 1) * SENT, SIDE), :] for k in range(2)]
            if 0 <= row < rows:
                own = slice(row * SIDE, (row + 1) * SIDE)
                mine = first[own], last[own]
            else:
                x = low if row < 0 else high
                mine = x[0:SIDE], x[cols - SIDE :]
            start = SIDE + (row + 1) * wide
            for k, part in enumerate((far[0], mine[0], mine[1], far[1])):
                e_ref[lv, start + k * SIDE : start + (k + 1) * SIDE] = part
        for row in range(rows + 2):
            for b in range(3):
                start = SIDE + row * wide + b
                x = [e_ref[lv, pl.ds(start, SIDE), :], e_ref[lv, pl.ds(start + 3 * SIDE - 2, SIDE), :]]
                x = jnp.concatenate(x, axis=0).astype(bf16)
                s_ref[lv, row * SLOT : (row + 1) * SLOT, b * ch : (b + 1) * ch] = x
    s = s_ref[...].reshape(levels, half + 1, 2, SLOT, 3 * ch)
    part = [s[:, 0:half, 0], s[:, 0:half, 1], s[:, 1:, 0], s[:, 1:, 1]]
    lhs = jnp.concatenate([p.reshape(levels * half * SLOT, 3 * ch) for p in part], axis=1)
    acc = jnp.dot(lhs, w1_ref[...], preferred_element_type=f32) + b1_ref[...]
    hid = silu(acc).reshape(levels, half, SLOT, 2 * ch) * keep_ref[...]
    for lv in range(levels):
        for m in range(half):
            here = hid[lv, m].astype(bf16)
            hs_ref[lv, 0, m * SLOT : (m + 1) * SLOT] = here[:, 0:ch]
            hs_ref[lv, 1, (m + 1) * SLOT : (m + 2) * SLOT] = here[:, ch:]
            if m == 0:
                z_ref[2 * lv * SLOT : (2 * lv + 1) * SLOT] = here[:, 0:ch]
            if m == half - 1:
                z_ref[(2 * lv + 1) * SLOT : (2 * lv + 2) * SLOT] = here[:, ch:]
    size = half * SLOT
    rhs = []
    for lv in range(levels):
        odd, ev = hs_ref.at[lv, 1], hs_ref.at[lv, 0]
        rhs.append(jnp.concatenate([odd[0:size], ev[0:size], odd[SLOT : size + SLOT], ev[SLOT : size + SLOT]], axis=1))
    q_side = nt(w2_ref[...], jnp.concatenate(rhs, axis=0))
    q_ends = nt(w2e_ref[...], z_ref[...])
    in_left = lanes((SLOT, WIDE)) % SLOT < SIDE

    def join_sides(q):
        taps = [q[b * SLOT : (b + 1) * SLOT] for b in range(3)]
        l = [jnp.where(in_left, x, 0.0) for x in taps]
        r = [jnp.where(in_left, 0.0, x) for x in taps]
        l = roll(l[0], 2) + roll(l[1], 1) + l[2]
        r = r[0] + roll(r[1], -1) + roll(r[2], -2)
        return mix(l, r), mix(r, l)

    for lv in range(levels):
        out, inn = {}, {}
        q = q_side[:, lv * size : (lv + 1) * size]
        for k in range(2):
            out[k], inn[k] = join_sides(q[k * 3 * SLOT : (k + 1) * 3 * SLOT])
        per = WIDE // (2 * SLOT)
        q = roll(q_ends[:, (lv // per) * WIDE : (lv // per + 1) * WIDE], -(lv % per) * 2 * SLOT)
        prev = join_sides(q[3 * SLOT : 6 * SLOT])
        nxt = join_sides(q[0 : 3 * SLOT])
        for k, x, spot, by in ((3, prev, end, WIDE - SLOT), (2, nxt, begin, -SLOT)):
            out[k], inn[k] = (jnp.where(spot, roll(y, by), 0.0) for y in x)
        for k in range(4):
            pm_ref[lv, k] = out[k]
            cm_ref[lv, k] = inn[k]
        mains = {}
        for k, row in enumerate((-1, 0, 1, rows - 2, rows - 1, rows)):
            mains[row] = pe_ref[lv, k]
        mains[2], mains[3] = ps0_ref[lv, 2], ps0_ref[lv, 3]
        mains[rows - 4], mains[rows - 3] = ps1_ref[lv, 0], ps1_ref[lv, 1]
        for row in mains:
            k, base = place(row, rows)
            mains[row] = add_columns(mains[row], inn[k], base)
        for k, row in enumerate((-1, 0, 1, rows - 2, rows - 1, rows)):
            pec_ref[lv, k] = mains[row]
        lane8 = lanes((VG, WIDE))
        st = sst_ref[lv, 0], sst_ref[lv, 1]

        def terms_of(x, here):
            first = x.astype(bf16).astype(f32)
            return jnp.where(here, first, roll(x - first, WIDE // 2))

        st_lo = terms_of(jnp.where(lane8 < 2 * SLOT, st[0], roll(st[1], 2 * SLOT)), lane8 < WIDE // 2)
        st_hi = terms_of(jnp.where(lane8 >= WIDE - 2 * SLOT, st[0], roll(st[1], -2 * SLOT)), lane8 >= WIDE // 2)
        side_lo = jnp.where(lane < 2 * SLOT, out[0], jnp.where(lane < 4 * SLOT, roll(out[1], 2 * SLOT), out[3]))
        side_hi = jnp.where(lane >= WIDE - 2 * SLOT, out[0],
                            jnp.where(lane >= WIDE - 4 * SLOT, roll(out[1], -2 * SLOT), out[2]))
        out_lo = [mains[-1], mains[0], side_lo, mains[1], mains[2], mains[3][0:VG], st_lo]
        out_hi = [mains[rows], mains[rows - 1], side_hi, mains[rows - 2], mains[rows - 3], mains[rows - 4][0:VG], st_hi]
        out_lo, out_hi = jnp.concatenate(out_lo, axis=0), jnp.concatenate(out_hi, axis=0)
        for ref, x in ((outa_ref, jnp.where(even, out_hi, out_lo)), (outb_ref, jnp.where(even, out_lo, out_hi))):
            terms = two_terms(x)
            ref[lv, 0 : x.shape[0]] = terms[0]
            ref[lv, x.shape[0] :] = terms[1][0:FINE]


def advect_kernel(flag_ref, ps_ref, pe_ref, pm_ref, cm_ref, a_ref, b_ref, st8_ref, halo_ref, sst_ref, own_ref,
                  b2_ref, lat_ref, lats_ref, *rest):
    vel_ref, ten_ref, out_ref = rest[-3:]
    rows = st8_ref.shape[1]
    nvar = ten_ref.shape[0]
    even = flag_ref[0] == 0
    lane16 = lanes((2 * VG, WIDE))
    lane = lanes((VG, WIDE))
    pair = 2 * VG

    def halos(xa, xb):
        return jnp.where(even, xb, xa), jnp.where(even, xa, xb)

    coarse = a_ref.shape[1] - FINE

    def both_terms(ref):
        x = ref[0].astype(f32)
        return jnp.concatenate([x[0:FINE] + x[coarse:], x[FINE:coarse]], axis=0)

    lo, hi = halos(both_terms(a_ref), both_terms(b_ref))
    main = {}
    for row in range(2, rows - 2):
        k, base = place(row, rows)
        main[row] = add_columns(ps_ref[0, row], cm_ref[0, k], base)
    for k, row in enumerate((-1, 0, 1, rows - 2, rows - 1, rows)):
        main[row] = pe_ref[0, k]
    for k in range(REACH + 1):
        first = k * pair if k < 2 else (k + 1) * pair
        there = slice(first, first + pair)
        for got, row in ((lo, -k), (hi, rows - 1 + k)):
            main[row] = main[row] + got[there] if row in main else got[there]
    slo, shi = (got[2 * pair : 3 * pair] for got in (lo, hi))
    zero = jnp.zeros((pair, WIDE), f32)
    last, front = lane16 >= WIDE - 2 * SLOT, lane16 < 2 * SLOT
    side = {
        0: pm_ref[0, 0] + jnp.where(lane16 < SLOT, slo, zero),
        1: pm_ref[0, 1] + jnp.where(lane16 >= WIDE - SLOT, shi, zero),
        2: pm_ref[0, 2] + jnp.where(last, slo, jnp.where(front, shi, zero)),
        3: pm_ref[0, 3] + jnp.where(last, roll(slo, 2 * SLOT), jnp.where(front, roll(shi, -2 * SLOT), zero)),
    }
    bias = b2_ref[...]
    main = {r: speed_cap * jnp.tanh(x + bias) for r, x in main.items()}
    side = {k: speed_cap * jnp.tanh(x + bias) * lats_ref[2, 0:1] for k, x in side.items()}
    for part in range(2):
        for row in range(rows):
            out_ref[part, row * VG : (row + 1) * VG] = main[row][part * VG : (part + 1) * VG]
        for n in range(nvar):
            vel_ref[2 * n + part, 0] = out_ref[part, pl.ds(n, rows, stride=VG), :]

    q0 = {row: st8_ref[0, row] for row in range(rows)}
    for k in range(REACH):
        q0[k - REACH], q0[rows + k] = halo_ref[0, k], halo_ref[0, REACH + k]
    hlo, hhi = (x[(REACH + 1) * pair + VG :] for x in (lo, hi))
    hlo, hhi = hlo + roll(hlo, WIDE // 2), hhi + roll(hhi, WIDE // 2)
    last, front = lane >= WIDE - 2 * SLOT, lane < 2 * SLOT
    nil = jnp.zeros((VG, WIDE), f32)
    out_q = {
        0: sst_ref[0, 0],
        1: sst_ref[0, 1],
        2: jnp.where(last, hlo, jnp.where(front, hhi, nil)),
        3: jnp.where(last, roll(hlo, 2 * SLOT), jnp.where(front, roll(hhi, -2 * SLOT), nil)),
    }
    own_q = {0: own_ref[0, 0], 1: own_ref[0, 1], 2: nil, 3: nil}
    for row in list(range(-REACH, 0)) + list(range(rows, rows + REACH)):
        k, base = place(row, rows)
        own_q[k] = jnp.where(lane // SLOT == base // SLOT, roll(q0[row], base + SIDE), own_q[k])

    everywhere = range(-REACH, rows + REACH)
    own = {k: jnp.zeros((pair, WIDE), f32) for k in range(4)}
    for row in everywhere:
        k, base = place(row, rows)
        own[k] = jnp.where(lane16 // SLOT == base // SLOT, roll(main[row], base + SIDE), own[k])

    def tiles(out, inner):
        return {**{k: mix(out[k], inner[k]) for k in range(4)}, **{4 + k: mix(inner[k], out[k]) for k in range(4)}}

    s0 = tiles(out_q, own_q)
    vel_s = tiles(side, own)

    def tile_rows(s):
        def turned(own, halo, by, first):
            own, halo = roll(own, by), roll(halo, by)
            return jnp.where(first, halo, own), jnp.where(first, own, halo)

        before, after = {}, {}
        for t in (0, 4):
            before[t + 1], before[t + 3], after[t], after[t + 2] = s[t], s[t + 2], s[t + 1], s[t + 3]
            before[t], before[t + 2] = turned(s[t + 1], s[t + 3], SLOT, lane < SLOT)
            after[t + 1], after[t + 3] = turned(s[t], s[t + 2], -SLOT, lane >= WIDE - SLOT)
        return before, after

    u = {r: x[0:VG] for r, x in main.items()}
    us = {k: x[0:VG] for k, x in vel_s.items()}
    inside = range(1 - REACH, rows + REACH - 1)
    v = {r: main[r][VG:] for r in inside}
    vs = {k: x[VG:] for k, x in vel_s.items()}
    cosine, metric = lat_ref[0], lat_ref[1]

    def side_table(n, k):
        return mix(lats_ref[n], lats_ref[n + 3]) if k < 4 else mix(lats_ref[n + 3], lats_ref[n])

    cosine_s, metric_s = ([side_table(n, k) for k in range(8)] for n in range(2))
    flux = {r: x * cosine for r, x in v.items()}
    flux_s = {k: x * cosine_s[k] for k, x in vs.items()}
    ub, ua = tile_rows(us)

    def coefs(m, uu, vv, udiff, vdiff):
        flow = m * uu
        cl = jnp.maximum(flow, 0.0)
        cr = cl - flow
        cd = jnp.maximum(vv, 0.0)
        cu = cd - vv
        div = (0.5 * m) * (udiff + vdiff)
        return -((cl + cr) + (cd + cu) + div), cl, cr, cd, cu

    cm = {r: coefs(metric, u[r], v[r], u[r + 1] - u[r - 1], roll(flux[r], -1) - roll(flux[r], 1)) for r in inside}
    cs = {k: coefs(metric_s[k], us[k], vs[k], ua[k] - ub[k], roll(flux_s[k], -1) - roll(flux_s[k], 1)) for k in range(8)}

    def stencil(c, x, left, right):
        return c[0] * x + c[1] * left + c[2] * right + c[3] * roll(x, 1) + c[4] * roll(x, -1)

    def rate(q, s, depth):
        rb, ra = tile_rows(s)
        inner = range(depth - REACH, rows + REACH - depth)
        wanted = [k for k in range(8) if depth < REACH or k % 4 < 2]
        return ({r: stencil(cm[r], q[r], q[r - 1], q[r + 1]) for r in inner},
                {k: stencil(cs[k], s[k], rb[k], ra[k]) for k in wanted})

    def moved(rates, by):
        return {r: q0[r] + by * x for r, x in rates[0].items()}, {k: s0[k] + by * x for k, x in rates[1].items()}

    one = rate(q0, s0, 1)
    two = rate(*moved(one, 0.5 * time_step), 2)
    three = rate(*moved(two, 0.5 * time_step), 3)
    four = rate(*moved(three, time_step), 4)

    def mean(n, k):
        return (one[n][k] + four[n][k] + 2.0 * (two[n][k] + three[n][k])) * (1.0 / 6.0)

    ends = {k: mix(mean(1, 4 + k), mean(1, k)) for k in range(2)}
    for row in range(rows):
        k, base = place(row, rows)
        at_end = (lane < REACH) | (lane >= WIDE - REACH)
        out_ref[0, row * VG : (row + 1) * VG] = jnp.where(at_end, roll(ends[k], -(base + SIDE)), mean(0, row))
    for n in range(nvar):
        ten_ref[n, 0] = out_ref[0, pl.ds(n, rows, stride=VG), :]


def full(shape):
    return pl.BlockSpec(shape, lambda *i: (0,) * len(shape))


def per_level(shape):
    return pl.BlockSpec((1,) + shape[1:], lambda i: (i,) + (0,) * (len(shape) - 1))


def level_part(shape, index, block=1, offset=0):
    return pl.BlockSpec((block,) + shape, lambda i: (i + offset, index) + (0,) * (len(shape) - 1))


def levels_of(shape, block=1, offset=0):
    return pl.BlockSpec((block,) + shape[1:], lambda i: (i + offset,) + (0,) * (len(shape) - 1))


def var_level(shape, offset=0):
    return pl.BlockSpec((shape[0], 1) + shape[2:], lambda i: (0, i + offset, 0, 0))


def body(hidden_in, w_conv1, b_conv1, w_conv2, b_conv2, state):
    lev, ch, rows, cols = hidden_in.shape
    nvar = state.shape[0]
    ext = cols + SLOT
    half = rows // 2
    params = pltpu.CompilerParams(vmem_limit_bytes=VMEM_LIMIT)
    smem = pl.BlockSpec(memory_space=pltpu.SMEM)
    sds = jax.ShapeDtypeStruct

    def call(kernel, steps, ins, outs, out_specs, scratch, args, cost=None, aliases={}):
        return pl.pallas_call(
            kernel,
            grid=(steps,),
            in_specs=ins,
            out_specs=out_specs,
            out_shape=outs,
            scratch_shapes=scratch,
            compiler_params=params,
            cost_estimate=cost,
            input_output_aliases=aliases,
        )(*args)

    vmem = pl.BlockSpec(memory_space=pltpu.VMEM)

    def levels(block=1, off=0, first=None, size=None):
        def view(ref, i):
            here = pl.ds(off + i * block, block)
            return ref.at[here] if first is None else ref.at[here, first : first + size]

        return view

    def whole(kernel, steps, ins, outs, scratch, cost, unroll=1, scratch_views=(), first=None):
        views = [v for _, v in ins] + [v for _, v in outs] + list(scratch_views)

        def run(*refs):
            def one(i, carry):
                kernel(*[v(r, i) if v else r for v, r in zip(views, refs)], *refs[len(views) :])
                return carry

            if first:
                first(*refs[len(views) :])
            if steps == 1:
                one(0, 0)
            else:
                lax.fori_loop(0, steps, one, 0, unroll=unroll)

        return pl.pallas_call(
            run,
            in_specs=[smem if x is flags else vmem for x, _ in ins],
            out_specs=[vmem] * len(outs),
            out_shape=[x for x, _ in outs],
            scratch_shapes=scratch,
            compiler_params=params,
            cost_estimate=pl.CostEstimate(flops=cost, bytes_accessed=2**20, transcendentals=0),
        )(*[x for x, _ in ins])

    flags = jnp.stack([lax.axis_index("lon") % 2, lax.axis_index("lat") % 2, lax.axis_index("lat")]).astype(jnp.int32)
    lon_wire = (lev, ch + 2 * nvar * REACH, cols)
    lon_a, lon_b = pl.pallas_call(
        rows_kernel,
        in_specs=[smem] + [pl.BlockSpec(memory_space=pltpu.HBM)] * 2,
        out_specs=[vmem] * 2,
        out_shape=[sds(lon_wire, bf16)] * 2,
        scratch_shapes=[
            pltpu.VMEM((ch * rows, cols), f32),
            pltpu.VMEM(hidden_in.shape, bf16),
            pltpu.VMEM(state.shape, f32),
            pltpu.SemaphoreType.DMA((lev + 1,)),
        ],
        compiler_params=pltpu.CompilerParams(vmem_limit_bytes=ROWS_LIMIT),
    )(flags, hidden_in, state)
    shapes = [((12 * ch, 2 * ch), bf16), ((6 * SLOT, 4 * ch), bf16), ((9 * SLOT, ch), bf16),
              ((6 * SLOT, ch), bf16), ((1, 2 * ch), f32), ((2 * VG, WIDE), f32), ((3, VG, WIDE), f32), ((6, VG, WIDE), f32),
              ((SLOT, 2 * ch), f32)]
    w1_one = w_conv1.reshape(9 * ch, ch)
    b1 = b_conv1.reshape(1, ch)
    n_lat = cols * lax.axis_size("lat")
    w1_pair, w2_pair, w2_one, w2_ends, b1_pair, b2, lat_main, lat_side, keep = pl.pallas_call(
        lambda flag_ref, *refs: prep_kernel(flag_ref, n_lat, cols, *refs),
        in_specs=[smem, smem] + [vmem] * 3,
        out_specs=[vmem] * len(shapes),
        out_shape=[sds(*x) for x in shapes],
        scratch_shapes=[pltpu.VMEM((4 * VG, ch), f32)],
        compiler_params=params,
    )(flags, b_conv2, w1_one, w_conv2.transpose(0, 1, 3, 2).reshape(9, 2 * nvar, ch), b1)
    lon_a = swap(lon_a, "lon", 0, True)
    lon_b = swap(lon_b, "lon", 1, True)

    hbm = pl.BlockSpec(memory_space=pltpu.HBM)
    g_pair = (lev, 2, cols, ch)
    st8_shape = (lev, rows, VG, WIDE)
    cut = (lev, rows * SIDE, ch)
    ps_shape = (lev, rows, 2 * VG, WIDE)
    own_shape = (lev, 2, VG, WIDE)
    halo_shape = (lev, 2 * REACH, VG, WIDE)
    shapes = [(g_pair, bf16), (g_pair, bf16), (cut, bf16), (cut, bf16), (st8_shape, f32), (own_shape, f32), (ps_shape, f32)]
    each = levels()
    g_lo, g_hi, first, last, st8, own, ps = whole(
        main_kernel,
        lev,
        [(hidden_in, each), (state, lambda ref, i: ref.at[:, pl.ds(i, 1)]), (w1_pair, None), (w2_pair, None), (b1_pair, None)],
        [(sds(*x), each) for x in shapes],
        [
            pltpu.VMEM((ch * (rows + VG), cols), f32),
            pltpu.VMEM((rows * (cols + SLOT), ch), f32),
            pltpu.VMEM((rows, cols, 3 * ch), bf16),
            pltpu.VMEM((rows + 2, cols, ch), bf16),
        ],
        2 * lev * rows * ext * 9 * ch * ch,
        first=main_start,
    )

    sent_rows = -(-((rows + 1) * SENT + SIDE) // SLOT) * SLOT
    lat_wire = (lev, sent_rows + 2 * VG, WIDE)
    pair_shape = (lev, 2, cols, ch)
    shapes = [(pair_shape, bf16), (halo_shape, f32), (lat_wire, bf16), (lat_wire, bf16)]
    each = levels()
    row_pair, halo, lat_a, lat_b = whole(
        pack_kernel,
        lev,
        [(flags, None)] + [(x, each) for x in (lon_a, lon_b, first, last, own)],
        [(sds(*x), each) for x in shapes],
        [pltpu.VMEM((lev, 2, sent_rows, ch), f32), pltpu.VMEM((nvar * REACH, WIDE), f32)],
        2**22,
        PACK_UNROLL,
        [each],
    )
    lat_a = swap(lat_a, "lat", 0, False)
    lat_b = swap(lat_b, "lat", 1, False)

    block = EDGE_LEVELS
    pe_shape = (lev, 6, 2 * VG, WIDE)
    each = levels(block)
    (pe,) = whole(
        edge_kernel,
        lev // block,
        [(row_pair, each), (g_lo, each), (g_hi, each), (w1_one, None), (w2_one, None), (b1, None),
         (ps, levels(block, 0, 0, 4)), (ps, levels(block, 0, rows - 4, 4))],
        [(sds(pe_shape, f32), each)],
        [
            pltpu.VMEM((6 * block * (cols + SLOT), ch), f32),
            pltpu.VMEM((2 * block, cols, 9 * ch), bf16),
            pltpu.VMEM((2 * block * cols, ch), bf16),
        ],
        lev * 4 * ext * 9 * ch * ch,
    )

    block = SIDE_LEVELS
    parts = PARTS
    count = lev // parts
    wire = (count, 2 * VG * (REACH + 2) + FINE, WIDE)
    pec_shape = (count,) + pe_shape[1:]
    pm4_shape = (count, 4, 2 * VG, WIDE)
    sst_shape = (count, 2, VG, WIDE)
    shapes = [(sst_shape, f32), (pm4_shape, f32), (pm4_shape, f32), (pec_shape, f32), (wire, bf16), (wire, bf16)]
    sent = []
    for part in range(parts):
        here = levels(block, part * count)
        each = levels(block)
        sst, pm, cm, pec, out_a, out_b = whole(
            side_kernel,
            count // block,
            [(flags, None)] + [(x, here) for x in (first, last, row_pair, lat_a, lat_b)]
            + [(x, None) for x in (w1_pair, w2_pair, w2_ends, b1_pair, keep)]
            + [(pe, here), (ps, levels(block, part * count, 0, 4)), (ps, levels(block, part * count, rows - 4, 4))],
            [(sds(*x), each) for x in shapes],
            [
                pltpu.VMEM((block, (rows + 2) * 2 * SLOT + 2 * SIDE, ch), f32),
                pltpu.VMEM((block, (rows + 2) * SLOT, 3 * ch), bf16),
                pltpu.VMEM((block, 2, (half + 1) * SLOT, ch), bf16),
                pltpu.VMEM((max(WIDE, block * 2 * SLOT), ch), bf16),
                pltpu.VMEM((block, 2, sent_rows, ch), f32),
            ],
            count * 512 * 12 * ch * ch,
        )
        sent.append((pec, pm, cm, sst, swap(out_a, "lon", 0, True), swap(out_b, "lon", 1, True)))

    outs = [sds((2 * nvar, lev, rows, cols), f32), sds(state.shape, f32)]
    done = ()
    for part, (pec, pm, cm, sst, out_a, out_b) in enumerate(sent):
        off = part * count
        here, each = levels(1, off), levels()
        ins = [(flags, None), (ps, here)] + [(x, each) for x in (pec, pm, cm, out_a, out_b)]
        ins += [(st8, here), (halo, here), (sst, each), (own, here)] + [(x, None) for x in (b2, lat_main, lat_side)]

        def run(*refs, off=off, ins=ins, given=len(done)):
            sources = [functools.partial(v, r) if v else (lambda i, r=r: r) for (_, v), r in zip(ins, refs)]
            vel_hbm, ten_hbm, vel_ref, ten_ref, out_ref, sem = refs[len(ins) + given :]

            def copies(i):
                at, to = pl.ds(i, 1), pl.ds(off + i, 1)
                return [
                    pltpu.make_async_copy(src.at[:, at], dst.at[:, to], sem.at[i, k])
                    for k, (src, dst) in enumerate(((vel_ref, vel_hbm), (ten_ref, ten_hbm)))
                ]

            def one(i, carry):
                at = pl.ds(i, 1)
                advect_kernel(*[f(i) for f in sources], vel_ref.at[:, at], ten_ref.at[:, at], out_ref.at[i])
                for copy in copies(i):
                    copy.start()
                return carry

            lax.fori_loop(0, count, one, 0, unroll=ADVECT_UNROLL)
            for i in range(count):
                for copy in copies(i):
                    copy.wait()

        done = pl.pallas_call(
            run,
            in_specs=[smem if x is flags else vmem for x, _ in ins] + [hbm] * len(done),
            out_specs=[hbm] * 2,
            out_shape=outs,
            scratch_shapes=[
                pltpu.VMEM((2 * nvar, count, rows, cols), f32),
                pltpu.VMEM((nvar, count, rows, cols), f32),
                pltpu.VMEM((count, 2, rows * VG, WIDE), f32),
                pltpu.SemaphoreType.DMA((count, 2)),
            ],
            compiler_params=params,
            cost_estimate=pl.CostEstimate(flops=count * 2**24, bytes_accessed=2 * 2**20, transcendentals=0),
            input_output_aliases={len(ins): 0, len(ins) + 1: 1} if done else {},
        )(*[x for x, _ in ins], *done)
    return tuple(done)


def solution(mesh):
    placed = (P(None, None, "lon", "lat"), P(), P(), P(), P(), P(None, None, "lon", "lat"))
    return jax.shard_map(
        body,
        mesh=mesh,
        in_specs=placed,
        out_specs=(P(None, None, "lon", "lat"), P(None, None, "lon", "lat")),
        check_vma=False,
    )
```

```python
import functools
import math

import jax
import jax.numpy as jnp
from jax import lax
from jax.experimental import pallas as pl
from jax.experimental.pallas import tpu as pltpu
from jax.sharding import PartitionSpec as P

time_step = 0.5
speed_cap = 0.6
cos_floor = 0.5

SIDE = 8
SLOT = 2 * SIDE
SENT = 6
FINE = 32
WIDE = 128
REACH = 4
VG = 8
VMEM_LIMIT = 24 * 2**20
ROWS_LIMIT = 50 * 2**20
EDGE_LEVELS = 8
ADVECT_UNROLL = 2
SIDE_LEVELS = 4
PARTS = 2
PACK_UNROLL = 4
f32 = jnp.float32
bf16 = jnp.bfloat16


def swap_pairs(count, first, closed):
    pairs = []
    for low in range(first, count, 2):
        high = low + 1
        if high >= count and not closed:
            continue
        pairs += [(low, high % count), (high % count, low)]
    return pairs


def swap(block, axis, first, closed):
    return lax.ppermute(block, axis, swap_pairs(lax.axis_size(axis), first, closed))


def place(row, rows):
    half, par = row // 2, row % 2
    own = 0 <= half < rows // 2
    return (0 if own else 2) + par, SLOT * (half % (rows // 2))


def lanes(shape):
    return lax.broadcasted_iota(jnp.int32, shape, len(shape) - 1)


def roll(x, by):
    by = by % WIDE
    return pltpu.roll(x, by, x.ndim - 1) if by else x


def col_before(mains, sides, at):
    lane = lanes(next(iter(mains.values())).shape)
    new_sides = {k: roll(s, 1) for k, s in sides.items()}
    new_mains = {}
    for row, main in mains.items():
        k, base = at(row)
        new_mains[row] = jnp.where(lane == 0, roll(sides[k], 1 - base - SIDE), roll(main, 1))
        new_sides[k] = jnp.where(lane == base + SIDE, roll(main, base + SIDE + 1), new_sides[k])
    return new_mains, new_sides


def col_after(mains, sides, at):
    lane = lanes(next(iter(mains.values())).shape)
    new_sides = {k: roll(s, -1) for k, s in sides.items()}
    new_mains = {}
    for row, main in mains.items():
        k, base = at(row)
        new_mains[row] = jnp.where(lane == WIDE - 1, roll(sides[k], WIDE - 1 - base - SIDE), roll(main, -1))
        new_sides[k] = jnp.where(lane == base + SIDE - 1, roll(main, base + SIDE - 1), new_sides[k])
    return new_mains, new_sides


def join_taps(x):
    return roll(x[0:SLOT], 1) + x[SLOT : 2 * SLOT] + roll(x[2 * SLOT : 3 * SLOT], -1)


def mix(first, second):
    return jnp.where(lanes(first.shape) % SLOT < SIDE, first, second)


def add_columns(main, side, base):
    lane = lanes(main.shape)
    return main + jnp.where((lane < SIDE) | (lane >= WIDE - SIDE), roll(side, -(base + SIDE)), 0.0)


def two_terms(x):
    first = x.astype(bf16)
    return [first, (x - first.astype(f32)).astype(bf16)]


def two_terms_stacked(x):
    first = x.astype(bf16).astype(f32)
    return jnp.concatenate([first, x - first], axis=0).astype(bf16)


def nt(lhs, rhs):
    return lax.dot_general(lhs, rhs, (((1,), (1,)), ((), ())), preferred_element_type=f32)


def silu(s):
    return s / (1.0 + jnp.exp(-s))


def shifted(e_ref, start, s_ref, to, count, first=0):
    ch = e_ref.shape[-1]
    for b in range(3):
        lane0 = first + b * ch
        s_ref[to, :, lane0 : lane0 + ch] = e_ref[pl.ds(start - 1 + b, count), :].astype(bf16)


def rows_kernel(flag_ref, x_hbm, st_hbm, outa_ref, outb_ref, x32_ref, x_ref, st_ref, sem):
    levels, ch, rows, cols = x_hbm.shape
    nvar = st_hbm.shape[0]
    size = nvar * REACH
    even = flag_ref[0] == 0

    def level_copy(lv):
        return pltpu.make_async_copy(x_hbm.at[lv], x_ref.at[lv], sem.at[lv])

    state_copy = pltpu.make_async_copy(st_hbm, st_ref, sem.at[levels])
    level_copy(0).start()
    state_copy.start()
    for lv in range(1, levels):
        level_copy(lv).start()
    state_copy.wait()

    def one(lv, carry):
        level_copy(lv).wait()
        x32_ref[...] = x_ref[lv].astype(f32).reshape(ch * rows, cols)
        lo, hi = (x32_ref[pl.ds(row, ch, stride=rows), :].astype(bf16) for row in (0, rows - 1))
        outa_ref[lv, 0:ch] = jnp.where(even, hi, lo)
        outb_ref[lv, 0:ch] = jnp.where(even, lo, hi)
        for n in range(nvar):
            x32_ref[n * REACH : (n + 1) * REACH] = st_ref[n, lv, 0:REACH]
            x32_ref[size + n * REACH : size + (n + 1) * REACH] = st_ref[n, lv, rows - REACH :]
        lo, hi = x32_ref[0:size], x32_ref[size : 2 * size]
        outa_ref[lv, ch:] = two_terms_stacked(jnp.where(even, hi, lo))
        outb_ref[lv, ch:] = two_terms_stacked(jnp.where(even, lo, hi))
        return carry

    lax.fori_loop(0, levels, one, 0)


def prep_kernel(flag_ref, n_lat, cols, b2_ref, w1_ref, w2_ref, b1_ref,
                w1p_ref, w2p_ref, w2o_ref, w2e_ref, b1p_ref, b2o_ref, lat_ref, lats_ref, keep_ref, w2s_ref):
    size, ch = w1_ref.shape
    nvar = w2_ref.shape[1] // 2
    w1p_ref[0:size, 0:ch] = w1_ref[...]
    w1p_ref[size:, 0:ch] = jnp.zeros((3 * ch, ch), bf16)
    w1p_ref[0 : 3 * ch, ch:] = jnp.zeros((3 * ch, ch), bf16)
    w1p_ref[3 * ch :, ch:] = w1_ref[...]
    b1p_ref[:, 0:ch] = b1_ref[...]
    b1p_ref[:, ch:] = b1_ref[...]
    w2p_ref[...] = jnp.zeros_like(w2p_ref)
    w2s_ref[0 : 2 * VG] = jnp.zeros((2 * VG, ch), f32)
    for a in range(3):
        for b in range(3):
            w2s_ref[2 * VG : 2 * VG + 2 * nvar] = w2_ref[3 * a + b].astype(f32)
            for part in range(2):
                w2s_ref[part * VG : part * VG + nvar] = w2s_ref[pl.ds(2 * VG + part, nvar, stride=2), :]
            here = w2s_ref[0 : 2 * VG].astype(bf16)
            at = 3 * a + b
            w2o_ref[at * SLOT : (at + 1) * SLOT] = here
            for k in range(2):
                first = (3 * k + b) * SLOT
                w2p_ref[first : first + SLOT, (a + k) * ch : (a + k + 1) * ch] = here
            if a != 1:
                first = (3 * (a // 2) + b) * SLOT
                w2e_ref[first : first + SLOT] = here
    b2o_ref[...] = jnp.zeros_like(b2o_ref)
    for v in range(2 * nvar):
        row = (v % 2) * VG + v // 2
        b2o_ref[row : row + 1] = jnp.full((1, WIDE), b2_ref[v], f32)

    def table(place_in):
        place_in = place_in + flag_ref[2] * cols
        keep = ((place_in >= 0) & (place_in < n_lat)).astype(f32)
        phi = (place_in.astype(f32) + 0.5) * (math.pi / n_lat) - 0.5 * math.pi
        cosine = jnp.maximum(jnp.cos(phi), cos_floor)
        return cosine, 1.0 / cosine, keep

    lane = lanes((VG, WIDE))
    slot = lane % SLOT
    beyond = jnp.where(slot < SIDE, slot - SIDE, cols + slot - SIDE)
    ends = jnp.where(slot < SIDE, cols - SIDE + slot, slot - SIDE)
    for ref, first, place_in in ((lat_ref, 0, lane), (lats_ref, 0, beyond), (lats_ref, 3, ends)):
        for k, x in enumerate(table(place_in)):
            ref[first + k] = x
    spot = lax.broadcasted_iota(jnp.int32, keep_ref.shape, 0)
    place_in = jnp.where(spot < SIDE, spot - SIDE + 1, cols - SIDE - 1 + spot) + flag_ref[2] * cols
    keep_ref[...] = ((place_in >= 0) & (place_in < n_lat)).astype(f32)


def main_kernel(x_ref, st_ref, w1_ref, w2_ref, b1_ref, glo_ref, ghi_ref, first_ref, last_ref, st8_ref, own_ref, ps_ref,
                x32_ref, e_ref, s_ref, h_ref):
    chans, rows, cols = x_ref.shape[1:]
    nvar = st_ref.shape[0]
    half = rows // 2
    pitch = cols + SLOT
    step = rows + VG
    x32_ref.reshape(chans, step, cols)[:, 0:rows] = x_ref[0].astype(f32)

    place_in = lax.broadcasted_iota(jnp.int32, (cols, 2 * chans), 0)
    within = (place_in > 0) & (place_in < cols - 1)

    def hidden_pair(m):
        lhs = jnp.concatenate([s_ref[2 * m + r] for r in range(4)], axis=1)
        acc = jnp.dot(lhs, w1_ref[...], preferred_element_type=f32) + b1_ref[...]
        hid = jnp.where(within, silu(acc), 0.0).astype(bf16)
        for k in range(2):
            h_ref[2 * m + 2 + k] = hid[:, k * chans : (k + 1) * chans]

    def sum_pair(m):
        q = nt(w2_ref[...], jnp.concatenate([h_ref[2 * m + r] for r in range(4)], axis=1))
        for k in range(2):
            ps_ref[0, 2 * m + k] = join_taps(q[k * 3 * SLOT : (k + 1) * 3 * SLOT])

    sides = [[], []]
    for row in range(rows):
        block = x32_ref[pl.ds(row, chans, stride=step), :].T
        start = row * pitch + SIDE
        e_ref[start : start + cols] = block
        for k, part in enumerate((block[0:SIDE], block[cols - SIDE :])):
            sides[k].append(part)
        if row < 2:
            glo_ref[0, row] = block.astype(bf16)
        if row >= rows - 2:
            ghi_ref[0, row - (rows - 2)] = block.astype(bf16)
        shifted(e_ref, start, s_ref, row, cols)
    first_ref[0] = jnp.concatenate(sides[0], axis=0).astype(bf16)
    last_ref[0] = jnp.concatenate(sides[1], axis=0).astype(bf16)
    for m in range(half - 1):
        hidden_pair(m)
    for m in range(half):
        sum_pair(m)
    for n in range(nvar):
        x32_ref[pl.ds(n, rows, stride=VG), :] = st_ref[n, 0]
    lane = lanes((VG, WIDE))
    own = [jnp.zeros((VG, WIDE), f32)] * 2
    for row in range(rows):
        block = x32_ref[row * VG : (row + 1) * VG]
        block = jnp.where(lax.broadcasted_iota(jnp.int32, (VG, WIDE), 0) < nvar, block, 0.0)
        st8_ref[0, row] = block
        par, base = place(row, rows)
        own[par] = jnp.where(lane // SLOT == base // SLOT, roll(block, base + SIDE), own[par])
    own_ref[0, 0], own_ref[0, 1] = own


def main_start(x32_ref, e_ref, s_ref, h_ref):
    e_ref[...] = jnp.zeros_like(e_ref)
    h_ref[...] = jnp.zeros_like(h_ref)


def pack_kernel(flag_ref, a_ref, b_ref, first_ref, last_ref, own_ref, row_ref, halo_ref, outa_ref, outb_ref, w_ref, x_ref):
    cols = a_ref.shape[2]
    rows = first_ref.shape[1] // SIDE
    ch = row_ref.shape[3]
    size = (a_ref.shape[1] - ch) // 2
    nvar = size // REACH
    even = flag_ref[0] == 0
    lat_even = flag_ref[1] == 0
    got_a, got_b = a_ref[0].astype(f32), b_ref[0].astype(f32)
    low, high = jnp.where(even, got_b, got_a), jnp.where(even, got_a, got_b)
    halo_ref[...] = jnp.zeros_like(halo_ref)
    for k, x in enumerate((low, high)):
        x_ref[0:size] = x[ch : ch + size] + x[ch + size :]
        for r in range(REACH):
            halo_ref[0, k * REACH + r, 0:nvar] = x_ref[pl.ds(r, nvar, stride=REACH), :]
    low, high = low[0:ch].T, high[0:ch].T
    row_ref[0, 0] = low.astype(bf16)
    row_ref[0, 1] = high.astype(bf16)
    spot = lanes((VG, WIDE)) % SLOT
    near = (spot >= SIDE - REACH) & (spot < SIDE + REACH)
    terms = two_terms_stacked(jnp.where(near, own_ref[0, 0], roll(own_ref[0, 1], SIDE)))
    first, last = first_ref[0].astype(f32), last_ref[0].astype(f32)
    firsts = [low[0:SIDE]] + [first[r * SIDE : (r + 1) * SIDE] for r in range(rows)] + [high[0:SIDE]]
    lasts = [low[cols - SIDE :]] + [last[r * SIDE : (r + 1) * SIDE] for r in range(rows)]
    lasts += [high[cols - SIDE :]]
    for r in range(rows + 2):
        w_ref[0, 0, r * SENT : r * SENT + SIDE] = firsts[r]
    for r in reversed(range(rows + 2)):
        w_ref[0, 1, r * SENT : r * SENT + SIDE] = lasts[r]
    count = w_ref.shape[2]
    first, last = w_ref[0, 0].astype(bf16), w_ref[0, 1].astype(bf16)
    for out, pick in ((outa_ref, jnp.where(lat_even, last, first)), (outb_ref, jnp.where(lat_even, first, last))):
        out[0, 0:count] = pick
        out[0, count:] = terms


def edge_kernel(row_ref, g0_ref, g1_ref, w1_ref, w2_ref, b1_ref, ps0_ref, ps1_ref, pe_ref, e_ref, s_ref, h_ref):
    levels = row_ref.shape[0]
    cols, ch = row_ref.shape[2:]
    pitch = cols + SLOT
    e_ref[...] = jnp.zeros_like(e_ref)
    for lv in range(levels):
        for k in range(2):
            part = [g0_ref[lv, 0], g0_ref[lv, 1]] if k == 0 else [g1_ref[lv, 0], g1_ref[lv, 1]]
            part = [row_ref[lv, 0]] + part if k == 0 else part + [row_ref[lv, 1]]
            for r in range(3):
                start = (6 * lv + 3 * k + r) * pitch + SIDE
                e_ref[start : start + cols] = part[r].astype(f32)
                shifted(e_ref, start, s_ref, 2 * lv + k, cols, 3 * ch * r)
    acc = jnp.dot(s_ref[...].reshape(2 * levels * cols, 9 * ch), w1_ref[...], preferred_element_type=f32) + b1_ref[...]
    place_in = lax.broadcasted_iota(jnp.int32, (cols, ch), 0)
    within = (place_in > 0) & (place_in < cols - 1)
    hid = silu(acc)
    for n in range(2 * levels):
        here = slice(n * cols, (n + 1) * cols)
        h_ref[here] = jnp.where(within, hid[here], 0.0).astype(bf16)
    q = nt(w2_ref[...], h_ref[...])
    for lv in range(levels):
        for k in range(2):
            here = slice((2 * lv + k) * cols, (2 * lv + k + 1) * cols)
            for a in range(3):
                x = join_taps(q[a * 3 * SLOT : (a + 1) * 3 * SLOT, here])
                if k == 0 and a < 2:
                    x = x + ps0_ref[lv, 1 - a]
                if k == 1 and a > 0:
                    x = x + ps1_ref[lv, 4 - a]
                pe_ref[lv, 3 * k + 2 - a] = x


def side_kernel(flag_ref, first_ref, last_ref, row_ref, la_ref, lb_ref, w1_ref, w2_ref, w2e_ref, b1_ref, keep_ref,
                pe_ref, ps0_ref, ps1_ref, sst_ref, pm_ref, cm_ref, pec_ref, outa_ref, outb_ref, e_ref, s_ref, hs_ref, z_ref, w_ref):
    levels = row_ref.shape[0]
    cols, ch = row_ref.shape[2:]
    rows = first_ref.shape[1] // SIDE
    half = rows // 2
    even = flag_ref[0] == 0
    lat_even = flag_ref[1] == 0
    wide = 2 * SLOT
    lane = lanes((2 * VG, WIDE))
    begin, end = lane < SLOT, lane >= WIDE - SLOT
    if z_ref.shape[0] > 2 * levels * SLOT:
        z_ref[...] = jnp.zeros_like(z_ref)
    for lv in range(levels):
        hs_ref[lv, 0, half * SLOT :] = jnp.zeros((SLOT, ch), bf16)
        hs_ref[lv, 1, 0:SLOT] = jnp.zeros((SLOT, ch), bf16)
    for lv in range(levels):
        a, b = la_ref[lv], lb_ref[lv]
        right, left = jnp.where(lat_even, a, b), jnp.where(lat_even, b, a)
        count = la_ref.shape[1] - 2 * VG
        st = []
        for x in (left, right):
            x = x[count:].astype(f32)
            st.append(x[0:VG] + x[VG:])
        sst_ref[lv, 0] = mix(st[0], st[1])
        sst_ref[lv, 1] = mix(roll(st[0], -SIDE), roll(st[1], -SIDE))
        w_ref[lv, 0], w_ref[lv, 1] = left[0:count].astype(f32), right[0:count].astype(f32)
        first, last = first_ref[lv].astype(f32), last_ref[lv].astype(f32)
        low, high = row_ref[lv, 0].astype(f32), row_ref[lv, 1].astype(f32)
        for row in range(-1, rows + 1):
            far = [w_ref[lv, k, pl.ds((row + 1) * SENT, SIDE), :] for k in range(2)]
            if 0 <= row < rows:
                own = slice(row * SIDE, (row + 1) * SIDE)
                mine = first[own], last[own]
            else:
                x = low if row < 0 else high
                mine = x[0:SIDE], x[cols - SIDE :]
            start = SIDE + (row + 1) * wide
            for k, part in enumerate((far[0], mine[0], mine[1], far[1])):
                e_ref[lv, start + k * SIDE : start + (k + 1) * SIDE] = part
        for row in range(rows + 2):
            for b in range(3):
                start = SIDE + row * wide + b
                x = [e_ref[lv, pl.ds(start, SIDE), :], e_ref[lv, pl.ds(start + 3 * SIDE - 2, SIDE), :]]
                x = jnp.concatenate(x, axis=0).astype(bf16)
                s_ref[lv, row * SLOT : (row + 1) * SLOT, b * ch : (b + 1) * ch] = x
    s = s_ref[...].reshape(levels, half + 1, 2, SLOT, 3 * ch)
    part = [s[:, 0:half, 0], s[:, 0:half, 1], s[:, 1:, 0], s[:, 1:, 1]]
    lhs = jnp.concatenate([p.reshape(levels * half * SLOT, 3 * ch) for p in part], axis=1)
    acc = jnp.dot(lhs, w1_ref[...], preferred_element_type=f32) + b1_ref[...]
    hid = silu(acc).reshape(levels, half, SLOT, 2 * ch) * keep_ref[...]
    for lv in range(levels):
        for m in range(half):
            here = hid[lv, m].astype(bf16)
            hs_ref[lv, 0, m * SLOT : (m + 1) * SLOT] = here[:, 0:ch]
            hs_ref[lv, 1, (m + 1) * SLOT : (m + 2) * SLOT] = here[:, ch:]
            if m == 0:
                z_ref[2 * lv * SLOT : (2 * lv + 1) * SLOT] = here[:, 0:ch]
            if m == half - 1:
                z_ref[(2 * lv + 1) * SLOT : (2 * lv + 2) * SLOT] = here[:, ch:]
    size = half * SLOT
    rhs = []
    for lv in range(levels):
        odd, ev = hs_ref.at[lv, 1], hs_ref.at[lv, 0]
        rhs.append(jnp.concatenate([odd[0:size], ev[0:size], odd[SLOT : size + SLOT], ev[SLOT : size + SLOT]], axis=1))
    q_side = nt(w2_ref[...], jnp.concatenate(rhs, axis=0))
    q_ends = nt(w2e_ref[...], z_ref[...])
    in_left = lanes((SLOT, WIDE)) % SLOT < SIDE

    def join_sides(q):
        taps = [q[b * SLOT : (b + 1) * SLOT] for b in range(3)]
        l = [jnp.where(in_left, x, 0.0) for x in taps]
        r = [jnp.where(in_left, 0.0, x) for x in taps]
        l = roll(l[0], 2) + roll(l[1], 1) + l[2]
        r = r[0] + roll(r[1], -1) + roll(r[2], -2)
        return mix(l, r), mix(r, l)

    for lv in range(levels):
        out, inn = {}, {}
        q = q_side[:, lv * size : (lv + 1) * size]
        for k in range(2):
            out[k], inn[k] = join_sides(q[k * 3 * SLOT : (k + 1) * 3 * SLOT])
        per = WIDE // (2 * SLOT)
        q = roll(q_ends[:, (lv // per) * WIDE : (lv // per + 1) * WIDE], -(lv % per) * 2 * SLOT)
        prev = join_sides(q[3 * SLOT : 6 * SLOT])
        nxt = join_sides(q[0 : 3 * SLOT])
        for k, x, spot, by in ((3, prev, end, WIDE - SLOT), (2, nxt, begin, -SLOT)):
            out[k], inn[k] = (jnp.where(spot, roll(y, by), 0.0) for y in x)
        for k in range(4):
            pm_ref[lv, k] = out[k]
            cm_ref[lv, k] = inn[k]
        mains = {}
        for k, row in enumerate((-1, 0, 1, rows - 2, rows - 1, rows)):
            mains[row] = pe_ref[lv, k]
        mains[2], mains[3] = ps0_ref[lv, 2], ps0_ref[lv, 3]
        mains[rows - 4], mains[rows - 3] = ps1_ref[lv, 0], ps1_ref[lv, 1]
        for row in mains:
            k, base = place(row, rows)
            mains[row] = add_columns(mains[row], inn[k], base)
        for k, row in enumerate((-1, 0, 1, rows - 2, rows - 1, rows)):
            pec_ref[lv, k] = mains[row]
        lane8 = lanes((VG, WIDE))
        st = sst_ref[lv, 0], sst_ref[lv, 1]

        def terms_of(x, here):
            first = x.astype(bf16).astype(f32)
            return jnp.where(here, first, roll(x - first, WIDE // 2))

        st_lo = terms_of(jnp.where(lane8 < 2 * SLOT, st[0], roll(st[1], 2 * SLOT)), lane8 < WIDE // 2)
        st_hi = terms_of(jnp.where(lane8 >= WIDE - 2 * SLOT, st[0], roll(st[1], -2 * SLOT)), lane8 >= WIDE // 2)
        side_lo = jnp.where(lane < 2 * SLOT, out[0], jnp.where(lane < 4 * SLOT, roll(out[1], 2 * SLOT), out[3]))
        side_hi = jnp.where(lane >= WIDE - 2 * SLOT, out[0],
                            jnp.where(lane >= WIDE - 4 * SLOT, roll(out[1], -2 * SLOT), out[2]))
        out_lo = [mains[-1], mains[0], side_lo, mains[1], mains[2], mains[3][0:VG], st_lo]
        out_hi = [mains[rows], mains[rows - 1], side_hi, mains[rows - 2], mains[rows - 3], mains[rows - 4][0:VG], st_hi]
        out_lo, out_hi = jnp.concatenate(out_lo, axis=0), jnp.concatenate(out_hi, axis=0)
        for ref, x in ((outa_ref, jnp.where(even, out_hi, out_lo)), (outb_ref, jnp.where(even, out_lo, out_hi))):
            terms = two_terms(x)
            ref[lv, 0 : x.shape[0]] = terms[0]
            ref[lv, x.shape[0] :] = terms[1][0:FINE]


def advect_kernel(flag_ref, ps_ref, pe_ref, pm_ref, cm_ref, a_ref, b_ref, st8_ref, halo_ref, sst_ref, own_ref,
                  b2_ref, lat_ref, lats_ref, *rest):
    vel_ref, ten_ref, out_ref = rest[-3:]
    rows = st8_ref.shape[1]
    nvar = ten_ref.shape[0]
    even = flag_ref[0] == 0
    lane16 = lanes((2 * VG, WIDE))
    lane = lanes((VG, WIDE))
    pair = 2 * VG

    def halos(xa, xb):
        return jnp.where(even, xb, xa), jnp.where(even, xa, xb)

    coarse = a_ref.shape[1] - FINE

    def both_terms(ref):
        x = ref[0].astype(f32)
        return jnp.concatenate([x[0:FINE] + x[coarse:], x[FINE:coarse]], axis=0)

    lo, hi = halos(both_terms(a_ref), both_terms(b_ref))
    main = {}
    for row in range(2, rows - 2):
        k, base = place(row, rows)
        main[row] = add_columns(ps_ref[0, row], cm_ref[0, k], base)
    for k, row in enumerate((-1, 0, 1, rows - 2, rows - 1, rows)):
        main[row] = pe_ref[0, k]
    for k in range(REACH + 1):
        first = k * pair if k < 2 else (k + 1) * pair
        there = slice(first, first + pair)
        for got, row in ((lo, -k), (hi, rows - 1 + k)):
            main[row] = main[row] + got[there] if row in main else got[there]
    slo, shi = (got[2 * pair : 3 * pair] for got in (lo, hi))
    zero = jnp.zeros((pair, WIDE), f32)
    last, front = lane16 >= WIDE - 2 * SLOT, lane16 < 2 * SLOT
    side = {
        0: pm_ref[0, 0] + jnp.where(lane16 < SLOT, slo, zero),
        1: pm_ref[0, 1] + jnp.where(lane16 >= WIDE - SLOT, shi, zero),
        2: pm_ref[0, 2] + jnp.where(last, slo, jnp.where(front, shi, zero)),
        3: pm_ref[0, 3] + jnp.where(last, roll(slo, 2 * SLOT), jnp.where(front, roll(shi, -2 * SLOT), zero)),
    }
    bias = b2_ref[...]
    main = {r: speed_cap * jnp.tanh(x + bias) for r, x in main.items()}
    side = {k: speed_cap * jnp.tanh(x + bias) * lats_ref[2, 0:1] for k, x in side.items()}
    for part in range(2):
        for row in range(rows):
            out_ref[part, row * VG : (row + 1) * VG] = main[row][part * VG : (part + 1) * VG]
        for n in range(nvar):
            vel_ref[2 * n + part, 0] = out_ref[part, pl.ds(n, rows, stride=VG), :]

    q0 = {row: st8_ref[0, row] for row in range(rows)}
    for k in range(REACH):
        q0[k - REACH], q0[rows + k] = halo_ref[0, k], halo_ref[0, REACH + k]
    hlo, hhi = (x[(REACH + 1) * pair + VG :] for x in (lo, hi))
    hlo, hhi = hlo + roll(hlo, WIDE // 2), hhi + roll(hhi, WIDE // 2)
    last, front = lane >= WIDE - 2 * SLOT, lane < 2 * SLOT
    nil = jnp.zeros((VG, WIDE), f32)
    out_q = {
        0: sst_ref[0, 0],
        1: sst_ref[0, 1],
        2: jnp.where(last, hlo, jnp.where(front, hhi, nil)),
        3: jnp.where(last, roll(hlo, 2 * SLOT), jnp.where(front, roll(hhi, -2 * SLOT), nil)),
    }
    own_q = {0: own_ref[0, 0], 1: own_ref[0, 1], 2: nil, 3: nil}
    for row in list(range(-REACH, 0)) + list(range(rows, rows + REACH)):
        k, base = place(row, rows)
        own_q[k] = jnp.where(lane // SLOT == base // SLOT, roll(q0[row], base + SIDE), own_q[k])

    everywhere = range(-REACH, rows + REACH)
    own = {k: jnp.zeros((pair, WIDE), f32) for k in range(4)}
    for row in everywhere:
        k, base = place(row, rows)
        own[k] = jnp.where(lane16 // SLOT == base // SLOT, roll(main[row], base + SIDE), own[k])

    def tiles(out, inner):
        return {**{k: mix(out[k], inner[k]) for k in range(4)}, **{4 + k: mix(inner[k], out[k]) for k in range(4)}}

    s0 = tiles(out_q, own_q)
    vel_s = tiles(side, own)

    def tile_rows(s):
        def turned(own, halo, by, first):
            own, halo = roll(own, by), roll(halo, by)
            return jnp.where(first, halo, own), jnp.where(first, own, halo)

        before, after = {}, {}
        for t in (0, 4):
            before[t + 1], before[t + 3], after[t], after[t + 2] = s[t], s[t + 2], s[t + 1], s[t + 3]
            before[t], before[t + 2] = turned(s[t + 1], s[t + 3], SLOT, lane < SLOT)
            after[t + 1], after[t + 3] = turned(s[t], s[t + 2], -SLOT, lane >= WIDE - SLOT)
        return before, after

    u = {r: x[0:VG] for r, x in main.items()}
    us = {k: x[0:VG] for k, x in vel_s.items()}
    inside = range(1 - REACH, rows + REACH - 1)
    v = {r: main[r][VG:] for r in inside}
    vs = {k: x[VG:] for k, x in vel_s.items()}
    cosine, metric = lat_ref[0], lat_ref[1]

    def side_table(n, k):
        return mix(lats_ref[n], lats_ref[n + 3]) if k < 4 else mix(lats_ref[n + 3], lats_ref[n])

    cosine_s, metric_s = ([side_table(n, k) for k in range(8)] for n in range(2))
    flux = {r: x * cosine for r, x in v.items()}
    flux_s = {k: x * cosine_s[k] for k, x in vs.items()}
    ub, ua = tile_rows(us)

    def coefs(m, uu, vv, udiff, vdiff):
        flow = m * uu
        cl = jnp.maximum(flow, 0.0)
        cr = cl - flow
        cd = jnp.maximum(vv, 0.0)
        cu = cd - vv
        div = (0.5 * m) * (udiff + vdiff)
        return -((cl + cr) + (cd + cu) + div), cl, cr, cd, cu

    cm = {r: coefs(metric, u[r], v[r], u[r + 1] - u[r - 1], roll(flux[r], -1) - roll(flux[r], 1)) for r in inside}
    cs = {k: coefs(metric_s[k], us[k], vs[k], ua[k] - ub[k], roll(flux_s[k], -1) - roll(flux_s[k], 1)) for k in range(8)}

    def stencil(c, x, left, right):
        return c[0] * x + c[1] * left + c[2] * right + c[3] * roll(x, 1) + c[4] * roll(x, -1)

    def rate(q, s, depth):
        rb, ra = tile_rows(s)
        inner = range(depth - REACH, rows + REACH - depth)
        wanted = [k for k in range(8) if depth < REACH or k % 4 < 2]
        return ({r: stencil(cm[r], q[r], q[r - 1], q[r + 1]) for r in inner},
                {k: stencil(cs[k], s[k], rb[k], ra[k]) for k in wanted})

    def moved(rates, by):
        return {r: q0[r] + by * x for r, x in rates[0].items()}, {k: s0[k] + by * x for k, x in rates[1].items()}

    one = rate(q0, s0, 1)
    two = rate(*moved(one, 0.5 * time_step), 2)
    three = rate(*moved(two, 0.5 * time_step), 3)
    four = rate(*moved(three, time_step), 4)

    def mean(n, k):
        return (one[n][k] + four[n][k] + 2.0 * (two[n][k] + three[n][k])) * (1.0 / 6.0)

    ends = {k: mix(mean(1, 4 + k), mean(1, k)) for k in range(2)}
    for row in range(rows):
        k, base = place(row, rows)
        at_end = (lane < REACH) | (lane >= WIDE - REACH)
        out_ref[0, row * VG : (row + 1) * VG] = jnp.where(at_end, roll(ends[k], -(base + SIDE)), mean(0, row))
    for n in range(nvar):
        ten_ref[n, 0] = out_ref[0, pl.ds(n, rows, stride=VG), :]


def full(shape):
    return pl.BlockSpec(shape, lambda *i: (0,) * len(shape))


def per_level(shape):
    return pl.BlockSpec((1,) + shape[1:], lambda i: (i,) + (0,) * (len(shape) - 1))


def level_part(shape, index, block=1, offset=0):
    return pl.BlockSpec((block,) + shape, lambda i: (i + offset, index) + (0,) * (len(shape) - 1))


def levels_of(shape, block=1, offset=0):
    return pl.BlockSpec((block,) + shape[1:], lambda i: (i + offset,) + (0,) * (len(shape) - 1))


def var_level(shape, offset=0):
    return pl.BlockSpec((shape[0], 1) + shape[2:], lambda i: (0, i + offset, 0, 0))


def body(hidden_in, w_conv1, b_conv1, w_conv2, b_conv2, state):
    lev, ch, rows, cols = hidden_in.shape
    nvar = state.shape[0]
    ext = cols + SLOT
    half = rows // 2
    params = pltpu.CompilerParams(vmem_limit_bytes=VMEM_LIMIT)
    smem = pl.BlockSpec(memory_space=pltpu.SMEM)
    sds = jax.ShapeDtypeStruct

    def call(kernel, steps, ins, outs, out_specs, scratch, args, cost=None, aliases={}):
        return pl.pallas_call(
            kernel,
            grid=(steps,),
            in_specs=ins,
            out_specs=out_specs,
            out_shape=outs,
            scratch_shapes=scratch,
            compiler_params=params,
            cost_estimate=cost,
            input_output_aliases=aliases,
        )(*args)

    vmem = pl.BlockSpec(memory_space=pltpu.VMEM)

    def levels(block=1, off=0, first=None, size=None):
        def view(ref, i):
            here = pl.ds(off + i * block, block)
            return ref.at[here] if first is None else ref.at[here, first : first + size]

        return view

    def whole(kernel, steps, ins, outs, scratch, cost, unroll=1, scratch_views=(), first=None):
        views = [v for _, v in ins] + [v for _, v in outs] + list(scratch_views)

        def run(*refs):
            def one(i, carry):
                kernel(*[v(r, i) if v else r for v, r in zip(views, refs)], *refs[len(views) :])
                return carry

            if first:
                first(*refs[len(views) :])
            if steps == 1:
                one(0, 0)
            else:
                lax.fori_loop(0, steps, one, 0, unroll=unroll)

        return pl.pallas_call(
            run,
            in_specs=[smem if x is flags else vmem for x, _ in ins],
            out_specs=[vmem] * len(outs),
            out_shape=[x for x, _ in outs],
            scratch_shapes=scratch,
            compiler_params=params,
            cost_estimate=pl.CostEstimate(flops=cost, bytes_accessed=2**20, transcendentals=0),
        )(*[x for x, _ in ins])

    flags = jnp.stack([lax.axis_index("lon") % 2, lax.axis_index("lat") % 2, lax.axis_index("lat")]).astype(jnp.int32)
    lon_wire = (lev, ch + 2 * nvar * REACH, cols)
    lon_a, lon_b = pl.pallas_call(
        rows_kernel,
        in_specs=[smem] + [pl.BlockSpec(memory_space=pltpu.HBM)] * 2,
        out_specs=[vmem] * 2,
        out_shape=[sds(lon_wire, bf16)] * 2,
        scratch_shapes=[
            pltpu.VMEM((ch * rows, cols), f32),
            pltpu.VMEM(hidden_in.shape, bf16),
            pltpu.VMEM(state.shape, f32),
            pltpu.SemaphoreType.DMA((lev + 1,)),
        ],
        compiler_params=pltpu.CompilerParams(vmem_limit_bytes=ROWS_LIMIT),
    )(flags, hidden_in, state)
    shapes = [((12 * ch, 2 * ch), bf16), ((6 * SLOT, 4 * ch), bf16), ((9 * SLOT, ch), bf16),
              ((6 * SLOT, ch), bf16), ((1, 2 * ch), f32), ((2 * VG, WIDE), f32), ((3, VG, WIDE), f32), ((6, VG, WIDE), f32),
              ((SLOT, 2 * ch), f32)]
    w1_one = w_conv1.reshape(9 * ch, ch)
    b1 = b_conv1.reshape(1, ch)
    n_lat = cols * lax.axis_size("lat")
    w1_pair, w2_pair, w2_one, w2_ends, b1_pair, b2, lat_main, lat_side, keep = pl.pallas_call(
        lambda flag_ref, *refs: prep_kernel(flag_ref, n_lat, cols, *refs),
        in_specs=[smem, smem] + [vmem] * 3,
        out_specs=[vmem] * len(shapes),
        out_shape=[sds(*x) for x in shapes],
        scratch_shapes=[pltpu.VMEM((4 * VG, ch), f32)],
        compiler_params=params,
    )(flags, b_conv2, w1_one, w_conv2.transpose(0, 1, 3, 2).reshape(9, 2 * nvar, ch), b1)
    lon_a = swap(lon_a, "lon", 0, True)
    lon_b = swap(lon_b, "lon", 1, True)

    hbm = pl.BlockSpec(memory_space=pltpu.HBM)
    g_pair = (lev, 2, cols, ch)
    st8_shape = (lev, rows, VG, WIDE)
    cut = (lev, rows * SIDE, ch)
    ps_shape = (lev, rows, 2 * VG, WIDE)
    own_shape = (lev, 2, VG, WIDE)
    halo_shape = (lev, 2 * REACH, VG, WIDE)
    shapes = [(g_pair, bf16), (g_pair, bf16), (cut, bf16), (cut, bf16), (st8_shape, f32), (own_shape, f32), (ps_shape, f32)]
    each = levels()
    g_lo, g_hi, first, last, st8, own, ps = whole(
        main_kernel,
        lev,
        [(hidden_in, each), (state, lambda ref, i: ref.at[:, pl.ds(i, 1)]), (w1_pair, None), (w2_pair, None), (b1_pair, None)],
        [(sds(*x), each) for x in shapes],
        [
            pltpu.VMEM((ch * (rows + VG), cols), f32),
            pltpu.VMEM((rows * (cols + SLOT), ch), f32),
            pltpu.VMEM((rows, cols, 3 * ch), bf16),
            pltpu.VMEM((rows + 2, cols, ch), bf16),
        ],
        2 * lev * rows * ext * 9 * ch * ch,
        first=main_start,
    )

    sent_rows = -(-((rows + 1) * SENT + SIDE) // SLOT) * SLOT
    lat_wire = (lev, sent_rows + 2 * VG, WIDE)
    pair_shape = (lev, 2, cols, ch)
    shapes = [(pair_shape, bf16), (halo_shape, f32), (lat_wire, bf16), (lat_wire, bf16)]
    each = levels()
    row_pair, halo, lat_a, lat_b = whole(
        pack_kernel,
        lev,
        [(flags, None)] + [(x, each) for x in (lon_a, lon_b, first, last, own)],
        [(sds(*x), each) for x in shapes],
        [pltpu.VMEM((lev, 2, sent_rows, ch), f32), pltpu.VMEM((VG * REACH, WIDE), f32)],
        2**22,
        PACK_UNROLL,
        [each],
    )
    lat_a = swap(lat_a, "lat", 0, False)
    lat_b = swap(lat_b, "lat", 1, False)

    block = EDGE_LEVELS
    pe_shape = (lev, 6, 2 * VG, WIDE)
    each = levels(block)
    (pe,) = whole(
        edge_kernel,
        lev // block,
        [(row_pair, each), (g_lo, each), (g_hi, each), (w1_one, None), (w2_one, None), (b1, None),
         (ps, levels(block, 0, 0, 4)), (ps, levels(block, 0, rows - 4, 4))],
        [(sds(pe_shape, f32), each)],
        [
            pltpu.VMEM((6 * block * (cols + SLOT), ch), f32),
            pltpu.VMEM((2 * block, cols, 9 * ch), bf16),
            pltpu.VMEM((2 * block * cols, ch), bf16),
        ],
        lev * 4 * ext * 9 * ch * ch,
    )

    block = SIDE_LEVELS
    parts = PARTS
    count = lev // parts
    wire = (count, 2 * VG * (REACH + 2) + FINE, WIDE)
    pec_shape = (count,) + pe_shape[1:]
    pm4_shape = (count, 4, 2 * VG, WIDE)
    sst_shape = (count, 2, VG, WIDE)
    shapes = [(sst_shape, f32), (pm4_shape, f32), (pm4_shape, f32), (pec_shape, f32), (wire, bf16), (wire, bf16)]
    sent = []
    for part in range(parts):
        here = levels(block, part * count)
        each = levels(block)
        sst, pm, cm, pec, out_a, out_b = whole(
            side_kernel,
            count // block,
            [(flags, None)] + [(x, here) for x in (first, last, row_pair, lat_a, lat_b)]
            + [(x, None) for x in (w1_pair, w2_pair, w2_ends, b1_pair, keep)]
            + [(pe, here), (ps, levels(block, part * count, 0, 4)), (ps, levels(block, part * count, rows - 4, 4))],
            [(sds(*x), each) for x in shapes],
            [
                pltpu.VMEM((block, (rows + 2) * 2 * SLOT + 2 * SIDE, ch), f32),
                pltpu.VMEM((block, (rows + 2) * SLOT, 3 * ch), bf16),
                pltpu.VMEM((block, 2, (half + 1) * SLOT, ch), bf16),
                pltpu.VMEM((max(WIDE, block * 2 * SLOT), ch), bf16),
                pltpu.VMEM((block, 2, sent_rows, ch), f32),
            ],
            count * 512 * 12 * ch * ch,
        )
        sent.append((pec, pm, cm, sst, swap(out_a, "lon", 0, True), swap(out_b, "lon", 1, True)))

    outs = [sds((2 * nvar, lev, rows, cols), f32), sds(state.shape, f32)]
    done = ()
    for part, (pec, pm, cm, sst, out_a, out_b) in enumerate(sent):
        off = part * count
        here, each = levels(1, off), levels()
        ins = [(flags, None), (ps, here)] + [(x, each) for x in (pec, pm, cm, out_a, out_b)]
        ins += [(st8, here), (halo, here), (sst, each), (own, here)] + [(x, None) for x in (b2, lat_main, lat_side)]

        def run(*refs, off=off, ins=ins, given=len(done)):
            sources = [functools.partial(v, r) if v else (lambda i, r=r: r) for (_, v), r in zip(ins, refs)]
            vel_hbm, ten_hbm, vel_ref, ten_ref, out_ref, sem = refs[len(ins) + given :]

            def copies(i):
                at, to = pl.ds(i, 1), pl.ds(off + i, 1)
                return [
                    pltpu.make_async_copy(src.at[:, at], dst.at[:, to], sem.at[i, k])
                    for k, (src, dst) in enumerate(((vel_ref, vel_hbm), (ten_ref, ten_hbm)))
                ]

            def one(i, carry):
                at = pl.ds(i, 1)
                advect_kernel(*[f(i) for f in sources], vel_ref.at[:, at], ten_ref.at[:, at], out_ref.at[i])
                for copy in copies(i):
                    copy.start()
                return carry

            lax.fori_loop(0, count, one, 0, unroll=ADVECT_UNROLL)
            for i in range(count):
                for copy in copies(i):
                    copy.wait()

        done = pl.pallas_call(
            run,
            in_specs=[smem if x is flags else vmem for x, _ in ins] + [hbm] * len(done),
            out_specs=[hbm] * 2,
            out_shape=outs,
            scratch_shapes=[
                pltpu.VMEM((2 * nvar, count, rows, cols), f32),
                pltpu.VMEM((nvar, count, rows, cols), f32),
                pltpu.VMEM((count, 2, rows * VG, WIDE), f32),
                pltpu.SemaphoreType.DMA((count, 2)),
            ],
            compiler_params=params,
            cost_estimate=pl.CostEstimate(flops=count * 2**24, bytes_accessed=2 * 2**20, transcendentals=0),
            input_output_aliases={len(ins): 0, len(ins) + 1: 1} if done else {},
        )(*[x for x, _ in ins], *done)
    return tuple(done)


def solution(mesh):
    placed = (P(None, None, "lon", "lat"), P(), P(), P(), P(), P(None, None, "lon", "lat"))
    return jax.shard_map(
        body,
        mesh=mesh,
        in_specs=placed,
        out_specs=(P(None, None, "lon", "lat"), P(None, None, "lon", "lat")),
        check_vma=False,
    )
```
